32 devices in a mesh: parts: 2 (over y), group: 4 (over z), ingroup: 2 (over x), dp: 2 (over core).
Axes of the slice: x: 2, y: 2, z: 4, core: 2. Of those that a mesh axis runs over, the one named last changes fastest.
Arguments:
- tokens: bfloat16 [4096, 1024], P(('parts', 'group', 'ingroup', 'dp')), parts along dimension 0, may hold values from -6 to 6
- upstream: bfloat16 [4096, 1024], P(('parts', 'group', 'ingroup', 'dp')), parts along dimension 0, may hold values from -6 to 6
- expert_ids: int32 [4096, 8], P(('parts', 'group', 'ingroup', 'dp')), parts along dimension 0, may hold values from 0 to 31, as said below
- gate_fixed: int32 [4096, 8], P(('parts', 'group', 'ingroup', 'dp')), parts along dimension 0, may hold values from 1 to 65535
- slots: int32 [4096, 8], P(('parts', 'group', 'ingroup', 'dp')), parts along dimension 0, may hold values from 0 to 48, as said below
- w_gate: bfloat16 [32, 1024, 256], P(('group', 'ingroup')), may hold values from -0.1875 to 0.1875
- w_up: bfloat16 [32, 1024, 256], P(('group', 'ingroup')), may hold values from -0.1875 to 0.1875
- w_down: bfloat16 [32, 256, 1024], P(('group', 'ingroup')), may hold values from -0.375 to 0.375
Outputs:
- grad_tokens: bfloat16 [4096, 1024], P(('parts', 'group', 'ingroup', 'dp')), parts along dimension 0
- grad_gate: bfloat16 [64, 1024, 256], P(('parts', 'group', 'ingroup'), 'dp'), parts along dimension 0
- grad_up: bfloat16 [64, 1024, 256], P(('parts', 'group', 'ingroup'), 'dp'), parts along dimension 0
- grad_down: bfloat16 [64, 256, 1024], P(('parts', 'group', 'ingroup'), None, 'dp'), parts along dimension 0
The draws below stay inside these ranges and needn't reach their ends.
There are 2 independent parts, one for each index of `parts`. The reference program is written for one: setup_inputs(seed, part) draws one part's arguments, and reference() takes and returns one part's arrays. A program takes and returns all parts, laid end to end along the dimension named above; an argument that names none is the same for every part. Nothing has to cross between parts.
Inputs may be any that keep to these rules, and one draw needn't show every extreme that they name: `expert_ids`: each token's 8 ids differ. The choices k with one value of k // 2 lie in one expert group (expert e belongs to group e // 8), and the 4 groups of a token differ. In every block of 128 rows at most 128 tokens have choices in one group, and some group has exactly 128 of them. In every block one expert, the same in all blocks, is chosen by 48 + 1 tokens or more. `slots`: within a block of 128 rows, the choices of one expert are numbered 0, 1, 2, ... in the order of tokens and then of k; numbers from 48 on are given as 48 (dropped). Some expert reaches 48 in every block.
All inputs are finite; a program needn't handle non-finite values.
Results may differ from the reference program's by a relative error of at most 0.0085.
Values may be sent and summed in bfloat16 or wider, within the bound.
No kernel may reach another device: no remote copies, remote signals or barrier semaphores. Data moves between devices by JAX's collectives and lax.ppermute only.
A program may use at most 128 MiB of HBM per device.

```python
import jax
import jax.numpy as jnp
from jax import lax

D = 1024
FF = 256
TOP = 8
GROUPS_TOK = 4
TOK_DEV = 128
GROUPS = 4
GROUP_EXPERTS = 8
EXPERTS = 32
TOKENS = 2048
CAP = 48
GCAP = 128


def routing(key):
    blocks = TOKENS // TOK_DEV
    per_group = TOP // GROUPS_TOK
    key_count, key_pair, key_perm, key_expert, key_hot, key_order = jax.random.split(key, 6)
    favored = jax.random.randint(key_hot, (), 0, EXPERTS)
    favored_group = favored // GROUP_EXPERTS
    favored_local = favored % GROUP_EXPERTS
    picks_total = TOK_DEV * GROUPS_TOK
    others = GROUPS - 1
    rest = picks_total - GCAP
    base = rest // max(others, 1)
    extra = rest % max(others, 1)
    spread = max(0, min(base, GCAP - base - 1))
    order = jax.vmap(lambda k: jax.random.permutation(k, others))(jax.random.split(key_count, blocks))
    pairs = others // 2
    swings = jax.random.randint(key_pair, (blocks, pairs), 0, spread + 1)
    delta = jnp.concatenate([jnp.stack([swings, -swings], axis=2).reshape(blocks, 2 * pairs), jnp.zeros((blocks, others - 2 * pairs), jnp.int32)], axis=1)
    counts_other = base + (order < extra).astype(jnp.int32) + delta
    other_ids = jnp.arange(others) + (jnp.arange(others) >= favored_group).astype(jnp.int32)
    match = (other_ids[:, None] == jnp.arange(GROUPS)[None, :]).astype(jnp.int32)
    counts = jnp.sum(counts_other[:, :, None] * match[None, :, :], axis=1)
    counts = counts + GCAP * (jnp.arange(GROUPS) == favored_group).astype(jnp.int32)[None, :]
    bounds = jnp.cumsum(counts, axis=1)
    positions = jnp.arange(picks_total)
    group_of = jnp.sum((positions[None, :, None] >= bounds[:, None, :]).astype(jnp.int32), axis=2)
    start_fav = bounds[:, favored_group] - GCAP
    hot_flat = (group_of == favored_group) & (positions[None, :] - start_fav[:, None] < CAP + 1)
    selected = group_of.reshape(blocks, GROUPS_TOK, TOK_DEV).transpose(0, 2, 1)
    hot = jnp.any(hot_flat.reshape(blocks, GROUPS_TOK, TOK_DEV), axis=1)
    perm = jax.vmap(lambda k: jax.random.permutation(k, TOK_DEV))(jax.random.split(key_perm, blocks))
    selected = jnp.take_along_axis(selected, perm[:, :, None], axis=1)
    hot = jnp.take_along_axis(hot, perm, axis=1)
    chosen_groups = selected.reshape(TOKENS, GROUPS_TOK)
    order_score = jax.random.randint(key_order, (TOKENS, GROUPS_TOK), 0, 1 << 20) * GROUPS_TOK + jnp.arange(GROUPS_TOK)[None, :]
    unused_order, columns = lax.top_k(order_score, GROUPS_TOK)
    chosen_groups = jnp.take_along_axis(chosen_groups, columns, axis=1)
    hot_rows = hot.reshape(TOKENS)
    local_score = jax.random.randint(key_expert, (TOKENS, GROUPS_TOK, GROUP_EXPERTS), 0, 1 << 20) * GROUP_EXPERTS + jnp.arange(GROUP_EXPERTS)[None, None, :]
    boost = hot_rows[:, None, None] & (chosen_groups[:, :, None] == favored_group) & (jnp.arange(GROUP_EXPERTS)[None, None, :] == favored_local)
    local_score = local_score + jnp.where(boost, 1 << 27, 0)
    unused, picks = lax.top_k(local_score, per_group)
    chosen = (chosen_groups[:, :, None] * GROUP_EXPERTS + picks).reshape(TOKENS, TOP)
    return chosen.astype(jnp.int32)


def draw_expert_ids(key, part):
    return routing(key)


def draw_slots(key, part):
    chosen = routing(key)
    blocks = TOKENS // TOK_DEV
    flat = chosen.reshape(blocks, TOK_DEV * TOP)
    onehot = (flat[:, :, None] == jnp.arange(EXPERTS)[None, None, :]).astype(jnp.int32)
    running = jnp.cumsum(onehot, axis=1)
    number = jnp.sum(running * onehot, axis=2) - 1
    slot = jnp.minimum(number, CAP)
    return slot.reshape(TOKENS, TOP).astype(jnp.int32)


def touch_ends(values, own_key, least, largest):
    index_at = [jax.random.randint(jax.random.fold_in(own_key, axis), (), 0, length) for axis, length in enumerate(values.shape)]
    longest = values.shape.index(max(values.shape))
    next_to = index_at[:longest] + [(index_at[longest] + 1) % values.shape[longest]] + index_at[longest + 1:]
    return values.at[tuple(index_at)].set(least).at[tuple(next_to)].set(largest)


def shard_levels(key, dims, pieces, least, largest):
    level = 1.0
    for dim, shards_of in pieces:
        heights = jax.random.uniform(jax.random.fold_in(jax.random.fold_in(key, 6), dim), (shards_of,), jnp.float32, least / len(pieces), largest / len(pieces))
        level = level * jnp.repeat(jnp.exp(heights), dims[dim] // shards_of).reshape((-1,) + (1,) * (len(dims) - 1 - dim))
    return level


def normal_values(key, shape, scale, bound, cuts=(), kind=jnp.bfloat16):
    values = jax.random.normal(key, shape, jnp.float32) * scale
    if len(cuts) > 0:
        values = shard_levels(key, shape, cuts, -0.22, 0.18) * values
    return jnp.clip(values, min=-bound, max=bound).astype(kind)


def setup_inputs(seed: int = 0, part: int = 0) -> dict:
    keys = jax.random.split(jax.random.key(seed), 9)
    part_keys = jax.random.split(jax.random.fold_in(keys[8], part), 9)
    tokens = normal_values(part_keys[0], (TOKENS, D), 1.0, 6.0, ((0, 16),))
    upstream = normal_values(part_keys[1], (TOKENS, D), 1.0, 6.0, ((0, 16),))
    expert_ids = draw_expert_ids(jax.random.fold_in(jax.random.fold_in(keys[8], part), 71), part)
    gate_fixed = touch_ends(jax.random.randint(part_keys[3], (TOKENS, TOP), 1, 65536), jax.random.fold_in(part_keys[3], 1), 1, 65535).astype(jnp.int32)
    slots = draw_slots(jax.random.fold_in(jax.random.fold_in(keys[8], part), 71), part)
    w_gate = normal_values(keys[5], (EXPERTS, D, FF), D ** -0.5, 0.1875, ((0, 8),))
    w_up = normal_values(keys[6], (EXPERTS, D, FF), D ** -0.5, 0.1875, ((0, 8),))
    w_down = normal_values(keys[7], (EXPERTS, FF, D), FF ** -0.5, 0.375, ((0, 8),))
    return {"tokens": tokens, "upstream": upstream, "expert_ids": expert_ids, "gate_fixed": gate_fixed, "slots": slots, "w_gate": w_gate, "w_up": w_up, "w_down": w_down}


def gated_parts(pre_gate):
    logistic = jax.nn.sigmoid(pre_gate)
    return pre_gate * logistic, logistic * (1.0 + pre_gate * (1.0 - logistic))


def place_rows(values, target, total):
    width = values.shape[-1]
    summed = jnp.zeros((total + 1, width), jnp.float32).at[target.reshape(-1)].add(values.reshape(-1, width))
    return summed[:total].astype(jnp.bfloat16)


def reference(tokens, upstream, expert_ids, gate_fixed, slots, w_gate, w_up, w_down):
    blocks = TOKENS // TOK_DEV
    total = EXPERTS * CAP
    per_group = TOP // GROUPS_TOK
    usable = slots < CAP
    target = jnp.where(usable, expert_ids * CAP + slots, total).astype(jnp.int32)
    gates = gate_fixed.astype(jnp.float32) / 65536.0
    gate_wide = w_gate.astype(jnp.float32)
    up_wide = w_up.astype(jnp.float32)
    down_wide = w_down.astype(jnp.float32)
    pairing = (jnp.arange(GROUPS_TOK)[:, None] == (jnp.arange(TOP) // per_group)[None, :])

    def one_block(carry, inputs):
        acc_gate, acc_up, acc_down = carry
        block_tokens, block_upstream, block_target, block_gates = inputs
        scaled = (block_gates[:, :, None] * block_upstream.astype(jnp.float32)[:, None, :]).astype(jnp.bfloat16)
        scaled = lax.optimization_barrier(scaled).astype(jnp.float32)
        copies = jnp.broadcast_to(block_tokens.astype(jnp.float32)[:, None, :], scaled.shape)
        x_rows = place_rows(copies, block_target, total).reshape(EXPERTS, CAP, D).astype(jnp.float32)
        s_rows = place_rows(scaled, block_target, total).reshape(EXPERTS, CAP, D).astype(jnp.float32)
        pre_gate = jnp.einsum("ecd,edf->ecf", x_rows, gate_wide)
        pre_up = jnp.einsum("ecd,edf->ecf", x_rows, up_wide)
        active, slope = gated_parts(pre_gate)
        hidden = (active * pre_up).astype(jnp.bfloat16).astype(jnp.float32)
        grad_hidden = jnp.einsum("ecd,efd->ecf", s_rows, down_wide)
        grad_gate_pre = (grad_hidden * pre_up * slope).astype(jnp.bfloat16).astype(jnp.float32)
        grad_up_pre = (grad_hidden * active).astype(jnp.bfloat16).astype(jnp.float32)
        acc_gate = acc_gate + jnp.einsum("ecd,ecf->edf", x_rows, grad_gate_pre)
        acc_up = acc_up + jnp.einsum("ecd,ecf->edf", x_rows, grad_up_pre)
        acc_down = acc_down + jnp.einsum("ecf,ecd->efd", hidden, s_rows)
        rows_back = (jnp.einsum("ecf,edf->ecd", grad_gate_pre, gate_wide)
                     + jnp.einsum("ecf,edf->ecd", grad_up_pre, up_wide)).astype(jnp.bfloat16)
        padded = jnp.concatenate([rows_back.reshape(total, D), jnp.zeros((1, D), jnp.bfloat16)], axis=0)
        picked = padded[block_target.reshape(-1)].reshape(TOK_DEV, TOP, D).astype(jnp.float32)
        member = pairing[None, :, :] & (block_target < total)[:, None, :]
        group_part = jnp.einsum("tjk,tkd->tjd", member.astype(jnp.float32), picked).astype(jnp.bfloat16)
        group_part = lax.optimization_barrier(group_part).astype(jnp.float32)
        grad_block = jnp.sum(group_part, axis=1).astype(jnp.bfloat16)
        return (acc_gate, acc_up, acc_down), grad_block

    start = (jnp.zeros((EXPERTS, D, FF), jnp.float32), jnp.zeros((EXPERTS, D, FF), jnp.float32),
             jnp.zeros((EXPERTS, FF, D), jnp.float32))
    inputs = (tokens.reshape(blocks, TOK_DEV, D), upstream.reshape(blocks, TOK_DEV, D),
              target.reshape(blocks, TOK_DEV, TOP), gates.reshape(blocks, TOK_DEV, TOP))
    (acc_gate, acc_up, acc_down), grad_blocks = lax.scan(one_block, start, inputs)
    grad_tokens = grad_blocks.reshape(TOKENS, D)
    return (grad_tokens, acc_gate.astype(jnp.bfloat16), acc_up.astype(jnp.bfloat16),
            acc_down.astype(jnp.bfloat16))
```

```python
import functools

import jax
import jax.numpy as jnp
from jax import lax
from jax.experimental import pallas as pl
from jax.experimental.pallas import tpu as pltpu
from jax.sharding import PartitionSpec as P

GROUPS_TOK = 4
ROUTE_ROWS = 16
VMEM_LIMIT = 48 * 1024 * 1024


def dot(a, b, contract):
    return lax.dot_general(a, b, ((contract[:1], contract[1:]), ((), ())), preferred_element_type=jnp.float32)


def gated_parts(pre_gate):
    logistic = jax.nn.sigmoid(pre_gate)
    return (pre_gate * logistic, logistic * (1.0 + pre_gate * (1.0 - logistic)))


def partner(z, k, size):
    return z ^ k if size & (size - 1) == 0 else (k - z) % size


def route_keys(route, first_expert, local_experts, capacity, rows, offset, tok_rows, per_group):
    expert = route[0:1, :].astype(jnp.int32) - first_expert
    slot = route[1:2, :].astype(jnp.int32)
    gate = (route[2:3, :] * 256.0 + route[3:4, :]) / 65536.0
    valid = (expert >= 0) & (expert < local_experts) & (slot < capacity)
    key = jnp.where(valid, expert * rows + offset + slot, -1)
    gate = jnp.where(valid, gate, 0.0)
    width = tok_rows * per_group
    key_out, gate_out = key[:, :width], gate[:, :width]
    for j in range(1, route.shape[1] // width):
        key_out = jnp.maximum(key_out, key[:, j * width : (j + 1) * width])
        gate_out = jnp.maximum(gate_out, gate[:, j * width : (j + 1) * width])
    return key_out, gate_out


def chunk_kernel(n_blocks, tok_rows, capacity, rows, per_group, first_ref, *refs):
    payloads = refs[:n_blocks]
    w_gate, w_up, w_down = refs[n_blocks : n_blocks + 3]
    parts = refs[n_blocks + 3 : 2 * n_blocks + 3]
    x_out, s_out, h_out = refs[2 * n_blocks + 3 : 2 * n_blocks + 6]
    x_all, u_all, key_all, gate_all, hot_all, back_all = refs[2 * n_blocks + 6 :]
    e = pl.program_id(0)
    local_experts = pl.num_programs(0)
    n_tok = n_blocks * tok_rows
    ff = w_gate.shape[2]

    @pl.when(e == 0)
    def _():
        for b in range(n_blocks):
            rows_b = slice(b * tok_rows, (b + 1) * tok_rows)
            x_all[rows_b, :] = payloads[b][:tok_rows, :]
            u_all[rows_b, :] = payloads[b][tok_rows : 2 * tok_rows, :]
            route = payloads[b][2 * tok_rows : 2 * tok_rows + ROUTE_ROWS, :].astype(jnp.float32)
            key, gate = route_keys(
                route, first_ref[0], local_experts, capacity, rows, b * capacity, tok_rows, per_group
            )
            for i in range(per_group):
                cols = slice(i * tok_rows, (i + 1) * tok_rows)
                key_all[i : i + 1, rows_b] = key[:, cols]
                gate_all[i : i + 1, rows_b] = gate[:, cols]

    place = lax.broadcasted_iota(jnp.int32, (rows, n_tok), 0) + e * rows
    hot = jnp.zeros((rows, n_tok), jnp.float32)
    gate_hot = jnp.zeros((rows, n_tok), jnp.float32)
    for i in range(per_group):
        match = place == key_all[i : i + 1, :]
        hot = jnp.where(match, 1.0, hot)
        gate_hot = jnp.where(match, gate_all[i : i + 1, :], gate_hot)
    hot = hot.astype(jnp.bfloat16)
    row_gate = jnp.sum(gate_hot, axis=1, keepdims=True)
    here = pl.ds(pl.multiple_of(e * rows, rows), rows)
    hot_all[here, :] = hot
    x_rows = dot(hot, x_all[...], (1, 0)).astype(jnp.bfloat16)
    s_rows = (dot(hot, u_all[...], (1, 0)) * row_gate).astype(jnp.bfloat16)
    x_out[0] = x_rows
    s_out[0] = s_rows
    pre_gate = dot(x_rows, w_gate[0], (1, 0))
    pre_up = dot(x_rows, w_up[0], (1, 0))
    grad_hidden = dot(s_rows, w_down[0], (1, 1))
    active, slope = gated_parts(pre_gate)
    grad_gate_pre = (grad_hidden * pre_up * slope).astype(jnp.bfloat16)
    grad_up_pre = (grad_hidden * active).astype(jnp.bfloat16)
    h_out[0, :, :ff] = grad_gate_pre
    h_out[0, :, ff : 2 * ff] = grad_up_pre
    h_out[0, :, 2 * ff :] = (active * pre_up).astype(jnp.bfloat16)
    back = dot(grad_gate_pre, w_gate[0], (1, 1)) + dot(grad_up_pre, w_up[0], (1, 1))
    back_all[here, :] = back.astype(jnp.bfloat16)

    @pl.when(e == local_experts - 1)
    def _():
        summed = dot(hot_all[...], back_all[...], (0, 0)).astype(jnp.bfloat16)
        for b in range(n_blocks):
            parts[b][...] = summed[b * tok_rows : (b + 1) * tok_rows, :]


def chunk_call(payloads, first_expert, w_gate, w_up, w_down, tok_rows, capacity, rows, per_group):
    n_blocks = len(payloads)
    n_tok = n_blocks * tok_rows
    experts, width, ff = w_gate.shape
    whole = lambda shape: pl.BlockSpec(shape, lambda e, first: (0, 0))
    per_expert = lambda shape: pl.BlockSpec((1,) + shape, lambda e, first: (e, 0, 0))
    flops = 2 * experts * rows * width * (5 * ff + 3 * n_tok)
    return pl.pallas_call(
        functools.partial(chunk_kernel, n_blocks, tok_rows, capacity, rows, per_group),
        grid_spec=pltpu.PrefetchScalarGridSpec(
            num_scalar_prefetch=1,
            grid=(experts,),
            in_specs=[whole(payloads[0].shape)] * n_blocks
            + [per_expert((width, ff)), per_expert((width, ff)), per_expert((ff, width))],
            out_specs=[whole((tok_rows, width))] * n_blocks
            + [per_expert((rows, width)), per_expert((rows, width)), per_expert((rows, 3 * ff))],
            scratch_shapes=[
                pltpu.VMEM((n_tok, width), jnp.bfloat16),
                pltpu.VMEM((n_tok, width), jnp.bfloat16),
                pltpu.VMEM((per_group, n_tok), jnp.int32),
                pltpu.VMEM((per_group, n_tok), jnp.float32),
                pltpu.VMEM((experts * rows, n_tok), jnp.bfloat16),
                pltpu.VMEM((experts * rows, width), jnp.bfloat16),
            ],
        ),
        out_shape=[jax.ShapeDtypeStruct((tok_rows, width), jnp.bfloat16)] * n_blocks
        + [
            jax.ShapeDtypeStruct((experts, rows, width), jnp.bfloat16),
            jax.ShapeDtypeStruct((experts, rows, width), jnp.bfloat16),
            jax.ShapeDtypeStruct((experts, rows, 3 * ff), jnp.bfloat16),
        ],
        compiler_params=pltpu.CompilerParams(vmem_limit_bytes=VMEM_LIMIT),
        cost_estimate=pl.CostEstimate(
            flops=flops, bytes_accessed=6 * experts * width * ff + 8 * n_tok * width, transcendentals=0
        ),
        name="chunk",
    )(first_expert, *payloads, w_gate, w_up, w_down)


def halves_of(n, ff, refs):
    cat = lambda part: jnp.concatenate([ref[0] for ref in part], axis=0)
    x_rows, s_rows, hid = cat(refs[:n]), cat(refs[n : 2 * n]), cat(refs[2 * n : 3 * n])
    return dot(x_rows, hid[:, : 2 * ff], (0, 0)), dot(hid[:, 2 * ff :], s_rows, (0, 0))


def send_kernel(n, ff, half_ref, *refs):
    gate_up, down = halves_of(n, ff, refs)
    out = refs[3 * n]
    depth = gate_up.shape[0]
    out[0, :depth, :] = gate_up.astype(jnp.bfloat16)
    out[0, depth:, :] = down.astype(jnp.bfloat16)


def keep_kernel(n, ff, half_ref, *refs):
    gate_up, down = halves_of(n, ff, refs)
    got = refs[3 * n]
    out_gate, out_up, out_down = refs[3 * n + 1 :]
    depth = gate_up.shape[0]
    gate_up = gate_up + got[0, :depth, :].astype(jnp.float32)
    out_gate[0] = gate_up[:, :ff].astype(jnp.bfloat16)
    out_up[0] = gate_up[:, ff:].astype(jnp.bfloat16)
    out_down[0] = (down + got[0, depth:, :].astype(jnp.float32)).astype(jnp.bfloat16)


def weight_call(half, x_rows, s_rows, hids, got=None):
    n = len(x_rows)
    experts, rows, width = x_rows[0].shape
    ff = hids[0].shape[2] // 3
    depth = width // 2
    piece = lambda shape: pl.BlockSpec((1,) + shape, lambda e, half: (e, 0, 0))
    split = pl.BlockSpec((1, rows, depth), lambda e, half: (e, 0, half[0]))
    in_specs = [split] * (2 * n) + [piece((rows, 3 * ff))] * n
    operands = [*x_rows, *s_rows, *hids]
    packed = (depth + ff, depth)
    if got is None:
        kernel = send_kernel
        out_specs = piece(packed)
        out_shape = jax.ShapeDtypeStruct((experts,) + packed, jnp.bfloat16)
    else:
        kernel = keep_kernel
        in_specs = in_specs + [piece(packed)]
        operands = operands + [got]
        shapes = [(depth, ff), (depth, ff), (ff, depth)]
        out_specs = [piece(s) for s in shapes]
        out_shape = [jax.ShapeDtypeStruct((experts,) + s, jnp.bfloat16) for s in shapes]
    return pl.pallas_call(
        functools.partial(kernel, n, ff),
        grid_spec=pltpu.PrefetchScalarGridSpec(
            num_scalar_prefetch=1, grid=(experts,), in_specs=in_specs, out_specs=out_specs
        ),
        out_shape=out_shape,
        compiler_params=pltpu.CompilerParams(vmem_limit_bytes=VMEM_LIMIT),
        cost_estimate=pl.CostEstimate(
            flops=2 * experts * n * rows * 3 * ff * depth,
            bytes_accessed=2 * experts * (n * rows * (width + 3 * ff) + 3 * ff * depth),
            transcendentals=0,
        ),
        name="weight_grads",
    )(half, *operands)


def per_device(tokens, upstream, expert_ids, gate_fixed, slots, w_gate, w_up, w_down):
    local_experts = w_gate.shape[0]
    n_group = lax.axis_size("group")
    n_ingroup = lax.axis_size("ingroup")
    experts_all = local_experts * n_group * n_ingroup
    tok_rows, top_count = expert_ids.shape
    width = tokens.shape[1]
    per_group = top_count // GROUPS_TOK
    capacity = max(2, 3 * tok_rows * top_count // (2 * experts_all))
    rows = -(-n_ingroup * capacity // 16) * 16
    z, x, core = (lax.axis_index(a) for a in ("group", "ingroup", "dp"))
    first_expert = ((z * n_ingroup + x) * local_experts).astype(jnp.int32).reshape(1)

    route = jnp.stack([expert_ids.T, slots.T, (gate_fixed // 256).T, (gate_fixed % 256).T])
    route = route.reshape(-1, width).astype(jnp.bfloat16)
    route = jnp.pad(route, ((0, ROUTE_ROWS - route.shape[0]), (0, 0)))
    own = jnp.concatenate([tokens, upstream, route], axis=0)

    ups, downs = {0: own}, {0: own}
    for s in range(1, n_group):
        ups[s] = lax.ppermute(ups[s - 1], "group", [(i, i + 1) for i in range(s - 1, n_group - 1)])
        downs[s] = lax.ppermute(downs[s - 1], "group", [(i, i - 1) for i in range(1, n_group - s + 1)])

    chunks = []
    for k in range(n_group):
        if k == 0:
            column = own
        else:
            offsets = [i - partner(i, k, n_group) for i in range(n_group)]
            kinds = sorted(set(offsets))
            column = None
            for off in kinds:
                case = ups[off] if off >= 0 else downs[-off]
                picks = functools.reduce(jnp.logical_or, [z == i for i in range(n_group) if offsets[i] == off])
                column = case if column is None else jnp.where(picks, case, column)
        blocks = [column] + [
            lax.ppermute(column, "ingroup", [(i, (i + s) % n_ingroup) for i in range(n_ingroup)])
            for s in range(1, n_ingroup)
        ]
        chunks.append(
            chunk_call(blocks, first_expert, w_gate, w_up, w_down, tok_rows, capacity, rows, per_group)
        )

    x_rows, s_rows, hids = ([c[n_ingroup + i] for c in chunks] for i in range(3))
    half = core.astype(jnp.int32).reshape(1)
    to_send = weight_call(1 - half, x_rows, s_rows, hids)
    got = lax.ppermute(to_send, "dp", [(0, 1), (1, 0)])

    total = jnp.zeros((tok_rows, width), jnp.float32)
    for k in range(n_group):
        parts = chunks[k][:n_ingroup]
        group_part = parts[0].astype(jnp.float32)
        for s in range(1, n_ingroup):
            back = lax.ppermute(parts[s], "ingroup", [(i, (i - s) % n_ingroup) for i in range(n_ingroup)])
            group_part = group_part + back.astype(jnp.float32)
        group_part = group_part.astype(jnp.bfloat16)
        if k > 0:
            group_part = lax.ppermute(
                group_part, "group", [(i, partner(i, k, n_group)) for i in range(n_group)]
            )
        total = total + group_part.astype(jnp.float32)
    grad_tokens = total.astype(jnp.bfloat16)

    grad_gate, grad_up, grad_down = weight_call(half, x_rows, s_rows, hids, got)
    return grad_tokens, grad_gate, grad_up, grad_down


def solution(mesh):
    rows_spec = P(("parts", "group", "ingroup", "dp"), None)
    weight_spec = P(("group", "ingroup"), None, None)
    out_specs = (
        rows_spec,
        P(("parts", "group", "ingroup"), "dp", None),
        P(("parts", "group", "ingroup"), "dp", None),
        P(("parts", "group", "ingroup"), None, "dp"),
    )
    return jax.shard_map(
        per_device,
        mesh=mesh,
        in_specs=(rows_spec,) * 5 + (weight_spec,) * 3,
        out_specs=out_specs,
        check_vma=False,
    )
```

```python
import functools

import jax
import jax.numpy as jnp
from jax import lax
from jax.experimental import pallas as pl
from jax.experimental.pallas import tpu as pltpu
from jax.sharding import PartitionSpec as P

GROUPS_TOK = 4
ROUTE_ROWS = 16
VMEM_LIMIT = 24 * 1024 * 1024


def dot(a, b, contract):
    return lax.dot_general(a, b, ((contract[:1], contract[1:]), ((), ())), preferred_element_type=jnp.float32)


def gated_parts(pre_gate):
    logistic = jax.nn.sigmoid(pre_gate)
    return (pre_gate * logistic, logistic * (1.0 + pre_gate * (1.0 - logistic)))


def partner(z, k, size):
    return z ^ k if size & (size - 1) == 0 else (k - z) % size


def pack_kernel(tokens, upstream, expert_ids, slots, gate_fixed, out, sem):
    top_count, tok_rows = expert_ids.shape
    copies = [
        pltpu.make_async_copy(src, out.at[pl.ds(i * tok_rows, tok_rows), :], sem.at[i])
        for i, src in enumerate((tokens, upstream))
    ]
    for copy in copies:
        copy.start()
    gate = gate_fixed[...]
    out[2 * tok_rows :, :] = jnp.zeros((ROUTE_ROWS, out.shape[1]), jnp.bfloat16)
    for i, field in enumerate((expert_ids[...], slots[...], gate >> 8, gate & 255)):
        field = jnp.concatenate([field.astype(jnp.float32), jnp.zeros((ROUTE_ROWS - top_count, tok_rows), jnp.float32)], axis=0)
        out[2 * tok_rows :, i * tok_rows : (i + 1) * tok_rows] = field.astype(jnp.bfloat16)
    for copy in copies:
        copy.wait()


def pack_call(tokens, upstream, expert_ids, slots, gate_fixed):
    tok_rows, width = tokens.shape
    vmem = pl.BlockSpec(memory_space=pltpu.VMEM)
    return pl.pallas_call(
        pack_kernel,
        in_specs=[pl.BlockSpec(memory_space=pltpu.HBM)] * 2 + [vmem] * 3,
        out_specs=vmem,
        out_shape=jax.ShapeDtypeStruct((2 * tok_rows + ROUTE_ROWS, width), jnp.bfloat16),
        scratch_shapes=[pltpu.SemaphoreType.DMA((2,))],
        compiler_params=pltpu.CompilerParams(vmem_limit_bytes=VMEM_LIMIT),
        name="pack",
    )(tokens, upstream, expert_ids.T, slots.T, gate_fixed.T)


def route_keys(route, first_expert, local_experts, capacity, rows, offset, tok_rows, per_group):
    field = lambda i: route[:, i * tok_rows : (i + 1) * tok_rows]
    expert = field(0).astype(jnp.int32) - first_expert
    slot = field(1).astype(jnp.int32)
    gate = (field(2) * 256.0 + field(3)) / 65536.0
    valid = (expert >= 0) & (expert < local_experts) & (slot < capacity)
    key = jnp.where(valid, expert * rows + offset + slot, -1)
    gate = jnp.where(valid, gate, 0.0)
    pairs = []
    for i in range(per_group):
        key_out, gate_out = key[i : i + 1, :], gate[i : i + 1, :]
        for j in range(i + per_group, route.shape[0], per_group):
            key_out = jnp.maximum(key_out, key[j : j + 1, :])
            gate_out = jnp.maximum(gate_out, gate[j : j + 1, :])
        pairs.append((key_out, gate_out))
    return pairs


def chunk_kernel(n_blocks, tok_rows, capacity, rows, top_count, per_group, first_ref, *refs):
    payloads = refs[:n_blocks]
    w_gate, w_up, w_down = refs[n_blocks : n_blocks + 3]
    n_parts = len(refs) - n_blocks - 12
    parts = refs[n_blocks + 3 : n_blocks + 3 + n_parts]
    x_out, s_out, h_out, x_all, u_all, key_all, gate_all, hot_all, back_all = refs[-9:]
    e = pl.program_id(0)
    local_experts = pl.num_programs(0)
    n_tok = n_blocks * tok_rows
    ff = w_gate.shape[2]

    @pl.when(e == 0)
    def _():
        for b in range(n_blocks):
            rows_b = slice(b * tok_rows, (b + 1) * tok_rows)
            x_all[rows_b, :] = payloads[b][:tok_rows, :]
            u_all[rows_b, :] = payloads[b][tok_rows : 2 * tok_rows, :]
            route = payloads[b][2 * tok_rows : 2 * tok_rows + ROUTE_ROWS, :].astype(jnp.float32)[:top_count]
            pairs = route_keys(
                route, first_ref[0], local_experts, capacity, rows, b * capacity, tok_rows, per_group
            )
            for i, (key, gate) in enumerate(pairs):
                key_all[i : i + 1, rows_b] = key
                gate_all[i : i + 1, rows_b] = gate

    place = lax.broadcasted_iota(jnp.int32, (rows, n_tok), 0) + e * rows
    hot = jnp.zeros((rows, n_tok), jnp.float32)
    gate_hot = jnp.zeros((rows, n_tok), jnp.float32)
    for i in range(per_group):
        match = place == key_all[i : i + 1, :]
        hot = jnp.where(match, 1.0, hot)
        gate_hot = jnp.where(match, gate_all[i : i + 1, :], gate_hot)
    hot = hot.astype(jnp.bfloat16)
    row_gate = jnp.sum(gate_hot, axis=1, keepdims=True)
    here = pl.ds(pl.multiple_of(e * rows, rows), rows)
    hot_all[here, :] = hot
    x_rows = dot(hot, x_all[...], (1, 0)).astype(jnp.bfloat16)
    s_rows = (dot(hot, u_all[...], (1, 0)) * row_gate).astype(jnp.bfloat16)
    x_out[0] = x_rows
    s_out[0] = s_rows
    pre_gate = dot(x_rows, w_gate[0], (1, 0))
    pre_up = dot(x_rows, w_up[0], (1, 0))
    grad_hidden = dot(s_rows, w_down[0], (1, 1))
    active, slope = gated_parts(pre_gate)
    grad_gate_pre = (grad_hidden * pre_up * slope).astype(jnp.bfloat16)
    grad_up_pre = (grad_hidden * active).astype(jnp.bfloat16)
    h_out[0, :, :ff] = grad_gate_pre
    h_out[0, :, ff : 2 * ff] = grad_up_pre
    h_out[0, :, 2 * ff :] = (active * pre_up).astype(jnp.bfloat16)
    back = dot(grad_gate_pre, w_gate[0], (1, 1)) + dot(grad_up_pre, w_up[0], (1, 1))
    back_all[here, :] = back.astype(jnp.bfloat16)

    @pl.when(e == local_experts - 1)
    def _():
        summed = dot(hot_all[...], back_all[...], (0, 0)).astype(jnp.bfloat16)
        start = 0
        for part in parts:
            part[...] = summed[start : start + part.shape[0], :]
            start += part.shape[0]


def chunk_call(payloads, first_expert, w_gate, w_up, w_down, tok_rows, capacity, rows, top_count, per_group, joined):
    n_blocks = len(payloads)
    n_tok = n_blocks * tok_rows
    experts, width, ff = w_gate.shape
    part_shapes = [(n_tok, width)] if joined else [(tok_rows, width), (n_tok - tok_rows, width)]
    whole = lambda shape: pl.BlockSpec(shape, lambda e, first: (0, 0))
    per_expert = lambda shape: pl.BlockSpec((1,) + shape, lambda e, first: (e, 0, 0))
    flops = 2 * experts * rows * width * (5 * ff + 3 * n_tok)
    return pl.pallas_call(
        functools.partial(chunk_kernel, n_blocks, tok_rows, capacity, rows, top_count, per_group),
        grid_spec=pltpu.PrefetchScalarGridSpec(
            num_scalar_prefetch=1,
            grid=(experts,),
            in_specs=[whole(payloads[0].shape)] * n_blocks
            + [per_expert((width, ff)), per_expert((width, ff)), per_expert((ff, width))],
            out_specs=[whole(shape) for shape in part_shapes]
            + [per_expert((rows, width)), per_expert((rows, width)), per_expert((rows, 3 * ff))],
            scratch_shapes=[
                pltpu.VMEM((n_tok, width), jnp.bfloat16),
                pltpu.VMEM((n_tok, width), jnp.bfloat16),
                pltpu.VMEM((per_group, n_tok), jnp.int32),
                pltpu.VMEM((per_group, n_tok), jnp.float32),
                pltpu.VMEM((experts * rows, n_tok), jnp.bfloat16),
                pltpu.VMEM((experts * rows, width), jnp.bfloat16),
            ],
        ),
        out_shape=[jax.ShapeDtypeStruct(shape, jnp.bfloat16) for shape in part_shapes]
        + [
            jax.ShapeDtypeStruct((experts, rows, width), jnp.bfloat16),
            jax.ShapeDtypeStruct((experts, rows, width), jnp.bfloat16),
            jax.ShapeDtypeStruct((experts, rows, 3 * ff), jnp.bfloat16),
        ],
        compiler_params=pltpu.CompilerParams(vmem_limit_bytes=VMEM_LIMIT),
        cost_estimate=pl.CostEstimate(
            flops=flops, bytes_accessed=6 * experts * width * ff + 8 * n_tok * width, transcendentals=0
        ),
        name="chunk",
    )(first_expert, *payloads, w_gate, w_up, w_down)


def halves_of(n, ff, refs):
    cat = lambda part: jnp.concatenate([ref[0] for ref in part], axis=0)
    x_rows, s_rows, hid = cat(refs[:n]), cat(refs[n : 2 * n]), cat(refs[2 * n : 3 * n])
    return dot(x_rows, hid[:, : 2 * ff], (0, 0)), dot(hid[:, 2 * ff :], s_rows, (0, 0))


def send_kernel(n, ff, half_ref, *refs):
    gate_up, down = halves_of(n, ff, refs)
    out = refs[3 * n]
    depth = gate_up.shape[0]
    out[0, :depth, :] = gate_up.astype(jnp.bfloat16)
    out[0, depth:, :] = down.astype(jnp.bfloat16)


def keep_kernel(n, ff, half_ref, *refs):
    gate_up, down = halves_of(n, ff, refs)
    got = refs[3 * n]
    out_gate, out_up, out_down = refs[3 * n + 1 :]
    depth = gate_up.shape[0]
    gate_up = gate_up + got[0, :depth, :].astype(jnp.float32)
    out_gate[0] = gate_up[:, :ff].astype(jnp.bfloat16)
    out_up[0] = gate_up[:, ff:].astype(jnp.bfloat16)
    out_down[0] = (down + got[0, depth:, :].astype(jnp.float32)).astype(jnp.bfloat16)


def weight_call(half, x_rows, s_rows, hids, got=None):
    n = len(x_rows)
    experts, rows, width = x_rows[0].shape
    ff = hids[0].shape[2] // 3
    depth = width // 2
    piece = lambda shape: pl.BlockSpec((1,) + shape, lambda e, half: (e, 0, 0))
    split = pl.BlockSpec((1, rows, depth), lambda e, half: (e, 0, half[0]))
    in_specs = [split] * (2 * n) + [piece((rows, 3 * ff))] * n
    operands = [*x_rows, *s_rows, *hids]
    packed = (depth + ff, depth)
    if got is None:
        kernel = send_kernel
        out_specs = piece(packed)
        out_shape = jax.ShapeDtypeStruct((experts,) + packed, jnp.bfloat16)
    else:
        kernel = keep_kernel
        in_specs = in_specs + [piece(packed)]
        operands = operands + [got]
        shapes = [(depth, ff), (depth, ff), (ff, depth)]
        out_specs = [piece(s) for s in shapes]
        out_shape = [jax.ShapeDtypeStruct((experts,) + s, jnp.bfloat16) for s in shapes]
    return pl.pallas_call(
        functools.partial(kernel, n, ff),
        grid_spec=pltpu.PrefetchScalarGridSpec(
            num_scalar_prefetch=1, grid=(experts,), in_specs=in_specs, out_specs=out_specs
        ),
        out_shape=out_shape,
        compiler_params=pltpu.CompilerParams(vmem_limit_bytes=VMEM_LIMIT),
        cost_estimate=pl.CostEstimate(
            flops=2 * experts * n * rows * 3 * ff * depth,
            bytes_accessed=2 * experts * (n * rows * (width + 3 * ff) + 3 * ff * depth),
            transcendentals=0,
        ),
        name="weight_grads",
    )(half, *operands)


def pass_steps(size):
    steps = [{} for _ in range(size - 1)]
    for z in range(size):
        for k in range(1, size):
            block = partner(z, k, size)
            via = z + (1 if block > z else -1)
            held = next(j for j in range(size) if partner(via, j, size) == block)
            steps[abs(block - z) - 1].setdefault((held, k), []).append((via, z))
    return steps


def merge(pieces, z):
    out = pieces[0][0]
    for piece, places in pieces[1:]:
        out = jnp.where(functools.reduce(jnp.logical_or, [z == i for i in places]), piece, out)
    return out


def piece_of(pieces, pairs, z):
    sources = {a for a, _ in pairs}
    for piece, places in pieces:
        if sources <= set(places):
            return piece
    return merge(pieces, z)


def per_device(tokens, upstream, expert_ids, gate_fixed, slots, w_gate, w_up, w_down):
    local_experts = w_gate.shape[0]
    n_group = lax.axis_size("group")
    n_ingroup = lax.axis_size("ingroup")
    experts_all = local_experts * n_group * n_ingroup
    tok_rows, top_count = expert_ids.shape
    width = tokens.shape[1]
    per_group = top_count // GROUPS_TOK
    capacity = max(2, 3 * tok_rows * top_count // (2 * experts_all))
    rows = -(-n_ingroup * capacity // 16) * 16
    z, x, core = (lax.axis_index(a) for a in ("group", "ingroup", "dp"))
    first_expert = ((z * n_ingroup + x) * local_experts).astype(jnp.int32).reshape(1)

    own = pack_call(tokens, upstream, expert_ids, slots, gate_fixed)
    swap = lambda k: [(i, partner(i, k, n_group)) for i in range(n_group)]
    shift = lambda s: [(i, (i + s) % n_ingroup) for i in range(n_ingroup)]
    spread = lambda column: [column] + [lax.ppermute(column, "ingroup", shift(s)) for s in range(1, n_ingroup)]
    steps = pass_steps(n_group)

    pieces = {0: [(own, range(n_group))]}
    ready = {0: 0}
    for step, table in enumerate(steps, 1):
        ready.update({k: step for _, k in table})
    wide = lambda v: v.astype(jnp.float32)

    def across(others):
        return [
            lax.ppermute(others[(s - 1) * tok_rows : s * tok_rows], "ingroup", [(b, a) for a, b in shift(s)])
            for s in range(1, n_ingroup)
        ]

    half = core.astype(jnp.int32).reshape(1)
    blocks, chunks, backs, near, to_send = {}, {}, {}, None, None
    for wave in range(1, n_group + 2):
        table = steps[wave - 1] if wave < n_group else {}
        moved = [
            lax.ppermute(piece_of(pieces[a], pairs, z), "group", pairs) for (a, b), pairs in table.items()
        ]
        new = [k for k in ready if ready[k] == wave - 1]
        spreads = [spread(merge(pieces[k], z)) for k in new]
        sums = []
        if wave == n_group + 1:
            other = (wide(chunks[0][1]) + wide(near[tok_rows:])).astype(jnp.bfloat16)
            sums = {k: across(other if k == 0 else chunks[k][1]) for k in chunks if k != 1}
        elif near is None and 1 in chunks:
            near = lax.ppermute(chunks[1][0], "group", swap(1))
        here = [k for k in ready if ready[k] == wave - 2]
        done = [
            chunk_call(
                blocks[k], first_expert, w_gate, w_up, w_down, tok_rows, capacity, rows, top_count, per_group, k == 1
            )
            for k in here
        ]
        if wave == n_group + 1:
            all_chunks = {**chunks, **dict(zip(here, done))}
            kept = [[all_chunks[k][i] for k in range(n_group)] for i in (-3, -2, -1)]
            to_send = weight_call(1 - half, *kept)
        moved, spreads, done, near, sums, to_send = lax.optimization_barrier(
            (moved, spreads, done, near, sums, to_send)
        )
        for (a, b), pairs, piece in zip(table.keys(), table.values(), moved):
            pieces.setdefault(b, []).append((piece, [to for _, to in pairs]))
        blocks.update(zip(new, spreads))
        chunks.update(zip(here, done))

    got = lax.ppermute(to_send, "dp", [(0, 1), (1, 0)])
    total = wide(chunks[0][0]) + wide(near[:tok_rows])
    for back in sums[0]:
        total = total + wide(back)
    last = {k: across(chunks[k][1]) for k in here}
    sent = {}
    for k in range(2, n_group):
        group_part = wide(chunks[k][0])
        for back in last[k] if k in last else sums[k]:
            group_part = group_part + wide(back)
        sent[k] = lax.ppermute(group_part.astype(jnp.bfloat16), "group", swap(k))
    for k in range(2, n_group):
        total = total + wide(sent[k])
    grad_tokens = total.astype(jnp.bfloat16)

    x_rows, s_rows, hids = ([chunks[k][i] for k in range(n_group)] for i in (-3, -2, -1))
    grad_gate, grad_up, grad_down = weight_call(half, x_rows, s_rows, hids, got)
    return grad_tokens, grad_gate, grad_up, grad_down


def solution(mesh):
    rows_spec = P(("parts", "group", "ingroup", "dp"), None)
    weight_spec = P(("group", "ingroup"), None, None)
    out_specs = (
        rows_spec,
        P(("parts", "group", "ingroup"), "dp", None),
        P(("parts", "group", "ingroup"), "dp", None),
        P(("parts", "group", "ingroup"), None, "dp"),
    )
    return jax.shard_map(
        per_device,
        mesh=mesh,
        in_specs=(rows_spec,) * 5 + (weight_spec,) * 3,
        out_specs=out_specs,
        check_vma=False,
    )
```

```python
import functools

import jax
import jax.numpy as jnp
from jax import lax
from jax.experimental import pallas as pl
from jax.experimental.pallas import tpu as pltpu
from jax.sharding import PartitionSpec as P

GROUPS_TOK = 4
VMEM_LIMIT = 24 * 1024 * 1024


def dot(a, b, contract):
    return lax.dot_general(a, b, ((contract[:1], contract[1:]), ((), ())), preferred_element_type=jnp.float32)


def in_hbm(v):
    return pltpu.with_memory_space_constraint(v, pltpu.HBM)


def gated_parts(pre_gate):
    logistic = jax.nn.sigmoid(pre_gate)
    return (pre_gate * logistic, logistic * (1.0 + pre_gate * (1.0 - logistic)))


def partner(z, k, size):
    return z ^ k if size & (size - 1) == 0 else (k - z) % size


def route_keys(route, first_expert, local_experts, capacity, rows, offset, top_count, per_group):
    expert = route[:top_count] - first_expert
    slot = route[top_count : 2 * top_count]
    gate = route[2 * top_count :].astype(jnp.float32) / 65536.0
    valid = (expert >= 0) & (expert < local_experts) & (slot < capacity)
    key = jnp.where(valid, expert * rows + offset + slot, -1)
    gate = jnp.where(valid, gate, 0.0)
    pairs = []
    for i in range(per_group):
        key_out, gate_out = key[i : i + 1, :], gate[i : i + 1, :]
        for j in range(i + per_group, top_count, per_group):
            key_out = jnp.maximum(key_out, key[j : j + 1, :])
            gate_out = jnp.maximum(gate_out, gate[j : j + 1, :])
        pairs.append((key_out, gate_out))
    return pairs


def chunk_kernel(n_blocks, tok_rows, capacity, rows, top_count, per_group, where_ref, *refs):
    tokens, upstream, routes = (refs[i * n_blocks : (i + 1) * n_blocks] for i in range(3))
    w_gate, w_up, w_down = refs[3 * n_blocks : 3 * n_blocks + 3]
    n_parts = len(refs) - 3 * n_blocks - 12
    parts = refs[3 * n_blocks + 3 : 3 * n_blocks + 3 + n_parts]
    x_out, s_out, h_out, x_all, u_all, key_all, gate_all, hot_all, back_all = refs[-9:]
    e = pl.program_id(0)
    local_experts = pl.num_programs(0)
    n_tok = n_blocks * tok_rows
    ff = w_gate.shape[2]

    @pl.when(e == 0)
    def _():
        for b in range(n_blocks):
            rows_b = slice(b * tok_rows, (b + 1) * tok_rows)
            x_all[rows_b, :] = tokens[b][0]
            u_all[rows_b, :] = upstream[b][0]
            pairs = route_keys(
                routes[b][0], where_ref[0], local_experts, capacity, rows, b * capacity, top_count, per_group
            )
            for i, (key, gate) in enumerate(pairs):
                key_all[i : i + 1, rows_b] = key
                gate_all[i : i + 1, rows_b] = gate

    place = lax.broadcasted_iota(jnp.int32, (rows, n_tok), 0) + e * rows
    hot = jnp.zeros((rows, n_tok), jnp.float32)
    gate_hot = jnp.zeros((rows, n_tok), jnp.float32)
    for i in range(per_group):
        match = place == key_all[i : i + 1, :]
        hot = jnp.where(match, 1.0, hot)
        gate_hot = jnp.where(match, gate_all[i : i + 1, :], gate_hot)
    hot = hot.astype(jnp.bfloat16)
    row_gate = jnp.sum(gate_hot, axis=1, keepdims=True)
    here = pl.ds(pl.multiple_of(e * rows, rows), rows)
    hot_all[here, :] = hot
    x_rows = dot(hot, x_all[...], (1, 0)).astype(jnp.bfloat16)
    s_rows = (dot(hot, u_all[...], (1, 0)) * row_gate).astype(jnp.bfloat16)
    x_out[0] = x_rows
    s_out[0] = s_rows
    pre_gate = dot(x_rows, w_gate[0], (1, 0))
    pre_up = dot(x_rows, w_up[0], (1, 0))
    grad_hidden = dot(s_rows, w_down[0], (1, 1))
    active, slope = gated_parts(pre_gate)
    grad_gate_pre = (grad_hidden * pre_up * slope).astype(jnp.bfloat16)
    grad_up_pre = (grad_hidden * active).astype(jnp.bfloat16)
    h_out[0, :, :ff] = grad_gate_pre
    h_out[0, :, ff : 2 * ff] = grad_up_pre
    h_out[0, :, 2 * ff :] = (active * pre_up).astype(jnp.bfloat16)
    back = dot(grad_gate_pre, w_gate[0], (1, 1)) + dot(grad_up_pre, w_up[0], (1, 1))
    back_all[here, :] = back.astype(jnp.bfloat16)

    @pl.when(e == local_experts - 1)
    def _():
        summed = dot(hot_all[...], back_all[...], (0, 0)).astype(jnp.bfloat16)
        start = 0
        for part in parts:
            part[...] = summed[start : start + part.shape[0], :]
            start += part.shape[0]


def chunk_call(tokens, upstream, routes, where, weights, capacity, rows, per_group, joined):
    n_blocks = where.shape[0] - 1
    tok_rows, width = tokens.shape[1:]
    top_count = routes.shape[1] // 3
    n_tok = n_blocks * tok_rows
    experts, _, ff = weights[0].shape
    part_shapes = [(n_tok, width)] if joined else [(tok_rows, width), (n_tok - tok_rows, width)]
    whole = lambda shape: pl.BlockSpec(shape, lambda e, where: (0, 0))
    per_expert = lambda shape: pl.BlockSpec((1,) + shape, lambda e, where: (e, 0, 0))
    picked = lambda shape: [
        pl.BlockSpec((1,) + shape[1:], lambda e, where, b=b: (where[b + 1], 0, 0)) for b in range(n_blocks)
    ]
    return pl.pallas_call(
        functools.partial(chunk_kernel, n_blocks, tok_rows, capacity, rows, top_count, per_group),
        grid_spec=pltpu.PrefetchScalarGridSpec(
            num_scalar_prefetch=1,
            grid=(experts,),
            in_specs=picked(tokens.shape) + picked(upstream.shape) + picked(routes.shape)
            + [per_expert((width, ff)), per_expert((width, ff)), per_expert((ff, width))],
            out_specs=[whole(shape) for shape in part_shapes]
            + [per_expert((rows, width)), per_expert((rows, width)), per_expert((rows, 3 * ff))],
            scratch_shapes=[
                pltpu.VMEM((n_tok, width), jnp.bfloat16),
                pltpu.VMEM((n_tok, width), jnp.bfloat16),
                pltpu.VMEM((per_group, n_tok), jnp.int32),
                pltpu.VMEM((per_group, n_tok), jnp.float32),
                pltpu.VMEM((experts * rows, n_tok), jnp.bfloat16),
                pltpu.VMEM((experts * rows, width), jnp.bfloat16),
            ],
        ),
        out_shape=[jax.ShapeDtypeStruct(shape, jnp.bfloat16) for shape in part_shapes]
        + [
            jax.ShapeDtypeStruct((experts, rows, width), jnp.bfloat16),
            jax.ShapeDtypeStruct((experts, rows, width), jnp.bfloat16),
            jax.ShapeDtypeStruct((experts, rows, 3 * ff), jnp.bfloat16),
        ],
        compiler_params=pltpu.CompilerParams(vmem_limit_bytes=VMEM_LIMIT),
        cost_estimate=pl.CostEstimate(
            flops=2 * experts * rows * width * (5 * ff + 3 * n_tok),
            bytes_accessed=6 * experts * width * ff + 8 * n_tok * width,
            transcendentals=0,
        ),
        name="chunk",
    )(where, *[in_hbm(v) for v in (tokens, upstream, routes) for _ in range(n_blocks)], *weights)


def halves_of(n, ff, refs):
    cat = lambda part: jnp.concatenate([ref[0] for ref in part], axis=0)
    x_rows, s_rows, hid = cat(refs[:n]), cat(refs[n : 2 * n]), cat(refs[2 * n : 3 * n])
    return dot(x_rows, hid[:, : 2 * ff], (0, 0)), dot(hid[:, 2 * ff :], s_rows, (0, 0))


def send_kernel(n, ff, half_ref, *refs):
    gate_up, down = halves_of(n, ff, refs)
    out = refs[3 * n]
    depth = gate_up.shape[0]
    out[0, :depth, :] = gate_up.astype(jnp.bfloat16)
    out[0, depth:, :] = down.astype(jnp.bfloat16)


def keep_kernel(n, ff, half_ref, *refs):
    gate_up, down = halves_of(n, ff, refs)
    got = refs[3 * n]
    out_gate, out_up, out_down = refs[3 * n + 1 :]
    depth = gate_up.shape[0]
    gate_up = gate_up + got[0, :depth, :].astype(jnp.float32)
    out_gate[0] = gate_up[:, :ff].astype(jnp.bfloat16)
    out_up[0] = gate_up[:, ff:].astype(jnp.bfloat16)
    out_down[0] = (down + got[0, depth:, :].astype(jnp.float32)).astype(jnp.bfloat16)


def weight_call(half, x_rows, s_rows, hids, got=None):
    n = len(x_rows)
    experts, rows, width = x_rows[0].shape
    ff = hids[0].shape[2] // 3
    depth = width // 2
    piece = lambda shape: pl.BlockSpec((1,) + shape, lambda e, half: (e, 0, 0))
    split = pl.BlockSpec((1, rows, depth), lambda e, half: (e, 0, half[0]))
    in_specs = [split] * (2 * n) + [piece((rows, 3 * ff))] * n
    operands = [*x_rows, *s_rows, *hids]
    packed = (depth + ff, depth)
    if got is None:
        kernel = send_kernel
        out_specs = piece(packed)
        out_shape = jax.ShapeDtypeStruct((experts,) + packed, jnp.bfloat16)
    else:
        kernel = keep_kernel
        in_specs = in_specs + [piece(packed)]
        operands = operands + [got]
        shapes = [(depth, ff), (depth, ff), (ff, depth)]
        out_specs = [piece(s) for s in shapes]
        out_shape = [jax.ShapeDtypeStruct((experts,) + s, jnp.bfloat16) for s in shapes]
    return pl.pallas_call(
        functools.partial(kernel, n, ff),
        grid_spec=pltpu.PrefetchScalarGridSpec(
            num_scalar_prefetch=1, grid=(experts,), in_specs=in_specs, out_specs=out_specs
        ),
        out_shape=out_shape,
        compiler_params=pltpu.CompilerParams(vmem_limit_bytes=VMEM_LIMIT),
        cost_estimate=pl.CostEstimate(
            flops=2 * experts * n * rows * 3 * ff * depth,
            bytes_accessed=2 * experts * (n * rows * (width + 3 * ff) + 3 * ff * depth),
            transcendentals=0,
        ),
        name="weight_grads",
    )(half, *operands)


def per_device(tokens, upstream, expert_ids, gate_fixed, slots, w_gate, w_up, w_down):
    local_experts = w_gate.shape[0]
    n_group = lax.axis_size("group")
    n_ingroup = lax.axis_size("ingroup")
    experts_all = local_experts * n_group * n_ingroup
    tok_rows, top_count = expert_ids.shape
    width = tokens.shape[1]
    per_group = top_count // GROUPS_TOK
    capacity = max(2, 3 * tok_rows * top_count // (2 * experts_all))
    rows = -(-n_ingroup * capacity // 16) * 16
    z, x, core = (lax.axis_index(a) for a in ("group", "ingroup", "dp"))
    first_expert = (z * n_ingroup + x) * local_experts
    weights = [in_hbm(w) for w in (w_gate, w_up, w_down)]
    wide = lambda v: v.astype(jnp.float32)
    tie = lambda *trees: lax.optimization_barrier(trees)
    swap = lambda k: [(i, partner(i, k, n_group)) for i in range(n_group)]

    gather = lambda v: lax.all_gather(v, ("group", "ingroup"))
    routes = gather(jnp.concatenate([expert_ids.T, slots.T, gate_fixed.T], axis=0))
    tokens, upstream = gather(tokens), gather(upstream)

    def chunk(k):
        column = partner(z, k, n_group) * n_ingroup
        where = [first_expert] + [column + (x - s) % n_ingroup for s in range(n_ingroup)]
        where = jnp.stack(where).astype(jnp.int32)
        return chunk_call(tokens, upstream, routes, where, weights, capacity, rows, per_group, k == 1)

    def across(others):
        return [
            lax.ppermute(
                others[(s - 1) * tok_rows : s * tok_rows], "ingroup", [(i, (i - s) % n_ingroup) for i in range(n_ingroup)]
            )
            for s in range(1, n_ingroup)
        ]

    def homeward(k):
        group_part = wide(chunks[k][0])
        for back in backs[k]:
            group_part = group_part + wide(back)
        return lax.ppermute(group_part.astype(jnp.bfloat16), "group", swap(k))

    chunks, backs, sent = {}, {}, {}
    chunks[1] = chunk(1)
    chunks[1], tokens = tie(chunks[1], tokens)
    near = lax.ppermute(chunks[1][0], "group", swap(1))
    for k in range(2, n_group):
        chunks[k] = chunk(k)
        if k > 2:
            chunks[k], backs[k - 1], tokens = tie(chunks[k], backs[k - 1], tokens)
            sent[k - 1] = homeward(k - 1)
        else:
            chunks[k], tokens = tie(chunks[k], tokens)
        backs[k] = across(chunks[k][1])
    chunks[0] = chunk(0)
    last = n_group - 1
    chunks[0], near, backs[last] = tie(chunks[0], near, backs[last])
    backs[0] = across((wide(chunks[0][1]) + wide(near[tok_rows:])).astype(jnp.bfloat16))
    sent[last] = homeward(last)

    x_rows, s_rows, hids = ([chunks[k][i] for k in range(n_group)] for i in (-3, -2, -1))
    half = core.astype(jnp.int32).reshape(1)
    to_send = weight_call(1 - half, x_rows, s_rows, hids)
    got = lax.ppermute(to_send, "dp", [(0, 1), (1, 0)])
    total = wide(chunks[0][0]) + wide(near[:tok_rows])
    for back in backs[0]:
        total = total + wide(back)
    for k in range(2, n_group):
        total = total + wide(sent[k])
    grad_tokens = total.astype(jnp.bfloat16)

    grad_gate, grad_up, grad_down = weight_call(half, x_rows, s_rows, hids, got)
    return grad_tokens, grad_gate, grad_up, grad_down


def solution(mesh):
    rows_spec = P(("parts", "group", "ingroup", "dp"), None)
    weight_spec = P(("group", "ingroup"), None, None)
    out_specs = (
        rows_spec,
        P(("parts", "group", "ingroup"), "dp", None),
        P(("parts", "group", "ingroup"), "dp", None),
        P(("parts", "group", "ingroup"), None, "dp"),
    )
    return jax.shard_map(
        per_device,
        mesh=mesh,
        in_specs=(rows_spec,) * 5 + (weight_spec,) * 3,
        out_specs=out_specs,
        check_vma=False,
    )
```

```python
import functools

import jax
import jax.numpy as jnp
from jax import lax
from jax.experimental import pallas as pl
from jax.experimental.pallas import tpu as pltpu
from jax.sharding import PartitionSpec as P

GROUPS_TOK = 4
ROUTE_ROWS = 16
VMEM_LIMIT = 32 * 1024 * 1024


def dot(a, b, contract):
    return lax.dot_general(a, b, ((contract[:1], contract[1:]), ((), ())), preferred_element_type=jnp.float32)


def in_hbm(v):
    return pltpu.with_memory_space_constraint(v, pltpu.HBM)


def gated_parts(pre_gate):
    logistic = jax.nn.sigmoid(pre_gate)
    return (pre_gate * logistic, logistic * (1.0 + pre_gate * (1.0 - logistic)))


def ring_order(size):
    return [0] + list(range(1, size, 2)) + list(range(2, size, 2))[::-1]


def pack_kernel(tokens, upstream, expert_ids, slots, gate_fixed, out, route, sem):
    top_count, tok_rows = expert_ids.shape
    copies = [
        pltpu.make_async_copy(src, out.at[pl.ds(i * tok_rows, tok_rows), :], sem.at[i])
        for i, src in enumerate((tokens, upstream))
    ]
    for copy in copies:
        copy.start()
    gate = gate_fixed[...]
    route[...] = jnp.zeros_like(route)
    for i, field in enumerate((expert_ids[...], slots[...], gate >> 8, gate & 255)):
        empty = jnp.zeros((ROUTE_ROWS - top_count, tok_rows), jnp.float32)
        field = jnp.concatenate([field.astype(jnp.float32), empty], axis=0)
        route[:, i * tok_rows : (i + 1) * tok_rows] = field.astype(jnp.bfloat16)
    copies.append(pltpu.make_async_copy(route, out.at[pl.ds(2 * tok_rows, ROUTE_ROWS), :], sem.at[2]))
    copies[2].start()
    for copy in copies:
        copy.wait()


def pack_call(tokens, upstream, expert_ids, slots, gate_fixed):
    tok_rows, width = tokens.shape
    vmem, hbm = (pl.BlockSpec(memory_space=m) for m in (pltpu.VMEM, pltpu.HBM))
    operands = [in_hbm(v) for v in (tokens, upstream, expert_ids.T, slots.T, gate_fixed.T)]
    return pl.pallas_call(
        pack_kernel,
        in_specs=[hbm] * 2 + [vmem] * 3,
        out_specs=pl.BlockSpec(memory_space=pl.ANY),
        out_shape=jax.ShapeDtypeStruct((2 * tok_rows + ROUTE_ROWS, width), jnp.bfloat16),
        scratch_shapes=[pltpu.VMEM((ROUTE_ROWS, width), jnp.bfloat16), pltpu.SemaphoreType.DMA((3,))],
        name="pack",
    )(*operands)


def route_keys(route, first_expert, local_experts, capacity, rows, offset, tok_rows, top_count, per_group):
    field = lambda i: route[:top_count, i * tok_rows : (i + 1) * tok_rows]
    expert = field(0).astype(jnp.int32) - first_expert
    slot = field(1).astype(jnp.int32)
    gate = (field(2) * 256.0 + field(3)) / 65536.0
    valid = (expert >= 0) & (expert < local_experts) & (slot < capacity)
    key = jnp.where(valid, expert * rows + offset + slot, -1)
    gate = jnp.where(valid, gate, 0.0)
    pairs = []
    for i in range(per_group):
        key_out, gate_out = key[i : i + 1, :], gate[i : i + 1, :]
        for j in range(i + per_group, top_count, per_group):
            key_out = jnp.maximum(key_out, key[j : j + 1, :])
            gate_out = jnp.maximum(gate_out, gate[j : j + 1, :])
        pairs.append((key_out, gate_out))
    return pairs


def chunk_kernel(n_blocks, tok_rows, capacity, rows, top_count, per_group, first_ref, *refs):
    payloads, weights = refs[:n_blocks], refs[n_blocks : n_blocks + 3]
    parts, kept = refs[n_blocks + 3 : -16], refs[-16:-13]
    x_all, u_all, routes, w_gate, w_up, w_down, back_all, x_rows, s_rows, hids = refs[-13:-3]
    sem_in, sem_weight, sem_out = refs[-3:]
    experts, width, ff = w_gate.shape

    def fetch(b, start, size, to, i):
        copy = pltpu.make_async_copy(payloads[b].at[pl.ds(start, size), :], to, sem_in.at[b, i])
        copy.start()
        return copy

    here = [pl.ds(b * tok_rows, tok_rows) for b in range(n_blocks)]
    get_route = [fetch(b, 2 * tok_rows, ROUTE_ROWS, routes.at[b], 0) for b in range(n_blocks)]
    get_x = [fetch(b, 0, tok_rows, x_all.at[here[b], :], 1) for b in range(n_blocks)]
    get_u = [fetch(b, tok_rows, tok_rows, u_all.at[here[b], :], 2) for b in range(n_blocks)]
    get_weight = [
        [
            pltpu.make_async_copy(src.at[e], to.at[e], sem_weight.at[e, i])
            for i, (src, to) in enumerate(zip(weights, (w_gate, w_up, w_down)))
        ]
        for e in range(experts)
    ]
    for copies in get_weight:
        for copy in copies:
            copy.start()
    keep = []

    def keep_out(i, e, src):
        copy = pltpu.make_async_copy(src.at[e], kept[i].at[e], sem_out.at[e, i])
        copy.start()
        keep.append(copy)

    pairs = []
    for b in range(n_blocks):
        get_route[b].wait()
        route = routes[b].astype(jnp.float32)
        pairs.append(
            route_keys(route, first_ref[0], experts, capacity, rows, b * capacity, tok_rows, top_count, per_group)
        )
    place = lax.broadcasted_iota(jnp.int32, (experts * rows, n_blocks * tok_rows), 0)
    hot = jnp.zeros(place.shape, jnp.float32)
    gate_hot = jnp.zeros(place.shape, jnp.float32)
    for i in range(per_group):
        key = jnp.concatenate([pair[i][0] for pair in pairs], axis=1)
        gate = jnp.concatenate([pair[i][1] for pair in pairs], axis=1)
        match = place == key
        hot = jnp.where(match, 1.0, hot)
        gate_hot = jnp.where(match, gate, gate_hot)
    hot = hot.astype(jnp.bfloat16)
    row_gate = jnp.sum(gate_hot, axis=1, keepdims=True)

    for copy in get_x:
        copy.wait()
    gathered = dot(hot, x_all[...], (1, 0)).astype(jnp.bfloat16)
    for e in range(experts):
        x_rows[e] = gathered[e * rows : (e + 1) * rows, :]
        keep_out(0, e, x_rows)
    for copy in get_u:
        copy.wait()
    scaled = (dot(hot, u_all[...], (1, 0)) * row_gate).astype(jnp.bfloat16)
    for e in range(experts):
        s_rows[e] = scaled[e * rows : (e + 1) * rows, :]
        keep_out(1, e, s_rows)

    for e in range(experts):
        for copy in get_weight[e]:
            copy.wait()
        pre_gate = dot(x_rows[e], w_gate[e], (1, 0))
        pre_up = dot(x_rows[e], w_up[e], (1, 0))
        grad_hidden = dot(s_rows[e], w_down[e], (1, 1))
        active, slope = gated_parts(pre_gate)
        grad_gate_pre = (grad_hidden * pre_up * slope).astype(jnp.bfloat16)
        grad_up_pre = (grad_hidden * active).astype(jnp.bfloat16)
        hids[e, :, :ff] = grad_gate_pre
        hids[e, :, ff : 2 * ff] = grad_up_pre
        hids[e, :, 2 * ff :] = (active * pre_up).astype(jnp.bfloat16)
        keep_out(2, e, hids)
        back = dot(grad_gate_pre, w_gate[e], (1, 1)) + dot(grad_up_pre, w_up[e], (1, 1))
        back_all[e * rows : (e + 1) * rows, :] = back.astype(jnp.bfloat16)

    summed = dot(hot, back_all[...], (0, 0)).astype(jnp.bfloat16)
    start = 0
    for part in parts:
        part[...] = summed[start : start + part.shape[0], :]
        start += part.shape[0]
    for copy in keep:
        copy.wait()


def chunk_call(payloads, first_expert, weights, tok_rows, capacity, rows, top_count, per_group, joined):
    n_blocks = len(payloads)
    n_tok = n_blocks * tok_rows
    experts, width, ff = weights[0].shape
    part_shapes = [(n_tok, width)] if joined else [(tok_rows, width), (n_tok - tok_rows, width)]
    kept_shapes = [(experts, rows, width), (experts, rows, width), (experts, rows, 3 * ff)]
    smem, vmem, hbm = (pl.BlockSpec(memory_space=m) for m in (pltpu.SMEM, pltpu.VMEM, pltpu.HBM))
    buffer = lambda *shape: pltpu.VMEM(shape, jnp.bfloat16)
    semaphores = lambda *shape: pltpu.SemaphoreType.DMA(shape)
    return pl.pallas_call(
        functools.partial(chunk_kernel, n_blocks, tok_rows, capacity, rows, top_count, per_group),
        in_specs=[smem] + [pl.BlockSpec(memory_space=pl.ANY)] * n_blocks + [hbm] * 3,
        out_specs=[vmem] * len(part_shapes) + [hbm] * 3,
        out_shape=[jax.ShapeDtypeStruct(shape, jnp.bfloat16) for shape in part_shapes]
        + [pltpu.HBM(shape, jnp.bfloat16) for shape in kept_shapes],
        scratch_shapes=[
            buffer(n_tok, width),
            buffer(n_tok, width),
            buffer(n_blocks, ROUTE_ROWS, width),
            buffer(experts, width, ff),
            buffer(experts, width, ff),
            buffer(experts, ff, width),
            buffer(experts * rows, width),
            *[buffer(*shape) for shape in kept_shapes],
            semaphores(n_blocks, 3),
            semaphores(experts, 3),
            semaphores(experts, 3),
        ],
        compiler_params=pltpu.CompilerParams(vmem_limit_bytes=VMEM_LIMIT),
        cost_estimate=pl.CostEstimate(
            flops=2 * experts * rows * width * (5 * ff + 3 * n_tok),
            bytes_accessed=6 * experts * width * ff + 8 * n_tok * width,
            transcendentals=0,
        ),
        name="chunk",
    )(first_expert, *payloads, *[in_hbm(w) for w in weights])


def halves_of(n, ff, refs):
    cat = lambda part: jnp.concatenate([ref[0] for ref in part], axis=0)
    x_rows, s_rows, hid = cat(refs[:n]), cat(refs[n : 2 * n]), cat(refs[2 * n : 3 * n])
    return dot(x_rows, hid[:, : 2 * ff], (0, 0)), dot(hid[:, 2 * ff :], s_rows, (0, 0))


def send_kernel(n, ff, half_ref, *refs):
    gate_up, down = halves_of(n, ff, refs)
    out = refs[3 * n]
    depth = gate_up.shape[0]
    out[0, :depth, :] = gate_up.astype(jnp.bfloat16)
    out[0, depth:, :] = down.astype(jnp.bfloat16)


def keep_kernel(n, ff, half_ref, *refs):
    gate_up, down = halves_of(n, ff, refs)
    got = refs[3 * n]
    out_gate, out_up, out_down = refs[3 * n + 1 :]
    depth = gate_up.shape[0]
    gate_up = gate_up + got[0, :depth, :].astype(jnp.float32)
    out_gate[0] = gate_up[:, :ff].astype(jnp.bfloat16)
    out_up[0] = gate_up[:, ff:].astype(jnp.bfloat16)
    out_down[0] = (down + got[0, depth:, :].astype(jnp.float32)).astype(jnp.bfloat16)


def weight_call(half, x_rows, s_rows, hids, got=None):
    n = len(x_rows)
    experts, rows, width = x_rows[0].shape
    ff = hids[0].shape[2] // 3
    depth = width // 2
    piece = lambda shape: pl.BlockSpec((1,) + shape, lambda e, half: (e, 0, 0))
    split = pl.BlockSpec((1, rows, depth), lambda e, half: (e, 0, half[0]))
    in_specs = [split] * (2 * n) + [piece((rows, 3 * ff))] * n
    operands = [in_hbm(v) for v in (*x_rows, *s_rows, *hids)]
    packed = (depth + ff, depth)
    if got is None:
        kernel = send_kernel
        out_specs = piece(packed)
        out_shape = jax.ShapeDtypeStruct((experts,) + packed, jnp.bfloat16)
    else:
        kernel = keep_kernel
        in_specs = in_specs + [piece(packed)]
        operands = operands + [got]
        shapes = [(depth, ff), (depth, ff), (ff, depth)]
        out_specs = [piece(s) for s in shapes]
        out_shape = [jax.ShapeDtypeStruct((experts,) + s, jnp.bfloat16) for s in shapes]
    return pl.pallas_call(
        functools.partial(kernel, n, ff),
        grid_spec=pltpu.PrefetchScalarGridSpec(
            num_scalar_prefetch=1, grid=(experts,), in_specs=in_specs, out_specs=out_specs
        ),
        out_shape=out_shape,
        compiler_params=pltpu.CompilerParams(vmem_limit_bytes=VMEM_LIMIT),
        cost_estimate=pl.CostEstimate(
            flops=2 * experts * n * rows * 3 * ff * depth,
            bytes_accessed=2 * experts * (n * rows * (width + 3 * ff) + 3 * ff * depth),
            transcendentals=0,
        ),
        name="weight_grads",
    )(half, *operands)


def per_device(tokens, upstream, expert_ids, gate_fixed, slots, w_gate, w_up, w_down):
    local_experts = w_gate.shape[0]
    n_group = lax.axis_size("group")
    n_ingroup = lax.axis_size("ingroup")
    experts_all = local_experts * n_group * n_ingroup
    tok_rows, top_count = expert_ids.shape
    width = tokens.shape[1]
    per_group = top_count // GROUPS_TOK
    capacity = max(2, 3 * tok_rows * top_count // (2 * experts_all))
    rows = -(-n_ingroup * capacity // 16) * 16
    z, x, core = (lax.axis_index(a) for a in ("group", "ingroup", "dp"))
    first_expert = ((z * n_ingroup + x) * local_experts).astype(jnp.int32).reshape(1)
    half = core.astype(jnp.int32).reshape(1)
    weights = (w_gate, w_up, w_down)
    wide = lambda v: v.astype(jnp.float32)
    tie = lambda *trees: lax.optimization_barrier(trees)
    order = ring_order(n_group)
    along = lambda k: [(order[i], order[(i + k) % n_group]) for i in range(n_group)]
    shift = lambda s: [(i, (i + s) % n_ingroup) for i in range(n_ingroup)]

    def spread(column):
        return [column] + [lax.ppermute(column, "ingroup", shift(s)) for s in range(1, n_ingroup)]

    def chunk(blocks, joined=False):
        return chunk_call(blocks, first_expert, weights, tok_rows, capacity, rows, top_count, per_group, joined)

    def across(others):
        return [
            lax.ppermute(others[(s - 1) * tok_rows : s * tok_rows], "ingroup", shift(-s)) for s in range(1, n_ingroup)
        ]

    def homeward(part, backs, k):
        group_part = wide(part)
        for back in backs:
            group_part = group_part + wide(back)
        return lax.ppermute(group_part.astype(jnp.bfloat16), "group", along(-k))

    column = pack_call(tokens, upstream, expert_ids, slots, gate_fixed)
    blocks, chunks, near, backs, sent = {}, {}, None, {}, {}
    for k in range(n_group):
        ahead = lax.ppermute(column, "group", along(1)) if k < n_group - 1 else None
        pair = spread(column)
        if k > 0:
            chunks[k - 1] = chunk(blocks[k - 1], k - 1 == 1)
        if k > 2 and near is None:
            near = lax.ppermute(chunks[1][0], "group", along(-1))
        blocks[k], column, chunks, near = tie(pair, ahead, chunks, near)

    last = n_group - 1
    for k in range(2, last):
        backs[k] = across(chunks[k][1])
    backs[0] = across((wide(chunks[0][1]) + wide(near[tok_rows:])).astype(jnp.bfloat16))
    chunks[last] = chunk(blocks[last])
    kept = [[chunks[k][i] for k in range(n_group)] for i in (-3, -2, -1)]
    to_send = weight_call(1 - half, *kept)
    chunks, backs, to_send = tie(chunks, backs, to_send)
    backs[last] = across(chunks[last][1])
    got = lax.ppermute(to_send, "dp", [(0, 1), (1, 0)])
    for k in range(2, n_group):
        sent[k] = homeward(chunks[k][0], backs[k], k)
    total = wide(chunks[0][0]) + wide(near[:tok_rows])
    for back in backs[0]:
        total = total + wide(back)
    for k in range(2, n_group):
        total = total + wide(sent[k])
    grad_tokens = total.astype(jnp.bfloat16)

    x_rows, s_rows, hids = ([chunks[k][i] for k in range(n_group)] for i in (-3, -2, -1))
    grad_gate, grad_up, grad_down = weight_call(half, x_rows, s_rows, hids, got)
    return grad_tokens, grad_gate, grad_up, grad_down


def solution(mesh):
    rows_spec = P(("parts", "group", "ingroup", "dp"), None)
    weight_spec = P(("group", "ingroup"), None, None)
    out_specs = (
        rows_spec,
        P(("parts", "group", "ingroup"), "dp", None),
        P(("parts", "group", "ingroup"), "dp", None),
        P(("parts", "group", "ingroup"), None, "dp"),
    )
    return jax.shard_map(
        per_device,
        mesh=mesh,
        in_specs=(rows_spec,) * 5 + (weight_spec,) * 3,
        out_specs=out_specs,
        check_vma=False,
    )
```

```python
import functools

import jax
import jax.numpy as jnp
from jax import lax
from jax.experimental import pallas as pl
from jax.experimental.pallas import tpu as pltpu
from jax.sharding import PartitionSpec as P

GROUPS_TOK = 4
ROUTE_ROWS = 16
VMEM_LIMIT = 32 * 1024 * 1024


def dot(a, b, contract):
    return lax.dot_general(a, b, ((contract[:1], contract[1:]), ((), ())), preferred_element_type=jnp.float32)


def in_hbm(v):
    return pltpu.with_memory_space_constraint(v, pltpu.HBM)


def gated_parts(pre_gate):
    logistic = jax.nn.sigmoid(pre_gate)
    return (pre_gate * logistic, logistic * (1.0 + pre_gate * (1.0 - logistic)))


def ring_order(size):
    return [0] + list(range(1, size, 2)) + list(range(2, size, 2))[::-1]


def pack_kernel(tokens, upstream, expert_ids, slots, gate_fixed, out, sem):
    top_count, tok_rows = expert_ids.shape
    copies = [
        pltpu.make_async_copy(src, out.at[pl.ds(i * tok_rows, tok_rows), :], sem.at[i])
        for i, src in enumerate((tokens, upstream))
    ]
    for copy in copies:
        copy.start()
    gate = gate_fixed[...]
    out[2 * tok_rows :, :] = jnp.zeros((ROUTE_ROWS, out.shape[1]), jnp.bfloat16)
    for i, field in enumerate((expert_ids[...], slots[...], gate >> 8, gate & 255)):
        empty = jnp.zeros((ROUTE_ROWS - top_count, tok_rows), jnp.float32)
        field = jnp.concatenate([field.astype(jnp.float32), empty], axis=0)
        out[2 * tok_rows :, i * tok_rows : (i + 1) * tok_rows] = field.astype(jnp.bfloat16)
    for copy in copies:
        copy.wait()


def pack_call(tokens, upstream, expert_ids, slots, gate_fixed):
    tok_rows, width = tokens.shape
    vmem, hbm = (pl.BlockSpec(memory_space=m) for m in (pltpu.VMEM, pltpu.HBM))
    operands = [in_hbm(v) for v in (tokens, upstream, expert_ids.T, slots.T, gate_fixed.T)]
    return pl.pallas_call(
        pack_kernel,
        in_specs=[hbm] * 2 + [vmem] * 3,
        out_specs=vmem,
        out_shape=jax.ShapeDtypeStruct((2 * tok_rows + ROUTE_ROWS, width), jnp.bfloat16),
        scratch_shapes=[pltpu.SemaphoreType.DMA((2,))],
        name="pack",
    )(*operands)


def route_keys(route, first_expert, local_experts, capacity, rows, offset, tok_rows, top_count, per_group):
    field = lambda i: route[:top_count, i * tok_rows : (i + 1) * tok_rows]
    expert = field(0).astype(jnp.int32) - first_expert
    slot = field(1).astype(jnp.int32)
    gate = (field(2) * 256.0 + field(3)) / 65536.0
    valid = (expert >= 0) & (expert < local_experts) & (slot < capacity)
    key = jnp.where(valid, expert * rows + offset + slot, -1)
    gate = jnp.where(valid, gate, 0.0)
    pairs = []
    for i in range(per_group):
        key_out, gate_out = key[i : i + 1, :], gate[i : i + 1, :]
        for j in range(i + per_group, top_count, per_group):
            key_out = jnp.maximum(key_out, key[j : j + 1, :])
            gate_out = jnp.maximum(gate_out, gate[j : j + 1, :])
        pairs.append((key_out, gate_out))
    return pairs


def chunk_kernel(n_blocks, tok_rows, capacity, rows, top_count, per_group, first_ref, *refs):
    payloads, weights = refs[:n_blocks], refs[n_blocks : n_blocks + 3]
    parts, kept = refs[n_blocks + 3 : -16], refs[-16:-13]
    x_all, u_all, routes, w_gate, w_up, w_down, back_all, x_rows, s_rows, hids = refs[-13:-3]
    sem_in, sem_weight, sem_out = refs[-3:]
    experts, width, ff = w_gate.shape

    def fetch(b, start, size, to, i):
        copy = pltpu.make_async_copy(payloads[b].at[pl.ds(start, size), :], to, sem_in.at[b, i])
        copy.start()
        return copy

    here = [pl.ds(b * tok_rows, tok_rows) for b in range(n_blocks)]
    get_route = [fetch(b, 2 * tok_rows, ROUTE_ROWS, routes.at[b], 0) for b in range(n_blocks)]
    get_x = [fetch(b, 0, tok_rows, x_all.at[here[b], :], 1) for b in range(n_blocks)]
    get_u = [fetch(b, tok_rows, tok_rows, u_all.at[here[b], :], 2) for b in range(n_blocks)]
    get_weight = [
        [
            pltpu.make_async_copy(src.at[e], to.at[e], sem_weight.at[e, i])
            for i, (src, to) in enumerate(zip(weights, (w_gate, w_up, w_down)))
        ]
        for e in range(experts)
    ]
    for copies in get_weight:
        for copy in copies:
            copy.start()
    keep = []

    def keep_out(i, e, src):
        copy = pltpu.make_async_copy(src.at[e], kept[i].at[e], sem_out.at[e, i])
        copy.start()
        keep.append(copy)

    pairs = []
    for b in range(n_blocks):
        get_route[b].wait()
        route = routes[b].astype(jnp.float32)
        pairs.append(
            route_keys(route, first_ref[0], experts, capacity, rows, b * capacity, tok_rows, top_count, per_group)
        )
    place = lax.broadcasted_iota(jnp.int32, (experts * rows, n_blocks * tok_rows), 0)
    hot = jnp.zeros(place.shape, jnp.float32)
    gate_hot = jnp.zeros(place.shape, jnp.float32)
    for i in range(per_group):
        key = jnp.concatenate([pair[i][0] for pair in pairs], axis=1)
        gate = jnp.concatenate([pair[i][1] for pair in pairs], axis=1)
        match = place == key
        hot = jnp.where(match, 1.0, hot)
        gate_hot = jnp.where(match, gate, gate_hot)
    hot = hot.astype(jnp.bfloat16)
    row_gate = jnp.sum(gate_hot, axis=1, keepdims=True)

    for copy in get_x:
        copy.wait()
    gathered = dot(hot, x_all[...], (1, 0)).astype(jnp.bfloat16)
    for e in range(experts):
        x_rows[e] = gathered[e * rows : (e + 1) * rows, :]
        keep_out(0, e, x_rows)
    for copy in get_u:
        copy.wait()
    scaled = (dot(hot, u_all[...], (1, 0)) * row_gate).astype(jnp.bfloat16)
    for e in range(experts):
        s_rows[e] = scaled[e * rows : (e + 1) * rows, :]
        keep_out(1, e, s_rows)

    for e in range(experts):
        for copy in get_weight[e]:
            copy.wait()
        pre_gate = dot(x_rows[e], w_gate[e], (1, 0))
        pre_up = dot(x_rows[e], w_up[e], (1, 0))
        grad_hidden = dot(s_rows[e], w_down[e], (1, 1))
        active, slope = gated_parts(pre_gate)
        grad_gate_pre = (grad_hidden * pre_up * slope).astype(jnp.bfloat16)
        grad_up_pre = (grad_hidden * active).astype(jnp.bfloat16)
        hids[e, :, :ff] = grad_gate_pre
        hids[e, :, ff : 2 * ff] = grad_up_pre
        hids[e, :, 2 * ff :] = (active * pre_up).astype(jnp.bfloat16)
        keep_out(2, e, hids)
        back = dot(grad_gate_pre, w_gate[e], (1, 1)) + dot(grad_up_pre, w_up[e], (1, 1))
        back_all[e * rows : (e + 1) * rows, :] = back.astype(jnp.bfloat16)

    summed = dot(hot, back_all[...], (0, 0)).astype(jnp.bfloat16)
    start = 0
    for part in parts:
        part[...] = summed[start : start + part.shape[0], :]
        start += part.shape[0]
    for copy in keep:
        copy.wait()


def chunk_call(payloads, first_expert, weights, tok_rows, capacity, rows, top_count, per_group, joined):
    n_blocks = len(payloads)
    n_tok = n_blocks * tok_rows
    experts, width, ff = weights[0].shape
    part_shapes = [(n_tok, width)] if joined else [(tok_rows, width), (n_tok - tok_rows, width)]
    kept_shapes = [(experts, rows, width), (experts, rows, width), (experts, rows, 3 * ff)]
    smem, vmem, hbm = (pl.BlockSpec(memory_space=m) for m in (pltpu.SMEM, pltpu.VMEM, pltpu.HBM))
    buffer = lambda *shape: pltpu.VMEM(shape, jnp.bfloat16)
    semaphores = lambda *shape: pltpu.SemaphoreType.DMA(shape)
    return pl.pallas_call(
        functools.partial(chunk_kernel, n_blocks, tok_rows, capacity, rows, top_count, per_group),
        in_specs=[smem] + [pl.BlockSpec(memory_space=pl.ANY)] * n_blocks + [hbm] * 3,
        out_specs=[vmem] * len(part_shapes) + [hbm] * 3,
        out_shape=[jax.ShapeDtypeStruct(shape, jnp.bfloat16) for shape in part_shapes]
        + [pltpu.HBM(shape, jnp.bfloat16) for shape in kept_shapes],
        scratch_shapes=[
            buffer(n_tok, width),
            buffer(n_tok, width),
            buffer(n_blocks, ROUTE_ROWS, width),
            buffer(experts, width, ff),
            buffer(experts, width, ff),
            buffer(experts, ff, width),
            buffer(experts * rows, width),
            *[buffer(*shape) for shape in kept_shapes],
            semaphores(n_blocks, 3),
            semaphores(experts, 3),
            semaphores(experts, 3),
        ],
        compiler_params=pltpu.CompilerParams(vmem_limit_bytes=VMEM_LIMIT),
        cost_estimate=pl.CostEstimate(
            flops=2 * experts * rows * width * (5 * ff + 3 * n_tok),
            bytes_accessed=6 * experts * width * ff + 8 * n_tok * width,
            transcendentals=0,
        ),
        name="chunk",
    )(first_expert, *payloads, *[in_hbm(w) for w in weights])


def halves_of(n, ff, refs):
    cat = lambda part: jnp.concatenate([ref[0] for ref in part], axis=0)
    x_rows, s_rows, hid = cat(refs[:n]), cat(refs[n : 2 * n]), cat(refs[2 * n : 3 * n])
    return dot(x_rows, hid[:, : 2 * ff], (0, 0)), dot(hid[:, 2 * ff :], s_rows, (0, 0))


def send_kernel(n, ff, half_ref, *refs):
    gate_up, down = halves_of(n, ff, refs)
    out = refs[3 * n]
    depth = gate_up.shape[0]
    out[0, :depth, :] = gate_up.astype(jnp.bfloat16)
    out[0, depth:, :] = down.astype(jnp.bfloat16)


def keep_kernel(n, ff, half_ref, *refs):
    gate_up, down = halves_of(n, ff, refs)
    got = refs[3 * n]
    out_gate, out_up, out_down = refs[3 * n + 1 :]
    depth = gate_up.shape[0]
    gate_up = gate_up + got[0, :depth, :].astype(jnp.float32)
    out_gate[0] = gate_up[:, :ff].astype(jnp.bfloat16)
    out_up[0] = gate_up[:, ff:].astype(jnp.bfloat16)
    out_down[0] = (down + got[0, depth:, :].astype(jnp.float32)).astype(jnp.bfloat16)


def weight_call(half, x_rows, s_rows, hids, got=None):
    n = len(x_rows)
    experts, rows, width = x_rows[0].shape
    ff = hids[0].shape[2] // 3
    depth = width // 2
    piece = lambda shape: pl.BlockSpec((1,) + shape, lambda e, half: (e, 0, 0))
    split = pl.BlockSpec((1, rows, depth), lambda e, half: (e, 0, half[0]))
    in_specs = [split] * (2 * n) + [piece((rows, 3 * ff))] * n
    operands = [in_hbm(v) for v in (*x_rows, *s_rows, *hids)]
    packed = (depth + ff, depth)
    if got is None:
        kernel = send_kernel
        out_specs = piece(packed)
        out_shape = jax.ShapeDtypeStruct((experts,) + packed, jnp.bfloat16)
    else:
        kernel = keep_kernel
        in_specs = in_specs + [piece(packed)]
        operands = operands + [got]
        shapes = [(depth, ff), (depth, ff), (ff, depth)]
        out_specs = [piece(s) for s in shapes]
        out_shape = [jax.ShapeDtypeStruct((experts,) + s, jnp.bfloat16) for s in shapes]
    return pl.pallas_call(
        functools.partial(kernel, n, ff),
        grid_spec=pltpu.PrefetchScalarGridSpec(
            num_scalar_prefetch=1, grid=(experts,), in_specs=in_specs, out_specs=out_specs
        ),
        out_shape=out_shape,
        compiler_params=pltpu.CompilerParams(vmem_limit_bytes=VMEM_LIMIT),
        cost_estimate=pl.CostEstimate(
            flops=2 * experts * n * rows * 3 * ff * depth,
            bytes_accessed=2 * experts * (n * rows * (width + 3 * ff) + 3 * ff * depth),
            transcendentals=0,
        ),
        name="weight_grads",
    )(half, *operands)


def per_device(tokens, upstream, expert_ids, gate_fixed, slots, w_gate, w_up, w_down):
    local_experts = w_gate.shape[0]
    n_group = lax.axis_size("group")
    n_ingroup = lax.axis_size("ingroup")
    experts_all = local_experts * n_group * n_ingroup
    tok_rows, top_count = expert_ids.shape
    width = tokens.shape[1]
    per_group = top_count // GROUPS_TOK
    capacity = max(2, 3 * tok_rows * top_count // (2 * experts_all))
    rows = -(-n_ingroup * capacity // 16) * 16
    z, x, core = (lax.axis_index(a) for a in ("group", "ingroup", "dp"))
    first_expert = ((z * n_ingroup + x) * local_experts).astype(jnp.int32).reshape(1)
    half = core.astype(jnp.int32).reshape(1)
    weights = (w_gate, w_up, w_down)
    wide = lambda v: v.astype(jnp.float32)
    tie = lambda *trees: lax.optimization_barrier(trees)
    order = ring_order(n_group)
    along = lambda k: [(order[i], order[(i + k) % n_group]) for i in range(n_group)]
    shift = lambda s: [(i, (i + s) % n_ingroup) for i in range(n_ingroup)]

    def spread(column):
        return [column] + [lax.ppermute(column, "ingroup", shift(s)) for s in range(1, n_ingroup)]

    def chunk(blocks, joined=False):
        return chunk_call(blocks, first_expert, weights, tok_rows, capacity, rows, top_count, per_group, joined)

    def across(others):
        return [
            lax.ppermute(others[(s - 1) * tok_rows : s * tok_rows], "ingroup", shift(-s)) for s in range(1, n_ingroup)
        ]

    def group_sum(part, backs):
        group_part = wide(part)
        for back in backs:
            group_part = group_part + wide(back)
        return group_part.astype(jnp.bfloat16)

    def homeward(group_part, k):
        return lax.ppermute(group_part, "group", along(-k))

    column = pack_call(tokens, upstream, expert_ids, slots, gate_fixed)
    blocks, chunks, near, backs, sent = {}, {}, None, {}, {}
    for k in range(n_group):
        ahead = lax.ppermute(column, "group", along(1)) if k < n_group - 1 else None
        pair = spread(column)
        if k > 0:
            chunks[k - 1] = chunk(blocks[k - 1], k - 1 == 1)
        if k > 2 and near is None:
            near = lax.ppermute(chunks[1][0], "group", along(-1))
        blocks[k], column, chunks, near = tie(pair, ahead, chunks, near)

    last = n_group - 1
    for k in range(2, last):
        backs[k] = across(chunks[k][1])
    backs[0] = across((wide(chunks[0][1]) + wide(near[tok_rows:])).astype(jnp.bfloat16))
    chunks[last] = chunk(blocks[last])
    backs[last] = across(chunks[last][1])
    x_rows, s_rows, hids = ([chunks[k][i] for k in range(n_group)] for i in (-3, -2, -1))
    group_parts = {k: group_sum(chunks[k][0], backs[k]) for k in range(2, last)}
    kept, group_parts, backs[0] = tie((x_rows, s_rows, hids), group_parts, backs[0])
    for k in range(2, last):
        sent[k] = homeward(group_parts[k], k)
    to_send = weight_call(1 - half, *kept)
    to_send, backs[last], sent = tie(to_send, backs[last], sent)
    got = lax.ppermute(to_send, "dp", [(0, 1), (1, 0)])
    group_parts[last] = group_sum(chunks[last][0], backs[last])
    sent[last] = homeward(group_parts[last], last)
    got, _ = tie(got, group_parts[last])
    grads = weight_call(half, *kept, got)
    grads, sent = tie(grads, sent)
    total = wide(chunks[0][0]) + wide(near[:tok_rows])
    for back in backs[0]:
        total = total + wide(back)
    for k in range(2, n_group):
        total = total + wide(sent[k])
    return (total.astype(jnp.bfloat16), *grads)


def solution(mesh):
    rows_spec = P(("parts", "group", "ingroup", "dp"), None)
    weight_spec = P(("group", "ingroup"), None, None)
    out_specs = (
        rows_spec,
        P(("parts", "group", "ingroup"), "dp", None),
        P(("parts", "group", "ingroup"), "dp", None),
        P(("parts", "group", "ingroup"), None, "dp"),
    )
    return jax.shard_map(
        per_device,
        mesh=mesh,
        in_specs=(rows_spec,) * 5 + (weight_spec,) * 3,
        out_specs=out_specs,
        check_vma=False,
    )
```

```python
import functools

import jax
import jax.numpy as jnp
from jax import lax
from jax.experimental import pallas as pl
from jax.experimental.pallas import tpu as pltpu
from jax.sharding import PartitionSpec as P

GROUPS_TOK = 4
ROUTE_ROWS = 16
VMEM_LIMIT = 32 * 1024 * 1024


def dot(a, b, contract):
    return lax.dot_general(a, b, ((contract[:1], contract[1:]), ((), ())), preferred_element_type=jnp.float32)


def in_hbm(v):
    return pltpu.with_memory_space_constraint(v, pltpu.HBM)


def gated_parts(pre_gate):
    logistic = jax.nn.sigmoid(pre_gate)
    return (pre_gate * logistic, logistic * (1.0 + pre_gate * (1.0 - logistic)))


def ring_order(size):
    return [0] + list(range(1, size, 2)) + list(range(2, size, 2))[::-1]


def pack_kernel(tokens, upstream, expert_ids, slots, gate_fixed, out, sem):
    top_count, tok_rows = expert_ids.shape
    copies = [
        pltpu.make_async_copy(src, out.at[pl.ds(i * tok_rows, tok_rows), :], sem.at[i])
        for i, src in enumerate((tokens, upstream))
    ]
    for copy in copies:
        copy.start()
    gate = gate_fixed[...]
    out[2 * tok_rows :, :] = jnp.zeros((ROUTE_ROWS, out.shape[1]), jnp.bfloat16)
    for i, field in enumerate((expert_ids[...], slots[...], gate >> 8, gate & 255)):
        empty = jnp.zeros((ROUTE_ROWS - top_count, tok_rows), jnp.float32)
        field = jnp.concatenate([field.astype(jnp.float32), empty], axis=0)
        out[2 * tok_rows :, i * tok_rows : (i + 1) * tok_rows] = field.astype(jnp.bfloat16)
    for copy in copies:
        copy.wait()


def pack_call(tokens, upstream, expert_ids, slots, gate_fixed):
    tok_rows, width = tokens.shape
    vmem, hbm = (pl.BlockSpec(memory_space=m) for m in (pltpu.VMEM, pltpu.HBM))
    operands = [in_hbm(v) for v in (tokens, upstream, expert_ids.T, slots.T, gate_fixed.T)]
    return pl.pallas_call(
        pack_kernel,
        in_specs=[hbm] * 2 + [vmem] * 3,
        out_specs=vmem,
        out_shape=jax.ShapeDtypeStruct((2 * tok_rows + ROUTE_ROWS, width), jnp.bfloat16),
        scratch_shapes=[pltpu.SemaphoreType.DMA((2,))],
        name="pack",
    )(*operands)


def route_keys(route, first_expert, local_experts, capacity, rows, offset, tok_rows, top_count, per_group):
    field = lambda i: route[:top_count, i * tok_rows : (i + 1) * tok_rows]
    expert = field(0).astype(jnp.int32) - first_expert
    slot = field(1).astype(jnp.int32)
    gate = (field(2) * 256.0 + field(3)) / 65536.0
    valid = (expert >= 0) & (expert < local_experts) & (slot < capacity)
    key = jnp.where(valid, expert * rows + offset + slot, -1)
    gate = jnp.where(valid, gate, 0.0)
    pairs = []
    for i in range(per_group):
        key_out, gate_out = key[i : i + 1, :], gate[i : i + 1, :]
        for j in range(i + per_group, top_count, per_group):
            key_out = jnp.maximum(key_out, key[j : j + 1, :])
            gate_out = jnp.maximum(gate_out, gate[j : j + 1, :])
        pairs.append((key_out, gate_out))
    return pairs


def chunk_kernel(n_blocks, tok_rows, capacity, rows, top_count, per_group, first_ref, *refs):
    payloads, weights = refs[:n_blocks], refs[n_blocks : n_blocks + 3]
    parts, kept = refs[n_blocks + 3 : -16], refs[-16:-13]
    x_all, u_all, routes, w_gate, w_up, w_down, back_all, x_rows, s_rows, hids = refs[-13:-3]
    sem_in, sem_weight, sem_out = refs[-3:]
    experts, width, ff = w_gate.shape

    def fetch(b, start, size, to, i):
        copy = pltpu.make_async_copy(payloads[b].at[pl.ds(start, size), :], to, sem_in.at[b, i])
        copy.start()
        return copy

    here = [pl.ds(b * tok_rows, tok_rows) for b in range(n_blocks)]
    get_route = [fetch(b, 2 * tok_rows, ROUTE_ROWS, routes.at[b], 0) for b in range(n_blocks)]
    get_x = [fetch(b, 0, tok_rows, x_all.at[here[b], :], 1) for b in range(n_blocks)]
    get_u = [fetch(b, tok_rows, tok_rows, u_all.at[here[b], :], 2) for b in range(n_blocks)]
    get_weight = [
        [
            pltpu.make_async_copy(src.at[e], to.at[e], sem_weight.at[e, i])
            for i, (src, to) in enumerate(zip(weights, (w_gate, w_up, w_down)))
        ]
        for e in range(experts)
    ]
    for copies in get_weight:
        for copy in copies:
            copy.start()
    keep = []

    def keep_out(i, e, src):
        copy = pltpu.make_async_copy(src.at[e], kept[i].at[e], sem_out.at[e, i])
        copy.start()
        keep.append(copy)

    pairs = []
    for b in range(n_blocks):
        get_route[b].wait()
        route = routes[b].astype(jnp.float32)
        pairs.append(
            route_keys(route, first_ref[0], experts, capacity, rows, b * capacity, tok_rows, top_count, per_group)
        )
    place = lax.broadcasted_iota(jnp.int32, (experts * rows, n_blocks * tok_rows), 0)
    hot = jnp.zeros(place.shape, jnp.float32)
    gate_hot = jnp.zeros(place.shape, jnp.float32)
    for i in range(per_group):
        key = jnp.concatenate([pair[i][0] for pair in pairs], axis=1)
        gate = jnp.concatenate([pair[i][1] for pair in pairs], axis=1)
        match = place == key
        hot = jnp.where(match, 1.0, hot)
        gate_hot = jnp.where(match, gate, gate_hot)
    hot = hot.astype(jnp.bfloat16)
    row_gate = jnp.sum(gate_hot, axis=1, keepdims=True)

    for copy in get_x:
        copy.wait()
    gathered = dot(hot, x_all[...], (1, 0)).astype(jnp.bfloat16)
    for e in range(experts):
        x_rows[e] = gathered[e * rows : (e + 1) * rows, :]
        keep_out(0, e, x_rows)
    for copy in get_u:
        copy.wait()
    scaled = (dot(hot, u_all[...], (1, 0)) * row_gate).astype(jnp.bfloat16)
    for e in range(experts):
        s_rows[e] = scaled[e * rows : (e + 1) * rows, :]
        keep_out(1, e, s_rows)

    for e in range(experts):
        for copy in get_weight[e]:
            copy.wait()
        pre_gate = dot(x_rows[e], w_gate[e], (1, 0))
        pre_up = dot(x_rows[e], w_up[e], (1, 0))
        grad_hidden = dot(s_rows[e], w_down[e], (1, 1))
        active, slope = gated_parts(pre_gate)
        grad_gate_pre = (grad_hidden * pre_up * slope).astype(jnp.bfloat16)
        grad_up_pre = (grad_hidden * active).astype(jnp.bfloat16)
        hids[e, :, :ff] = grad_gate_pre
        hids[e, :, ff : 2 * ff] = grad_up_pre
        hids[e, :, 2 * ff :] = (active * pre_up).astype(jnp.bfloat16)
        keep_out(2, e, hids)
        back = dot(grad_gate_pre, w_gate[e], (1, 1)) + dot(grad_up_pre, w_up[e], (1, 1))
        back_all[e * rows : (e + 1) * rows, :] = back.astype(jnp.bfloat16)

    summed = dot(hot, back_all[...], (0, 0)).astype(jnp.bfloat16)
    start = 0
    for part in parts:
        part[...] = summed[start : start + part.shape[0], :]
        start += part.shape[0]
    for copy in keep:
        copy.wait()


def chunk_call(payloads, first_expert, weights, tok_rows, capacity, rows, top_count, per_group, joined):
    n_blocks = len(payloads)
    n_tok = n_blocks * tok_rows
    experts, width, ff = weights[0].shape
    part_shapes = [(n_tok, width)] if joined else [(tok_rows, width), (n_tok - tok_rows, width)]
    kept_shapes = [(experts, rows, width), (experts, rows, width), (experts, rows, 3 * ff)]
    smem, vmem, hbm = (pl.BlockSpec(memory_space=m) for m in (pltpu.SMEM, pltpu.VMEM, pltpu.HBM))
    buffer = lambda *shape: pltpu.VMEM(shape, jnp.bfloat16)
    semaphores = lambda *shape: pltpu.SemaphoreType.DMA(shape)
    return pl.pallas_call(
        functools.partial(chunk_kernel, n_blocks, tok_rows, capacity, rows, top_count, per_group),
        in_specs=[smem] + [pl.BlockSpec(memory_space=pl.ANY)] * n_blocks + [hbm] * 3,
        out_specs=[vmem] * len(part_shapes) + [hbm] * 3,
        out_shape=[jax.ShapeDtypeStruct(shape, jnp.bfloat16) for shape in part_shapes]
        + [pltpu.HBM(shape, jnp.bfloat16) for shape in kept_shapes],
        scratch_shapes=[
            buffer(n_tok, width),
            buffer(n_tok, width),
            buffer(n_blocks, ROUTE_ROWS, width),
            buffer(experts, width, ff),
            buffer(experts, width, ff),
            buffer(experts, ff, width),
            buffer(experts * rows, width),
            *[buffer(*shape) for shape in kept_shapes],
            semaphores(n_blocks, 3),
            semaphores(experts, 3),
            semaphores(experts, 3),
        ],
        compiler_params=pltpu.CompilerParams(vmem_limit_bytes=VMEM_LIMIT),
        cost_estimate=pl.CostEstimate(
            flops=2 * experts * rows * width * (5 * ff + 3 * n_tok),
            bytes_accessed=6 * experts * width * ff + 8 * n_tok * width,
            transcendentals=0,
        ),
        name="chunk",
    )(first_expert, *payloads, *[in_hbm(w) for w in weights])


def halves_of(n, ff, refs):
    cat = lambda part: jnp.concatenate([ref[0] for ref in part], axis=0)
    x_rows, s_rows, hid = cat(refs[:n]), cat(refs[n : 2 * n]), cat(refs[2 * n : 3 * n])
    return dot(x_rows, hid[:, : 2 * ff], (0, 0)), dot(hid[:, 2 * ff :], s_rows, (0, 0))


def send_kernel(n, ff, half_ref, *refs):
    gate_up, down = halves_of(n, ff, refs)
    out = refs[3 * n]
    depth = gate_up.shape[0]
    out[0, :depth, :] = gate_up.astype(jnp.bfloat16)
    out[0, depth:, :] = down.astype(jnp.bfloat16)


def keep_kernel(n, ff, half_ref, *refs):
    gate_up, down = halves_of(n, ff, refs)
    got = refs[3 * n]
    out_gate, out_up, out_down = refs[3 * n + 1 :]
    depth = gate_up.shape[0]
    gate_up = gate_up + got[0, :depth, :].astype(jnp.float32)
    out_gate[0] = gate_up[:, :ff].astype(jnp.bfloat16)
    out_up[0] = gate_up[:, ff:].astype(jnp.bfloat16)
    out_down[0] = (down + got[0, depth:, :].astype(jnp.float32)).astype(jnp.bfloat16)


def weight_call(half, x_rows, s_rows, hids, got=None):
    n = len(x_rows)
    experts, rows, width = x_rows[0].shape
    ff = hids[0].shape[2] // 3
    depth = width // 2
    piece = lambda shape: pl.BlockSpec((1,) + shape, lambda e, half: (e, 0, 0))
    split = pl.BlockSpec((1, rows, depth), lambda e, half: (e, 0, half[0]))
    in_specs = [split] * (2 * n) + [piece((rows, 3 * ff))] * n
    operands = [in_hbm(v) for v in (*x_rows, *s_rows, *hids)]
    packed = (depth + ff, depth)
    if got is None:
        kernel = send_kernel
        out_specs = piece(packed)
        out_shape = jax.ShapeDtypeStruct((experts,) + packed, jnp.bfloat16)
    else:
        kernel = keep_kernel
        in_specs = in_specs + [piece(packed)]
        operands = operands + [got]
        shapes = [(depth, ff), (depth, ff), (ff, depth)]
        out_specs = [piece(s) for s in shapes]
        out_shape = [jax.ShapeDtypeStruct((experts,) + s, jnp.bfloat16) for s in shapes]
    return pl.pallas_call(
        functools.partial(kernel, n, ff),
        grid_spec=pltpu.PrefetchScalarGridSpec(
            num_scalar_prefetch=1, grid=(experts,), in_specs=in_specs, out_specs=out_specs
        ),
        out_shape=out_shape,
        compiler_params=pltpu.CompilerParams(vmem_limit_bytes=VMEM_LIMIT),
        cost_estimate=pl.CostEstimate(
            flops=2 * experts * n * rows * 3 * ff * depth,
            bytes_accessed=2 * experts * (n * rows * (width + 3 * ff) + 3 * ff * depth),
            transcendentals=0,
        ),
        name="weight_grads",
    )(half, *operands)


def per_device(tokens, upstream, expert_ids, gate_fixed, slots, w_gate, w_up, w_down):
    local_experts = w_gate.shape[0]
    n_group = lax.axis_size("group")
    n_ingroup = lax.axis_size("ingroup")
    experts_all = local_experts * n_group * n_ingroup
    tok_rows, top_count = expert_ids.shape
    width = tokens.shape[1]
    per_group = top_count // GROUPS_TOK
    capacity = max(2, 3 * tok_rows * top_count // (2 * experts_all))
    rows = -(-n_ingroup * capacity // 16) * 16
    z, x, core = (lax.axis_index(a) for a in ("group", "ingroup", "dp"))
    first_expert = ((z * n_ingroup + x) * local_experts).astype(jnp.int32).reshape(1)
    half = core.astype(jnp.int32).reshape(1)
    weights = (w_gate, w_up, w_down)
    wide = lambda v: v.astype(jnp.float32)
    tie = lambda *trees: lax.optimization_barrier(trees)
    order = ring_order(n_group)
    along = lambda k: [(order[i], order[(i + k) % n_group]) for i in range(n_group)]
    shift = lambda s: [(i, (i + s) % n_ingroup) for i in range(n_ingroup)]

    def spread(column):
        return [column] + [lax.ppermute(column, "ingroup", shift(s)) for s in range(1, n_ingroup)]

    def chunk(blocks, joined=False):
        return chunk_call(blocks, first_expert, weights, tok_rows, capacity, rows, top_count, per_group, joined)

    def across(others):
        return [
            lax.ppermute(others[(s - 1) * tok_rows : s * tok_rows], "ingroup", shift(-s)) for s in range(1, n_ingroup)
        ]

    def group_sum(part, backs):
        group_part = wide(part)
        for back in backs:
            group_part = group_part + wide(back)
        return group_part.astype(jnp.bfloat16)

    def homeward(group_part, k):
        return lax.ppermute(group_part, "group", along(-k))

    column = pack_call(tokens, upstream, expert_ids, slots, gate_fixed)
    blocks, chunks, backs, sent = {}, {}, {}, {}
    for k in range(n_group):
        ahead = lax.ppermute(column, "group", along(1)) if k < n_group - 1 else None
        pair = spread(column)
        if k > 0:
            chunks[k - 1] = chunk(blocks[k - 1], k - 1 == 1)
        blocks[k], column, chunks = tie(pair, ahead, chunks)

    last = n_group - 1
    for k in range(2, last - 1):
        sent[k] = homeward(group_sum(chunks[k][0], across(chunks[k][1])), k)
    near = lax.ppermute(chunks[1][0], "group", along(-1))
    backs[last - 1] = across(chunks[last - 1][1])
    chunks[last] = chunk(blocks[last])
    chunks, near, backs = tie(chunks, near, backs)

    backs[last] = across(chunks[last][1])
    carried = homeward(group_sum(chunks[last - 1][0], backs[last - 1]), last)
    kept = [[chunks[k][i] for k in range(n_group)] for i in (-3, -2, -1)]
    to_send = weight_call(1 - half, *kept)
    to_send, backs[last], carried = tie(to_send, backs[last], carried)

    got = lax.ppermute(to_send, "dp", [(0, 1), (1, 0)])
    sent[last] = homeward(group_sum(chunks[last][0], [*backs[last], carried]), last)
    backs[0] = across((wide(chunks[0][1]) + wide(near[tok_rows:])).astype(jnp.bfloat16))
    grads = weight_call(half, *kept, got)
    grads, sent, backs[0] = tie(grads, sent, backs[0])
    total = wide(chunks[0][0]) + wide(near[:tok_rows])
    for back in backs[0]:
        total = total + wide(back)
    for back in sent.values():
        total = total + wide(back)
    return (total.astype(jnp.bfloat16), *grads)


def solution(mesh):
    rows_spec = P(("parts", "group", "ingroup", "dp"), None)
    weight_spec = P(("group", "ingroup"), None, None)
    out_specs = (
        rows_spec,
        P(("parts", "group", "ingroup"), "dp", None),
        P(("parts", "group", "ingroup"), "dp", None),
        P(("parts", "group", "ingroup"), None, "dp"),
    )
    return jax.shard_map(
        per_device,
        mesh=mesh,
        in_specs=(rows_spec,) * 5 + (weight_spec,) * 3,
        out_specs=out_specs,
        check_vma=False,
    )
```

```python
import functools

import jax
import jax.numpy as jnp
from jax import lax
from jax.experimental import pallas as pl
from jax.experimental.pallas import tpu as pltpu
from jax.sharding import PartitionSpec as P

GROUPS_TOK = 4
ROUTE_ROWS = 16
VMEM_LIMIT = 32 * 1024 * 1024


def dot(a, b, contract):
    return lax.dot_general(a, b, ((contract[:1], contract[1:]), ((), ())), preferred_element_type=jnp.float32)


def in_hbm(v):
    return pltpu.with_memory_space_constraint(v, pltpu.HBM)


def gated_parts(pre_gate):
    logistic = jax.nn.sigmoid(pre_gate)
    return (pre_gate * logistic, logistic * (1.0 + pre_gate * (1.0 - logistic)))


def ring_order(size):
    return [0] + list(range(1, size, 2)) + list(range(2, size, 2))[::-1]


def pack_kernel(tokens, upstream, expert_ids, slots, gate_fixed, out, sem):
    top_count, tok_rows = expert_ids.shape
    copies = [
        pltpu.make_async_copy(src, out.at[pl.ds(i * tok_rows, tok_rows), :], sem.at[i])
        for i, src in enumerate((tokens, upstream))
    ]
    for copy in copies:
        copy.start()
    gate = gate_fixed[...]
    out[2 * tok_rows :, :] = jnp.zeros((ROUTE_ROWS, out.shape[1]), jnp.bfloat16)
    for i, field in enumerate((expert_ids[...], slots[...], gate >> 8, gate & 255)):
        empty = jnp.zeros((ROUTE_ROWS - top_count, tok_rows), jnp.float32)
        field = jnp.concatenate([field.astype(jnp.float32), empty], axis=0)
        out[2 * tok_rows :, i * tok_rows : (i + 1) * tok_rows] = field.astype(jnp.bfloat16)
    for copy in copies:
        copy.wait()


def pack_call(tokens, upstream, expert_ids, slots, gate_fixed):
    tok_rows, width = tokens.shape
    vmem, hbm = (pl.BlockSpec(memory_space=m) for m in (pltpu.VMEM, pltpu.HBM))
    operands = [in_hbm(v) for v in (tokens, upstream, expert_ids.T, slots.T, gate_fixed.T)]
    return pl.pallas_call(
        pack_kernel,
        in_specs=[hbm] * 2 + [vmem] * 3,
        out_specs=vmem,
        out_shape=jax.ShapeDtypeStruct((2 * tok_rows + ROUTE_ROWS, width), jnp.bfloat16),
        scratch_shapes=[pltpu.SemaphoreType.DMA((2,))],
        name="pack",
    )(*operands)


def route_keys(route, first_expert, local_experts, capacity, rows, offset, tok_rows, top_count, per_group):
    field = lambda i: route[:top_count, i * tok_rows : (i + 1) * tok_rows]
    expert = field(0).astype(jnp.int32) - first_expert
    slot = field(1).astype(jnp.int32)
    gate = (field(2) * 256.0 + field(3)) / 65536.0
    valid = (expert >= 0) & (expert < local_experts) & (slot < capacity)
    key = jnp.where(valid, expert * rows + offset + slot, -1)
    gate = jnp.where(valid, gate, 0.0)
    pairs = []
    for i in range(per_group):
        key_out, gate_out = key[i : i + 1, :], gate[i : i + 1, :]
        for j in range(i + per_group, top_count, per_group):
            key_out = jnp.maximum(key_out, key[j : j + 1, :])
            gate_out = jnp.maximum(gate_out, gate[j : j + 1, :])
        pairs.append((key_out, gate_out))
    return pairs


def chunk_kernel(n_blocks, tok_rows, capacity, rows, top_count, per_group, place_ref, *refs):
    payloads, weights = refs[:n_blocks], refs[n_blocks : n_blocks + 3]
    parts, kept = refs[n_blocks + 3 : -15], refs[-15:-13]
    x_all, u_all, routes, w_gate, w_up, w_down, back_all, x_rows, s_rows, hids = refs[-13:-3]
    sem_in, sem_weight, sem_out = refs[-3:]
    experts, width, ff = w_gate.shape

    def fetch(b, start, size, to, i):
        copy = pltpu.make_async_copy(payloads[b].at[pl.ds(start, size), :], to, sem_in.at[b, i])
        copy.start()
        return copy

    here = [pl.ds(b * tok_rows, tok_rows) for b in range(n_blocks)]
    get_route = [fetch(b, 2 * tok_rows, ROUTE_ROWS, routes.at[b], 0) for b in range(n_blocks)]
    get_x = [fetch(b, 0, tok_rows, x_all.at[here[b], :], 1) for b in range(n_blocks)]
    get_u = [fetch(b, tok_rows, tok_rows, u_all.at[here[b], :], 2) for b in range(n_blocks)]
    get_weight = [
        [
            pltpu.make_async_copy(src.at[e], to.at[e], sem_weight.at[e, i])
            for i, (src, to) in enumerate(zip(weights, (w_gate, w_up, w_down)))
        ]
        for e in range(experts)
    ]
    for copies in get_weight:
        for copy in copies:
            copy.start()
    keep = []
    depth = width // 2
    core = place_ref[1]

    def keep_out(e, src, start):
        for i, out in enumerate(kept):
            side = core if i == 0 else 1 - core
            cols = pl.ds(pl.multiple_of(side * depth, depth), depth) if src.shape[2] == width else slice(None)
            size = depth if src.shape[2] == width else src.shape[2]
            copy = pltpu.make_async_copy(
                src.at[e, :, cols], out.at[e, :, pl.ds(start, size)], sem_out.at[e, start // depth, i]
            )
            copy.start()
            keep.append(copy)

    pairs = []
    for b in range(n_blocks):
        get_route[b].wait()
        route = routes[b].astype(jnp.float32)
        pairs.append(
            route_keys(route, place_ref[0], experts, capacity, rows, b * capacity, tok_rows, top_count, per_group)
        )
    place = lax.broadcasted_iota(jnp.int32, (experts * rows, n_blocks * tok_rows), 0)
    hot = jnp.zeros(place.shape, jnp.float32)
    gate_hot = jnp.zeros(place.shape, jnp.float32)
    for i in range(per_group):
        key = jnp.concatenate([pair[i][0] for pair in pairs], axis=1)
        gate = jnp.concatenate([pair[i][1] for pair in pairs], axis=1)
        match = place == key
        hot = jnp.where(match, 1.0, hot)
        gate_hot = jnp.where(match, gate, gate_hot)
    hot = hot.astype(jnp.bfloat16)
    row_gate = jnp.sum(gate_hot, axis=1, keepdims=True)

    for copy in get_x:
        copy.wait()
    gathered = dot(hot, x_all[...], (1, 0)).astype(jnp.bfloat16)
    for e in range(experts):
        x_rows[e] = gathered[e * rows : (e + 1) * rows, :]
        keep_out(e, x_rows, 0)
    for copy in get_u:
        copy.wait()
    scaled = (dot(hot, u_all[...], (1, 0)) * row_gate).astype(jnp.bfloat16)
    for e in range(experts):
        s_rows[e] = scaled[e * rows : (e + 1) * rows, :]
        keep_out(e, s_rows, depth)

    for e in range(experts):
        for copy in get_weight[e]:
            copy.wait()
        pre_gate = dot(x_rows[e], w_gate[e], (1, 0))
        pre_up = dot(x_rows[e], w_up[e], (1, 0))
        grad_hidden = dot(s_rows[e], w_down[e], (1, 1))
        active, slope = gated_parts(pre_gate)
        grad_gate_pre = (grad_hidden * pre_up * slope).astype(jnp.bfloat16)
        grad_up_pre = (grad_hidden * active).astype(jnp.bfloat16)
        hids[e, :, :ff] = grad_gate_pre
        hids[e, :, ff : 2 * ff] = grad_up_pre
        hids[e, :, 2 * ff :] = (active * pre_up).astype(jnp.bfloat16)
        keep_out(e, hids, 2 * depth)
        back = dot(grad_gate_pre, w_gate[e], (1, 1)) + dot(grad_up_pre, w_up[e], (1, 1))
        back_all[e * rows : (e + 1) * rows, :] = back.astype(jnp.bfloat16)

    summed = dot(hot, back_all[...], (0, 0)).astype(jnp.bfloat16)
    start = 0
    for part in parts:
        part[...] = summed[start : start + part.shape[0], :]
        start += part.shape[0]
    for copy in keep:
        copy.wait()


def chunk_call(payloads, place, weights, tok_rows, capacity, rows, top_count, per_group, joined):
    n_blocks = len(payloads)
    n_tok = n_blocks * tok_rows
    experts, width, ff = weights[0].shape
    part_shapes = [(n_tok, width)] if joined else [(tok_rows, width), (n_tok - tok_rows, width)]
    kept_shape = (experts, rows, width + 3 * ff)
    smem, vmem, hbm = (pl.BlockSpec(memory_space=m) for m in (pltpu.SMEM, pltpu.VMEM, pltpu.HBM))
    buffer = lambda *shape: pltpu.VMEM(shape, jnp.bfloat16)
    semaphores = lambda *shape: pltpu.SemaphoreType.DMA(shape)
    return pl.pallas_call(
        functools.partial(chunk_kernel, n_blocks, tok_rows, capacity, rows, top_count, per_group),
        in_specs=[smem] + [pl.BlockSpec(memory_space=pl.ANY)] * n_blocks + [hbm] * 3,
        out_specs=[vmem] * len(part_shapes) + [hbm] * 2,
        out_shape=[jax.ShapeDtypeStruct(shape, jnp.bfloat16) for shape in part_shapes]
        + [pltpu.HBM(kept_shape, jnp.bfloat16)] * 2,
        scratch_shapes=[
            buffer(n_tok, width),
            buffer(n_tok, width),
            buffer(n_blocks, ROUTE_ROWS, width),
            buffer(experts, width, ff),
            buffer(experts, width, ff),
            buffer(experts, ff, width),
            buffer(experts * rows, width),
            buffer(experts, rows, width),
            buffer(experts, rows, width),
            buffer(experts, rows, 3 * ff),
            semaphores(n_blocks, 3),
            semaphores(experts, 3),
            semaphores(experts, 3, 2),
        ],
        compiler_params=pltpu.CompilerParams(vmem_limit_bytes=VMEM_LIMIT),
        cost_estimate=pl.CostEstimate(
            flops=2 * experts * rows * width * (5 * ff + 3 * n_tok),
            bytes_accessed=6 * experts * width * ff + 8 * n_tok * width,
            transcendentals=0,
        ),
        name="chunk",
    )(place, *payloads, *[in_hbm(w) for w in weights])


def weight_kernel(ff, n, *refs):
    rows = jnp.concatenate([ref[0] for ref in refs[:n]], axis=0)
    out_gate, out_up, out_down = refs[-3:]
    depth = (rows.shape[1] - 3 * ff) // 2
    x_rows, s_rows, hid = rows[:, :depth], rows[:, depth : 2 * depth], rows[:, 2 * depth :]
    gate_up = dot(x_rows, hid[:, : 2 * ff], (0, 0))
    out_gate[0] = gate_up[:, :ff].astype(jnp.bfloat16)
    out_up[0] = gate_up[:, ff:].astype(jnp.bfloat16)
    out_down[0] = dot(hid[:, 2 * ff :], s_rows, (0, 0)).astype(jnp.bfloat16)


def weight_call(kept, ff, first, count, before):
    n = len(kept)
    experts, rows, width = kept[0].shape
    depth = (width - 3 * ff) // 2
    piece = lambda shape: pl.BlockSpec((1,) + shape, lambda e: (e + first, 0, 0))
    shapes = [(depth, ff), (depth, ff), (ff, depth)]
    return pl.pallas_call(
        functools.partial(weight_kernel, ff, n),
        grid=(count,),
        in_specs=[piece((rows, width))] * n + [pl.BlockSpec(memory_space=pl.ANY)] * len(before),
        out_specs=[piece(s) for s in shapes],
        out_shape=[jax.ShapeDtypeStruct((experts,) + s, jnp.bfloat16) for s in shapes],
        input_output_aliases={n + i: i for i in range(len(before))},
        compiler_params=pltpu.CompilerParams(vmem_limit_bytes=VMEM_LIMIT),
        cost_estimate=pl.CostEstimate(
            flops=2 * count * n * rows * 3 * ff * depth,
            bytes_accessed=2 * count * (n * rows * width + 3 * ff * depth),
            transcendentals=0,
        ),
        name="weight_grads",
    )(*kept, *before)


def per_device(tokens, upstream, expert_ids, gate_fixed, slots, w_gate, w_up, w_down):
    local_experts = w_gate.shape[0]
    n_group = lax.axis_size("group")
    n_ingroup = lax.axis_size("ingroup")
    experts_all = local_experts * n_group * n_ingroup
    tok_rows, top_count = expert_ids.shape
    width = tokens.shape[1]
    per_group = top_count // GROUPS_TOK
    capacity = max(2, 3 * tok_rows * top_count // (2 * experts_all))
    rows = -(-n_ingroup * capacity // 16) * 16
    z, x, core = (lax.axis_index(a) for a in ("group", "ingroup", "dp"))
    place = jnp.stack([(z * n_ingroup + x) * local_experts, core]).astype(jnp.int32)
    weights = (w_gate, w_up, w_down)
    wide = lambda v: v.astype(jnp.float32)
    tie = lambda *trees: lax.optimization_barrier(trees)
    order = ring_order(n_group)
    along = lambda k: [(order[i], order[(i + k) % n_group]) for i in range(n_group)]
    shift = lambda s: [(i, (i + s) % n_ingroup) for i in range(n_ingroup)]

    def spread(column):
        return [column] + [lax.ppermute(column, "ingroup", shift(s)) for s in range(1, n_ingroup)]

    def chunk(blocks, joined=False):
        return chunk_call(blocks, place, weights, tok_rows, capacity, rows, top_count, per_group, joined)

    def across(others):
        return [
            lax.ppermute(others[(s - 1) * tok_rows : s * tok_rows], "ingroup", shift(-s)) for s in range(1, n_ingroup)
        ]

    def group_sum(part, backs):
        group_part = wide(part)
        for back in backs:
            group_part = group_part + wide(back)
        return group_part.astype(jnp.bfloat16)

    def homeward(group_part, k):
        return lax.ppermute(group_part, "group", along(-k))

    column = pack_call(tokens, upstream, expert_ids, slots, gate_fixed)
    def give(k):
        return lax.ppermute(chunks[k][-1], "dp", [(0, 1), (1, 0)])

    blocks, chunks, backs, sent, theirs = {}, {}, {}, {}, {}
    for k in range(n_group):
        ahead = lax.ppermute(column, "group", along(1)) if k < n_group - 1 else None
        pair = spread(column)
        if k > 1:
            theirs[k - 2] = give(k - 2)
        if k > 0:
            chunks[k - 1] = chunk(blocks[k - 1], k - 1 == 1)
        blocks[k], column, chunks, theirs = tie(pair, ahead, chunks, theirs)

    last = n_group - 1
    for k in range(2, last - 1):
        sent[k] = homeward(group_sum(chunks[k][0], across(chunks[k][1])), k)
    near = lax.ppermute(chunks[1][0], "group", along(-1))
    backs[last - 1] = across(chunks[last - 1][1])
    theirs[last - 1] = give(last - 1)
    chunks[last] = chunk(blocks[last])
    chunks, near, backs, theirs = tie(chunks, near, backs, theirs)

    theirs[last] = give(last)
    backs[last] = across(chunks[last][1])
    carried = homeward(group_sum(chunks[last - 1][0], backs[last - 1]), last)
    kept = [in_hbm(chunks[k][-2]) for k in range(n_group)] + [theirs[k] for k in range(n_group)]
    ff = w_gate.shape[2]
    grads = weight_call(kept, ff, 0, local_experts // 2, [])
    other = (wide(chunks[0][1]) + wide(near[tok_rows:])).astype(jnp.bfloat16)
    grads, backs[last], carried, other = tie(grads, backs[last], carried, other)

    sent[last] = homeward(group_sum(chunks[last][0], [*backs[last], carried]), last)
    backs[0] = across(other)
    grads = weight_call(kept, ff, local_experts // 2, local_experts - local_experts // 2, grads)
    grads, sent, backs[0] = tie(grads, sent, backs[0])
    total = wide(chunks[0][0]) + wide(near[:tok_rows])
    for back in backs[0]:
        total = total + wide(back)
    for back in sent.values():
        total = total + wide(back)
    return (total.astype(jnp.bfloat16), *grads)


def solution(mesh):
    rows_spec = P(("parts", "group", "ingroup", "dp"), None)
    weight_spec = P(("group", "ingroup"), None, None)
    out_specs = (
        rows_spec,
        P(("parts", "group", "ingroup"), "dp", None),
        P(("parts", "group", "ingroup"), "dp", None),
        P(("parts", "group", "ingroup"), None, "dp"),
    )
    return jax.shard_map(
        per_device,
        mesh=mesh,
        in_specs=(rows_spec,) * 5 + (weight_spec,) * 3,
        out_specs=out_specs,
        check_vma=False,
    )
```

```python
import functools

import jax
import jax.numpy as jnp
from jax import lax
from jax.experimental import pallas as pl
from jax.experimental.pallas import tpu as pltpu
from jax.sharding import PartitionSpec as P

GROUPS_TOK = 4
ROUTE_ROWS = 16
VMEM_LIMIT = 24 * 1024 * 1024


def dot(a, b, contract):
    return lax.dot_general(a, b, ((contract[:1], contract[1:]), ((), ())), preferred_element_type=jnp.float32)


def in_hbm(v):
    return pltpu.with_memory_space_constraint(v, pltpu.HBM)


def in_vmem(v):
    return pltpu.with_memory_space_constraint(v, pltpu.VMEM)


def gated_parts(pre_gate):
    logistic = jax.nn.sigmoid(pre_gate)
    return (pre_gate * logistic, logistic * (1.0 + pre_gate * (1.0 - logistic)))


def ring_order(size):
    return [0] + list(range(1, size, 2)) + list(range(2, size, 2))[::-1]


def pack_kernel(tokens, upstream, expert_ids, slots, gate_fixed, out, sem):
    top_count, tok_rows = expert_ids.shape
    copies = [
        pltpu.make_async_copy(src, out.at[pl.ds(i * tok_rows, tok_rows), :], sem.at[i])
        for i, src in enumerate((tokens, upstream))
    ]
    for copy in copies:
        copy.start()
    gate = gate_fixed[...]
    out[2 * tok_rows :, :] = jnp.zeros((ROUTE_ROWS, out.shape[1]), jnp.bfloat16)
    for i, field in enumerate((expert_ids[...], slots[...], gate >> 8, gate & 255)):
        empty = jnp.zeros((ROUTE_ROWS - top_count, tok_rows), jnp.float32)
        field = jnp.concatenate([field.astype(jnp.float32), empty], axis=0)
        out[2 * tok_rows :, i * tok_rows : (i + 1) * tok_rows] = field.astype(jnp.bfloat16)
    for copy in copies:
        copy.wait()


def pack_call(tokens, upstream, expert_ids, slots, gate_fixed):
    tok_rows, width = tokens.shape
    vmem, hbm = (pl.BlockSpec(memory_space=m) for m in (pltpu.VMEM, pltpu.HBM))
    operands = [in_hbm(v) for v in (tokens, upstream, expert_ids.T, slots.T, gate_fixed.T)]
    return pl.pallas_call(
        pack_kernel,
        in_specs=[hbm] * 2 + [vmem] * 3,
        out_specs=vmem,
        out_shape=pltpu.VMEM((2 * tok_rows + ROUTE_ROWS, width), jnp.bfloat16),
        scratch_shapes=[pltpu.SemaphoreType.DMA((2,))],
        compiler_params=pltpu.CompilerParams(vmem_limit_bytes=VMEM_LIMIT),
        name="pack",
    )(*operands)


def route_keys(route, first_expert, local_experts, capacity, rows, offset, tok_rows, top_count, per_group):
    field = lambda i: route[:top_count, i * tok_rows : (i + 1) * tok_rows]
    expert = field(0).astype(jnp.int32) - first_expert
    slot = field(1).astype(jnp.int32)
    gate = (field(2) * 256.0 + field(3)) / 65536.0
    valid = (expert >= 0) & (expert < local_experts) & (slot < capacity)
    key = jnp.where(valid, expert * rows + offset + slot, -1)
    gate = jnp.where(valid, gate, 0.0)
    pairs = []
    for i in range(per_group):
        key_out, gate_out = key[i : i + 1, :], gate[i : i + 1, :]
        for j in range(i + per_group, top_count, per_group):
            key_out = jnp.maximum(key_out, key[j : j + 1, :])
            gate_out = jnp.maximum(gate_out, gate[j : j + 1, :])
        pairs.append((key_out, gate_out))
    return pairs


def load_kernel(*refs):
    n = len(refs) // 2
    copies = [pltpu.make_async_copy(refs[i], refs[n + i], refs[-1].at[i]) for i in range(n)]
    for copy in copies:
        copy.start()
    for copy in copies:
        copy.wait()


def load_call(arrays):
    hbm, vmem = (pl.BlockSpec(memory_space=m) for m in (pltpu.HBM, pltpu.VMEM))
    return pl.pallas_call(
        load_kernel,
        in_specs=[hbm] * len(arrays),
        out_specs=[vmem] * len(arrays),
        out_shape=[pltpu.VMEM(v.shape, v.dtype) for v in arrays],
        scratch_shapes=[pltpu.SemaphoreType.DMA((len(arrays),))],
        compiler_params=pltpu.CompilerParams(vmem_limit_bytes=VMEM_LIMIT),
        name="load",
    )(*[in_hbm(v) for v in arrays])


def chunk_kernel(n_blocks, tok_rows, capacity, rows, top_count, per_group, first_ref, *refs):
    payloads = refs[:n_blocks]
    w_gate, w_up, w_down = refs[n_blocks : n_blocks + 3]
    parts = refs[n_blocks + 3 : -4]
    x_rows, s_rows, hids, back_all = refs[-4:]
    experts, width, ff = w_gate.shape

    pairs = []
    for b in range(n_blocks):
        route = payloads[b][2 * tok_rows : 2 * tok_rows + ROUTE_ROWS, :].astype(jnp.float32)
        pairs.append(
            route_keys(route, first_ref[0], experts, capacity, rows, b * capacity, tok_rows, top_count, per_group)
        )
    place = lax.broadcasted_iota(jnp.int32, (experts * rows, n_blocks * tok_rows), 0)
    hot = jnp.zeros(place.shape, jnp.float32)
    gate_hot = jnp.zeros(place.shape, jnp.float32)
    for i in range(per_group):
        key = jnp.concatenate([pair[i][0] for pair in pairs], axis=1)
        gate = jnp.concatenate([pair[i][1] for pair in pairs], axis=1)
        match = place == key
        hot = jnp.where(match, 1.0, hot)
        gate_hot = jnp.where(match, gate, gate_hot)
    hot = hot.astype(jnp.bfloat16)
    row_gate = jnp.sum(gate_hot, axis=1, keepdims=True)

    x_all = jnp.concatenate([payload[:tok_rows, :] for payload in payloads], axis=0)
    gathered = dot(hot, x_all, (1, 0)).astype(jnp.bfloat16)
    for e in range(experts):
        x_rows[e] = gathered[e * rows : (e + 1) * rows, :]
    u_all = jnp.concatenate([payload[tok_rows : 2 * tok_rows, :] for payload in payloads], axis=0)
    scaled = (dot(hot, u_all, (1, 0)) * row_gate).astype(jnp.bfloat16)
    for e in range(experts):
        s_rows[e] = scaled[e * rows : (e + 1) * rows, :]

    for e in range(experts):
        pre_gate = dot(x_rows[e], w_gate[e], (1, 0))
        pre_up = dot(x_rows[e], w_up[e], (1, 0))
        grad_hidden = dot(s_rows[e], w_down[e], (1, 1))
        active, slope = gated_parts(pre_gate)
        grad_gate_pre = (grad_hidden * pre_up * slope).astype(jnp.bfloat16)
        grad_up_pre = (grad_hidden * active).astype(jnp.bfloat16)
        hids[e, :, :ff] = grad_gate_pre
        hids[e, :, ff : 2 * ff] = grad_up_pre
        hids[e, :, 2 * ff :] = (active * pre_up).astype(jnp.bfloat16)
        back = dot(grad_gate_pre, w_gate[e], (1, 1)) + dot(grad_up_pre, w_up[e], (1, 1))
        back_all[e * rows : (e + 1) * rows, :] = back.astype(jnp.bfloat16)

    summed = dot(hot, back_all[...], (0, 0)).astype(jnp.bfloat16)
    start = 0
    for part in parts:
        part[...] = summed[start : start + part.shape[0], :]
        start += part.shape[0]


def chunk_call(payloads, first_expert, weights, tok_rows, capacity, rows, top_count, per_group, joined):
    n_blocks = len(payloads)
    n_tok = n_blocks * tok_rows
    experts, width, ff = weights[0].shape
    part_shapes = [(n_tok, width)] if joined else [(tok_rows, width), (n_tok - tok_rows, width)]
    kept_shapes = [(experts, rows, width), (experts, rows, width), (experts, rows, 3 * ff)]
    smem, vmem = (pl.BlockSpec(memory_space=m) for m in (pltpu.SMEM, pltpu.VMEM))
    out_shapes = part_shapes + kept_shapes
    return pl.pallas_call(
        functools.partial(chunk_kernel, n_blocks, tok_rows, capacity, rows, top_count, per_group),
        in_specs=[smem] + [vmem] * (n_blocks + 3),
        out_specs=[vmem] * len(out_shapes),
        out_shape=[pltpu.VMEM(shape, jnp.bfloat16) for shape in out_shapes],
        scratch_shapes=[pltpu.VMEM((experts * rows, width), jnp.bfloat16)],
        compiler_params=pltpu.CompilerParams(vmem_limit_bytes=VMEM_LIMIT),
        cost_estimate=pl.CostEstimate(
            flops=2 * experts * rows * width * (5 * ff + 3 * n_tok),
            bytes_accessed=6 * experts * width * ff + 8 * n_tok * width,
            transcendentals=0,
        ),
        name="chunk",
    )(first_expert, *[in_vmem(v) for v in payloads], *[in_vmem(w) for w in weights])


def halves_of(n, e, side, refs):
    depth = refs[0].shape[2] // 2
    cols = pl.ds(pl.multiple_of(side * depth, depth), depth)
    cat = lambda parts: jnp.concatenate(parts, axis=0)
    x_rows, s_rows = (cat([ref[e, :, cols] for ref in refs[i * n : (i + 1) * n]]) for i in range(2))
    hid = cat([ref[e] for ref in refs[2 * n : 3 * n]])
    ff = hid.shape[1] // 3
    return dot(x_rows, hid[:, : 2 * ff], (0, 0)), dot(hid[:, 2 * ff :], s_rows, (0, 0))


def send_kernel(n, side_ref, *refs):
    out = refs[3 * n]
    for e in range(out.shape[0]):
        gate_up, down = halves_of(n, e, side_ref[0], refs)
        depth = gate_up.shape[0]
        out[e, :depth, :] = gate_up.astype(jnp.bfloat16)
        out[e, depth:, :] = down.astype(jnp.bfloat16)


def keep_kernel(n, side_ref, *refs):
    got, outs = refs[3 * n], refs[3 * n + 1 : 3 * n + 4]
    buffers, sem = refs[3 * n + 4 : 3 * n + 7], refs[3 * n + 7]
    copies = []
    for e in range(got.shape[0]):
        gate_up, down = halves_of(n, e, side_ref[0], refs)
        depth = gate_up.shape[0]
        ff = down.shape[0]
        gate_up = gate_up + got[e, :depth, :].astype(jnp.float32)
        buffers[0][e] = gate_up[:, :ff].astype(jnp.bfloat16)
        buffers[1][e] = gate_up[:, ff:].astype(jnp.bfloat16)
        buffers[2][e] = (down + got[e, depth:, :].astype(jnp.float32)).astype(jnp.bfloat16)
        for i in range(3):
            copy = pltpu.make_async_copy(buffers[i].at[e], outs[i].at[e], sem.at[e, i])
            copy.start()
            copies.append(copy)
    for copy in copies:
        copy.wait()


def weight_call(side, x_rows, s_rows, hids, got=None):
    n = len(x_rows)
    experts, rows, width = x_rows[0].shape
    ff = hids[0].shape[2] // 3
    depth = width // 2
    smem, vmem = (pl.BlockSpec(memory_space=m) for m in (pltpu.SMEM, pltpu.VMEM))
    operands = [*x_rows, *s_rows, *hids]
    scratch = []
    if got is None:
        kernel, out_specs = send_kernel, vmem
        out_shape = pltpu.VMEM((experts, depth + ff, depth), jnp.bfloat16)
    else:
        kernel = keep_kernel
        operands = operands + [got]
        shapes = [(experts, depth, ff), (experts, depth, ff), (experts, ff, depth)]
        out_specs = [pl.BlockSpec(memory_space=pl.ANY)] * 3
        out_shape = [jax.ShapeDtypeStruct(s, jnp.bfloat16) for s in shapes]
        scratch = [pltpu.VMEM(s, jnp.bfloat16) for s in shapes] + [pltpu.SemaphoreType.DMA((experts, 3))]
    return pl.pallas_call(
        functools.partial(kernel, n),
        in_specs=[smem] + [vmem] * len(operands),
        out_specs=out_specs,
        out_shape=out_shape,
        scratch_shapes=scratch,
        compiler_params=pltpu.CompilerParams(vmem_limit_bytes=VMEM_LIMIT),
        cost_estimate=pl.CostEstimate(
            flops=2 * experts * n * rows * 3 * ff * depth,
            bytes_accessed=2 * experts * (n * rows * (width + 3 * ff) + 3 * ff * depth),
            transcendentals=0,
        ),
        name="weight_grads",
    )(side, *[in_vmem(v) for v in operands])


def per_device(tokens, upstream, expert_ids, gate_fixed, slots, w_gate, w_up, w_down):
    local_experts = w_gate.shape[0]
    n_group = lax.axis_size("group")
    n_ingroup = lax.axis_size("ingroup")
    experts_all = local_experts * n_group * n_ingroup
    tok_rows, top_count = expert_ids.shape
    width = tokens.shape[1]
    per_group = top_count // GROUPS_TOK
    capacity = max(2, 3 * tok_rows * top_count // (2 * experts_all))
    rows = -(-n_ingroup * capacity // 16) * 16
    z, x, core = (lax.axis_index(a) for a in ("group", "ingroup", "dp"))
    first_expert = ((z * n_ingroup + x) * local_experts).astype(jnp.int32).reshape(1)
    half = core.astype(jnp.int32).reshape(1)
    weights = load_call((w_gate, w_up, w_down))
    wide = lambda v: v.astype(jnp.float32)
    tie = lambda *trees: lax.optimization_barrier(trees)
    order = ring_order(n_group)
    along = lambda k: [(order[i], order[(i + k) % n_group]) for i in range(n_group)]
    shift = lambda s: [(i, (i + s) % n_ingroup) for i in range(n_ingroup)]

    def spread(column):
        return [column] + [lax.ppermute(column, "ingroup", shift(s)) for s in range(1, n_ingroup)]

    def chunk(blocks, joined=False):
        return chunk_call(blocks, first_expert, weights, tok_rows, capacity, rows, top_count, per_group, joined)

    def across(others):
        return [
            lax.ppermute(others[(s - 1) * tok_rows : s * tok_rows], "ingroup", shift(-s)) for s in range(1, n_ingroup)
        ]

    def group_sum(part, backs):
        group_part = wide(part)
        for back in backs:
            group_part = group_part + wide(back)
        return group_part.astype(jnp.bfloat16)

    def homeward(group_part, k):
        return lax.ppermute(group_part, "group", along(-k))

    column = pack_call(tokens, upstream, expert_ids, slots, gate_fixed)
    blocks, chunks, backs, sent = {}, {}, {}, {}
    for k in range(n_group):
        ahead = lax.ppermute(column, "group", along(1)) if k < n_group - 1 else None
        pair = spread(column)
        if k > 0:
            chunks[k - 1] = chunk(blocks[k - 1], k - 1 == 1)
        blocks[k], column, chunks, weights = tie(pair, ahead, chunks, weights)

    last = n_group - 1
    for k in range(2, last - 1):
        sent[k] = homeward(group_sum(chunks[k][0], across(chunks[k][1])), k)
    near = lax.ppermute(chunks[1][0], "group", along(-1))
    backs[last - 1] = across(chunks[last - 1][1])
    chunks[last] = chunk(blocks[last])
    chunks, near, backs = tie(chunks, near, backs)

    backs[last] = across(chunks[last][1])
    carried = homeward(group_sum(chunks[last - 1][0], backs[last - 1]), last)
    kept = [[chunks[k][i] for k in range(n_group)] for i in (-3, -2, -1)]
    to_send = weight_call(1 - half, *kept)
    to_send, backs[last], carried = tie(to_send, backs[last], carried)

    got = lax.ppermute(to_send, "dp", [(0, 1), (1, 0)])
    sent[last] = homeward(group_sum(chunks[last][0], [*backs[last], carried]), last)
    backs[0] = across((wide(chunks[0][1]) + wide(near[tok_rows:])).astype(jnp.bfloat16))
    grads = weight_call(half, *kept, got)
    grads, sent, backs[0] = tie(grads, sent, backs[0])
    total = wide(chunks[0][0]) + wide(near[:tok_rows])
    for back in backs[0]:
        total = total + wide(back)
    for back in sent.values():
        total = total + wide(back)
    return (total.astype(jnp.bfloat16), *grads)


def solution(mesh):
    rows_spec = P(("parts", "group", "ingroup", "dp"), None)
    weight_spec = P(("group", "ingroup"), None, None)
    out_specs = (
        rows_spec,
        P(("parts", "group", "ingroup"), "dp", None),
        P(("parts", "group", "ingroup"), "dp", None),
        P(("parts", "group", "ingroup"), None, "dp"),
    )
    return jax.shard_map(
        per_device,
        mesh=mesh,
        in_specs=(rows_spec,) * 5 + (weight_spec,) * 3,
        out_specs=out_specs,
        check_vma=False,
    )
```

```python
import functools

import jax
import jax.numpy as jnp
from jax import lax
from jax.experimental import pallas as pl
from jax.experimental.pallas import tpu as pltpu
from jax.sharding import PartitionSpec as P

GROUPS_TOK = 4
ROUTE_ROWS = 16
VMEM_LIMIT = 24 * 1024 * 1024


def dot(a, b, contract):
    return lax.dot_general(a, b, ((contract[:1], contract[1:]), ((), ())), preferred_element_type=jnp.float32)


def in_hbm(v):
    return pltpu.with_memory_space_constraint(v, pltpu.HBM)


def in_vmem(v):
    return pltpu.with_memory_space_constraint(v, pltpu.VMEM)


def gated_parts(pre_gate):
    logistic = jax.nn.sigmoid(pre_gate)
    return (pre_gate * logistic, logistic * (1.0 + pre_gate * (1.0 - logistic)))


def ring_order(size):
    return [0] + list(range(1, size, 2)) + list(range(2, size, 2))[::-1]


def pack_kernel(tokens, upstream, expert_ids, slots, gate_fixed, out, sem):
    top_count, tok_rows = expert_ids.shape
    copies = [
        pltpu.make_async_copy(src, out.at[pl.ds(i * tok_rows, tok_rows), :], sem.at[i])
        for i, src in enumerate((tokens, upstream))
    ]
    for copy in copies:
        copy.start()
    gate = gate_fixed[...]
    out[2 * tok_rows :, :] = jnp.zeros((ROUTE_ROWS, out.shape[1]), jnp.bfloat16)
    for i, field in enumerate((expert_ids[...], slots[...], gate >> 8, gate & 255)):
        empty = jnp.zeros((ROUTE_ROWS - top_count, tok_rows), jnp.float32)
        field = jnp.concatenate([field.astype(jnp.float32), empty], axis=0)
        out[2 * tok_rows :, i * tok_rows : (i + 1) * tok_rows] = field.astype(jnp.bfloat16)
    for copy in copies:
        copy.wait()


def pack_call(tokens, upstream, expert_ids, slots, gate_fixed):
    tok_rows, width = tokens.shape
    vmem, hbm = (pl.BlockSpec(memory_space=m) for m in (pltpu.VMEM, pltpu.HBM))
    operands = [in_hbm(v) for v in (tokens, upstream, expert_ids.T, slots.T, gate_fixed.T)]
    return pl.pallas_call(
        pack_kernel,
        in_specs=[hbm] * 2 + [vmem] * 3,
        out_specs=vmem,
        out_shape=pltpu.VMEM((2 * tok_rows + ROUTE_ROWS, width), jnp.bfloat16),
        scratch_shapes=[pltpu.SemaphoreType.DMA((2,))],
        compiler_params=pltpu.CompilerParams(vmem_limit_bytes=VMEM_LIMIT),
        name="pack",
    )(*operands)


def route_keys(route, first_expert, local_experts, capacity, rows, offset, tok_rows, top_count, per_group):
    field = lambda i: route[:top_count, i * tok_rows : (i + 1) * tok_rows]
    expert = field(0).astype(jnp.int32) - first_expert
    slot = field(1).astype(jnp.int32)
    gate = (field(2) * 256.0 + field(3)) / 65536.0
    valid = (expert >= 0) & (expert < local_experts) & (slot < capacity)
    key = jnp.where(valid, expert * rows + offset + slot, -1)
    gate = jnp.where(valid, gate, 0.0)
    pairs = []
    for i in range(per_group):
        key_out, gate_out = key[i : i + 1, :], gate[i : i + 1, :]
        for j in range(i + per_group, top_count, per_group):
            key_out = jnp.maximum(key_out, key[j : j + 1, :])
            gate_out = jnp.maximum(gate_out, gate[j : j + 1, :])
        pairs.append((key_out, gate_out))
    return pairs


def load_kernel(*refs):
    n = len(refs) // 2
    copies = [pltpu.make_async_copy(refs[i], refs[n + i], refs[-1].at[i]) for i in range(n)]
    for copy in copies:
        copy.start()
    for copy in copies:
        copy.wait()


def load_call(arrays):
    hbm, vmem = (pl.BlockSpec(memory_space=m) for m in (pltpu.HBM, pltpu.VMEM))
    return pl.pallas_call(
        load_kernel,
        in_specs=[hbm] * len(arrays),
        out_specs=[vmem] * len(arrays),
        out_shape=[pltpu.VMEM(v.shape, v.dtype) for v in arrays],
        scratch_shapes=[pltpu.SemaphoreType.DMA((len(arrays),))],
        compiler_params=pltpu.CompilerParams(vmem_limit_bytes=VMEM_LIMIT),
        name="load",
    )(*[in_hbm(v) for v in arrays])


def chunk_kernel(n_blocks, tok_rows, capacity, rows, top_count, per_group, first_ref, *refs):
    payloads = refs[:n_blocks]
    w_gate, w_up, w_down = refs[n_blocks : n_blocks + 3]
    parts = refs[n_blocks + 3 : -4]
    x_rows, s_rows, hids, back_all = refs[-4:]
    experts, width, ff = w_gate.shape

    pairs = []
    for b in range(n_blocks):
        route = payloads[b][2 * tok_rows : 2 * tok_rows + ROUTE_ROWS, :].astype(jnp.float32)
        pairs.append(
            route_keys(route, first_ref[0], experts, capacity, rows, b * capacity, tok_rows, top_count, per_group)
        )
    place = lax.broadcasted_iota(jnp.int32, (experts * rows, n_blocks * tok_rows), 0)
    hot = jnp.zeros(place.shape, jnp.float32)
    gate_hot = jnp.zeros(place.shape, jnp.float32)
    for i in range(per_group):
        key = jnp.concatenate([pair[i][0] for pair in pairs], axis=1)
        gate = jnp.concatenate([pair[i][1] for pair in pairs], axis=1)
        match = place == key
        hot = jnp.where(match, 1.0, hot)
        gate_hot = jnp.where(match, gate, gate_hot)
    hot = hot.astype(jnp.bfloat16)
    row_gate = jnp.sum(gate_hot, axis=1, keepdims=True)

    x_all = jnp.concatenate([payload[:tok_rows, :] for payload in payloads], axis=0)
    gathered = dot(hot, x_all, (1, 0)).astype(jnp.bfloat16)
    for e in range(experts):
        x_rows[e] = gathered[e * rows : (e + 1) * rows, :]
    u_all = jnp.concatenate([payload[tok_rows : 2 * tok_rows, :] for payload in payloads], axis=0)
    scaled = (dot(hot, u_all, (1, 0)) * row_gate).astype(jnp.bfloat16)
    for e in range(experts):
        s_rows[e] = scaled[e * rows : (e + 1) * rows, :]

    for e in range(experts):
        pre_gate = dot(x_rows[e], w_gate[e], (1, 0))
        pre_up = dot(x_rows[e], w_up[e], (1, 0))
        grad_hidden = dot(s_rows[e], w_down[e], (1, 1))
        active, slope = gated_parts(pre_gate)
        grad_gate_pre = (grad_hidden * pre_up * slope).astype(jnp.bfloat16)
        grad_up_pre = (grad_hidden * active).astype(jnp.bfloat16)
        hids[e, :, :ff] = grad_gate_pre
        hids[e, :, ff : 2 * ff] = grad_up_pre
        hids[e, :, 2 * ff :] = (active * pre_up).astype(jnp.bfloat16)
        back = dot(grad_gate_pre, w_gate[e], (1, 1)) + dot(grad_up_pre, w_up[e], (1, 1))
        back_all[e * rows : (e + 1) * rows, :] = back.astype(jnp.bfloat16)

    summed = dot(hot, back_all[...], (0, 0)).astype(jnp.bfloat16)
    start = 0
    for part in parts:
        part[...] = summed[start : start + part.shape[0], :]
        start += part.shape[0]


def chunk_call(payloads, first_expert, weights, tok_rows, capacity, rows, top_count, per_group, joined):
    n_blocks = len(payloads)
    n_tok = n_blocks * tok_rows
    experts, width, ff = weights[0].shape
    part_shapes = [(n_tok, width)] if joined else [(tok_rows, width), (n_tok - tok_rows, width)]
    kept_shapes = [(experts, rows, width), (experts, rows, width), (experts, rows, 3 * ff)]
    smem, vmem = (pl.BlockSpec(memory_space=m) for m in (pltpu.SMEM, pltpu.VMEM))
    out_shapes = part_shapes + kept_shapes
    return pl.pallas_call(
        functools.partial(chunk_kernel, n_blocks, tok_rows, capacity, rows, top_count, per_group),
        in_specs=[smem] + [vmem] * (n_blocks + 3),
        out_specs=[vmem] * len(out_shapes),
        out_shape=[pltpu.VMEM(shape, jnp.bfloat16) for shape in out_shapes],
        scratch_shapes=[pltpu.VMEM((experts * rows, width), jnp.bfloat16)],
        compiler_params=pltpu.CompilerParams(vmem_limit_bytes=VMEM_LIMIT),
        cost_estimate=pl.CostEstimate(
            flops=2 * experts * rows * width * (5 * ff + 3 * n_tok),
            bytes_accessed=6 * experts * width * ff + 8 * n_tok * width,
            transcendentals=0,
        ),
        name="chunk",
    )(first_expert, *[in_vmem(v) for v in payloads], *[in_vmem(w) for w in weights])


def halves_of(n, e, side, refs):
    depth = refs[0].shape[2] // 2
    cols = pl.ds(pl.multiple_of(side * depth, depth), depth)
    cat = lambda parts: jnp.concatenate(parts, axis=0)
    x_rows, s_rows = (cat([ref[e, :, cols] for ref in refs[i * n : (i + 1) * n]]) for i in range(2))
    hid = cat([ref[e] for ref in refs[2 * n : 3 * n]])
    ff = hid.shape[1] // 3
    return dot(x_rows, hid[:, : 2 * ff], (0, 0)), dot(hid[:, 2 * ff :], s_rows, (0, 0))


def send_kernel(n, side_ref, *refs):
    out = refs[3 * n]
    for e in range(out.shape[0]):
        gate_up, down = halves_of(n, e, side_ref[0], refs)
        depth = gate_up.shape[0]
        out[e, :depth, :] = gate_up.astype(jnp.bfloat16)
        out[e, depth:, :] = down.astype(jnp.bfloat16)


def keep_kernel(n, side_ref, *refs):
    got, outs = refs[3 * n], refs[3 * n + 1 : 3 * n + 4]
    buffers, sem = refs[3 * n + 4 : 3 * n + 7], refs[3 * n + 7]
    copies = []
    for e in range(got.shape[0]):
        gate_up, down = halves_of(n, e, side_ref[0], refs)
        depth = gate_up.shape[0]
        ff = down.shape[0]
        gate_up = gate_up + got[e, :depth, :].astype(jnp.float32)
        buffers[0][e] = gate_up[:, :ff].astype(jnp.bfloat16)
        buffers[1][e] = gate_up[:, ff:].astype(jnp.bfloat16)
        buffers[2][e] = (down + got[e, depth:, :].astype(jnp.float32)).astype(jnp.bfloat16)
        for i in range(3):
            copy = pltpu.make_async_copy(buffers[i].at[e], outs[i].at[e], sem.at[e, i])
            copy.start()
            copies.append(copy)
    for copy in copies:
        copy.wait()


def weight_call(side, x_rows, s_rows, hids, got=None):
    n = len(x_rows)
    experts, rows, width = x_rows[0].shape
    ff = hids[0].shape[2] // 3
    depth = width // 2
    smem, vmem = (pl.BlockSpec(memory_space=m) for m in (pltpu.SMEM, pltpu.VMEM))
    operands = [*x_rows, *s_rows, *hids]
    scratch = []
    if got is None:
        kernel, out_specs = send_kernel, vmem
        out_shape = pltpu.VMEM((experts, depth + ff, depth), jnp.bfloat16)
    else:
        kernel = keep_kernel
        operands = operands + [got]
        shapes = [(experts, depth, ff), (experts, depth, ff), (experts, ff, depth)]
        out_specs = [pl.BlockSpec(memory_space=pl.ANY)] * 3
        out_shape = [jax.ShapeDtypeStruct(s, jnp.bfloat16) for s in shapes]
        scratch = [pltpu.VMEM(s, jnp.bfloat16) for s in shapes] + [pltpu.SemaphoreType.DMA((experts, 3))]
    return pl.pallas_call(
        functools.partial(kernel, n),
        in_specs=[smem] + [vmem] * len(operands),
        out_specs=out_specs,
        out_shape=out_shape,
        scratch_shapes=scratch,
        compiler_params=pltpu.CompilerParams(vmem_limit_bytes=VMEM_LIMIT),
        cost_estimate=pl.CostEstimate(
            flops=2 * experts * n * rows * 3 * ff * depth,
            bytes_accessed=2 * experts * (n * rows * (width + 3 * ff) + 3 * ff * depth),
            transcendentals=0,
        ),
        name="weight_grads",
    )(side, *[in_vmem(v) for v in operands])


def per_device(tokens, upstream, expert_ids, gate_fixed, slots, w_gate, w_up, w_down):
    local_experts = w_gate.shape[0]
    n_group = lax.axis_size("group")
    n_ingroup = lax.axis_size("ingroup")
    experts_all = local_experts * n_group * n_ingroup
    tok_rows, top_count = expert_ids.shape
    width = tokens.shape[1]
    per_group = top_count // GROUPS_TOK
    capacity = max(2, 3 * tok_rows * top_count // (2 * experts_all))
    rows = -(-n_ingroup * capacity // 16) * 16
    z, x, core = (lax.axis_index(a) for a in ("group", "ingroup", "dp"))
    first_expert = ((z * n_ingroup + x) * local_experts).astype(jnp.int32).reshape(1)
    half = core.astype(jnp.int32).reshape(1)
    weights = load_call((w_gate, w_up, w_down))
    wide = lambda v: v.astype(jnp.float32)
    tie = lambda *trees: lax.optimization_barrier(trees)
    order = ring_order(n_group)
    along = lambda k: [(order[i], order[(i + k) % n_group]) for i in range(n_group)]
    shift = lambda s: [(i, (i + s) % n_ingroup) for i in range(n_ingroup)]

    def spread(column):
        return [column] + [lax.ppermute(column, "ingroup", shift(s)) for s in range(1, n_ingroup)]

    def chunk(blocks, joined=False):
        return chunk_call(blocks, first_expert, weights, tok_rows, capacity, rows, top_count, per_group, joined)

    def across(others):
        return [
            lax.ppermute(others[(s - 1) * tok_rows : s * tok_rows], "ingroup", shift(-s)) for s in range(1, n_ingroup)
        ]

    def group_sum(part, backs):
        group_part = wide(part)
        for back in backs:
            group_part = group_part + wide(back)
        return group_part.astype(jnp.bfloat16)

    def homeward(group_part, k):
        return lax.ppermute(group_part, "group", along(-k))

    tokens, first_expert, half, other_half = tie(tokens, first_expert, half, 1 - half)
    column = pack_call(tokens, upstream, expert_ids, slots, gate_fixed)
    blocks, chunks, backs, sent = {}, {}, {}, {}
    for k in range(n_group):
        ahead = lax.ppermute(column, "group", along(1)) if k < n_group - 1 else None
        pair = spread(column)
        if k > 0:
            chunks[k - 1] = chunk(blocks[k - 1], k - 1 == 1)
        blocks[k], column, chunks, weights = tie(pair, ahead, chunks, weights)

    last = n_group - 1
    for k in range(2, last - 1):
        sent[k] = homeward(group_sum(chunks[k][0], across(chunks[k][1])), k)
    near = lax.ppermute(chunks[1][0], "group", along(-1))
    backs[last - 1] = across(chunks[last - 1][1])
    chunks[last] = chunk(blocks[last])
    chunks, near, backs = tie(chunks, near, backs)

    backs[last] = across(chunks[last][1])
    carried = homeward(group_sum(chunks[last - 1][0], backs[last - 1]), last)
    kept = [[chunks[k][i] for k in range(n_group)] for i in (-3, -2, -1)]
    to_send = weight_call(other_half, *kept)
    to_send, backs[last], carried = tie(to_send, backs[last], carried)

    got = lax.ppermute(to_send, "dp", [(0, 1), (1, 0)])
    sent[last] = homeward(group_sum(chunks[last][0], [*backs[last], carried]), last)
    backs[0] = across((wide(chunks[0][1]) + wide(near[tok_rows:])).astype(jnp.bfloat16))
    grads = weight_call(half, *kept, got)
    grads, sent, backs[0] = tie(grads, sent, backs[0])
    total = wide(chunks[0][0]) + wide(near[:tok_rows])
    for back in backs[0]:
        total = total + wide(back)
    for back in sent.values():
        total = total + wide(back)
    return (total.astype(jnp.bfloat16), *grads)


def solution(mesh):
    rows_spec = P(("parts", "group", "ingroup", "dp"), None)
    weight_spec = P(("group", "ingroup"), None, None)
    out_specs = (
        rows_spec,
        P(("parts", "group", "ingroup"), "dp", None),
        P(("parts", "group", "ingroup"), "dp", None),
        P(("parts", "group", "ingroup"), None, "dp"),
    )
    return jax.shard_map(
        per_device,
        mesh=mesh,
        in_specs=(rows_spec,) * 5 + (weight_spec,) * 3,
        out_specs=out_specs,
        check_vma=False,
    )
```

```python
import functools

import jax
import jax.numpy as jnp
from jax import lax
from jax.experimental import pallas as pl
from jax.experimental.pallas import tpu as pltpu
from jax.sharding import PartitionSpec as P

GROUPS_TOK = 4
ROUTE_ROWS = 16
VMEM_LIMIT = 24 * 1024 * 1024


def dot(a, b, contract):
    return lax.dot_general(a, b, ((contract[:1], contract[1:]), ((), ())), preferred_element_type=jnp.float32)


def in_hbm(v):
    return pltpu.with_memory_space_constraint(v, pltpu.HBM)


def in_vmem(v):
    return pltpu.with_memory_space_constraint(v, pltpu.VMEM)


def gated_parts(pre_gate):
    logistic = jax.nn.sigmoid(pre_gate)
    return (pre_gate * logistic, logistic * (1.0 + pre_gate * (1.0 - logistic)))


def ring_order(size):
    return [0] + list(range(1, size, 2)) + list(range(2, size, 2))[::-1]


def pack_kernel(tokens, upstream, expert_ids, slots, gate_fixed, tokens_out, out, sem):
    top_count, tok_rows = expert_ids.shape
    copies = [
        pltpu.make_async_copy(tokens, tokens_out, sem.at[0]),
        pltpu.make_async_copy(upstream, out.at[pl.ds(0, tok_rows), :], sem.at[1]),
    ]
    for copy in copies:
        copy.start()
    gate = gate_fixed[...]
    out[tok_rows:, :] = jnp.zeros((ROUTE_ROWS, out.shape[1]), jnp.bfloat16)
    for i, field in enumerate((expert_ids[...], slots[...], gate >> 8, gate & 255)):
        empty = jnp.zeros((ROUTE_ROWS - top_count, tok_rows), jnp.float32)
        field = jnp.concatenate([field.astype(jnp.float32), empty], axis=0)
        out[tok_rows:, i * tok_rows : (i + 1) * tok_rows] = field.astype(jnp.bfloat16)
    for copy in copies:
        copy.wait()


def pack_call(tokens, upstream, expert_ids, slots, gate_fixed):
    tok_rows, width = tokens.shape
    vmem, hbm = (pl.BlockSpec(memory_space=m) for m in (pltpu.VMEM, pltpu.HBM))
    operands = [in_hbm(v) for v in (tokens, upstream, expert_ids.T, slots.T, gate_fixed.T)]
    return pl.pallas_call(
        pack_kernel,
        in_specs=[hbm] * 2 + [vmem] * 3,
        out_specs=[vmem] * 2,
        out_shape=[pltpu.VMEM((rows, width), jnp.bfloat16) for rows in (tok_rows, tok_rows + ROUTE_ROWS)],
        scratch_shapes=[pltpu.SemaphoreType.DMA((2,))],
        compiler_params=pltpu.CompilerParams(vmem_limit_bytes=VMEM_LIMIT),
        name="pack",
    )(*operands)


def route_keys(route, first_expert, local_experts, capacity, rows, offset, tok_rows, top_count, per_group):
    field = lambda i: route[:top_count, i * tok_rows : (i + 1) * tok_rows]
    expert = field(0).astype(jnp.int32) - first_expert
    slot = field(1).astype(jnp.int32)
    gate = (field(2) * 256.0 + field(3)) / 65536.0
    valid = (expert >= 0) & (expert < local_experts) & (slot < capacity)
    key = jnp.where(valid, expert * rows + offset + slot, -1)
    gate = jnp.where(valid, gate, 0.0)
    pairs = []
    for i in range(per_group):
        key_out, gate_out = key[i : i + 1, :], gate[i : i + 1, :]
        for j in range(i + per_group, top_count, per_group):
            key_out = jnp.maximum(key_out, key[j : j + 1, :])
            gate_out = jnp.maximum(gate_out, gate[j : j + 1, :])
        pairs.append((key_out, gate_out))
    return pairs


def load_kernel(*refs):
    n = len(refs) // 2
    copies = [pltpu.make_async_copy(refs[i], refs[n + i], refs[-1].at[i]) for i in range(n)]
    for copy in copies:
        copy.start()
    for copy in copies:
        copy.wait()


def load_call(arrays):
    hbm, vmem = (pl.BlockSpec(memory_space=m) for m in (pltpu.HBM, pltpu.VMEM))
    return pl.pallas_call(
        load_kernel,
        in_specs=[hbm] * len(arrays),
        out_specs=[vmem] * len(arrays),
        out_shape=[pltpu.VMEM(v.shape, v.dtype) for v in arrays],
        scratch_shapes=[pltpu.SemaphoreType.DMA((len(arrays),))],
        compiler_params=pltpu.CompilerParams(vmem_limit_bytes=VMEM_LIMIT),
        name="load",
    )(*[in_hbm(v) for v in arrays])


def chunk_kernel(n_blocks, tok_rows, capacity, rows, top_count, per_group, first_ref, *refs):
    tokens, upstream = refs[:n_blocks], refs[n_blocks : 2 * n_blocks]
    w_gate, w_up, w_down = refs[2 * n_blocks : 2 * n_blocks + 3]
    parts = refs[2 * n_blocks + 3 : -4]
    x_rows, s_rows, hids, back_all = refs[-4:]
    experts, width, ff = w_gate.shape

    pairs = []
    for b in range(n_blocks):
        route = upstream[b][tok_rows : tok_rows + ROUTE_ROWS, :].astype(jnp.float32)
        pairs.append(
            route_keys(route, first_ref[0], experts, capacity, rows, b * capacity, tok_rows, top_count, per_group)
        )
    place = lax.broadcasted_iota(jnp.int32, (experts * rows, n_blocks * tok_rows), 0)
    hot = jnp.zeros(place.shape, jnp.float32)
    gate_hot = jnp.zeros(place.shape, jnp.float32)
    for i in range(per_group):
        key = jnp.concatenate([pair[i][0] for pair in pairs], axis=1)
        gate = jnp.concatenate([pair[i][1] for pair in pairs], axis=1)
        match = place == key
        hot = jnp.where(match, 1.0, hot)
        gate_hot = jnp.where(match, gate, gate_hot)
    hot = hot.astype(jnp.bfloat16)
    row_gate = jnp.sum(gate_hot, axis=1, keepdims=True)

    x_all = jnp.concatenate([block[...] for block in tokens], axis=0)
    gathered = dot(hot, x_all, (1, 0)).astype(jnp.bfloat16)
    for e in range(experts):
        x_rows[e] = gathered[e * rows : (e + 1) * rows, :]
    u_all = jnp.concatenate([block[:tok_rows, :] for block in upstream], axis=0)
    scaled = (dot(hot, u_all, (1, 0)) * row_gate).astype(jnp.bfloat16)
    for e in range(experts):
        s_rows[e] = scaled[e * rows : (e + 1) * rows, :]

    for e in range(experts):
        pre_gate = dot(x_rows[e], w_gate[e], (1, 0))
        pre_up = dot(x_rows[e], w_up[e], (1, 0))
        grad_hidden = dot(s_rows[e], w_down[e], (1, 1))
        active, slope = gated_parts(pre_gate)
        grad_gate_pre = (grad_hidden * pre_up * slope).astype(jnp.bfloat16)
        grad_up_pre = (grad_hidden * active).astype(jnp.bfloat16)
        hids[e, :, :ff] = grad_gate_pre
        hids[e, :, ff : 2 * ff] = grad_up_pre
        hids[e, :, 2 * ff :] = (active * pre_up).astype(jnp.bfloat16)
        back = dot(grad_gate_pre, w_gate[e], (1, 1)) + dot(grad_up_pre, w_up[e], (1, 1))
        back_all[e * rows : (e + 1) * rows, :] = back.astype(jnp.bfloat16)

    summed = dot(hot, back_all[...], (0, 0)).astype(jnp.bfloat16)
    start = 0
    for part in parts:
        part[...] = summed[start : start + part.shape[0], :]
        start += part.shape[0]


def chunk_call(tokens, upstream, first_expert, weights, tok_rows, capacity, rows, top_count, per_group, joined):
    n_blocks = len(tokens)
    n_tok = n_blocks * tok_rows
    experts, width, ff = weights[0].shape
    part_shapes = [(n_tok, width)] if joined else [(tok_rows, width), (n_tok - tok_rows, width)]
    kept_shapes = [(experts, rows, width), (experts, rows, width), (experts, rows, 3 * ff)]
    smem, vmem = (pl.BlockSpec(memory_space=m) for m in (pltpu.SMEM, pltpu.VMEM))
    out_shapes = part_shapes + kept_shapes
    return pl.pallas_call(
        functools.partial(chunk_kernel, n_blocks, tok_rows, capacity, rows, top_count, per_group),
        in_specs=[smem] + [vmem] * (2 * n_blocks + 3),
        out_specs=[vmem] * len(out_shapes),
        out_shape=[pltpu.VMEM(shape, jnp.bfloat16) for shape in out_shapes],
        scratch_shapes=[pltpu.VMEM((experts * rows, width), jnp.bfloat16)],
        compiler_params=pltpu.CompilerParams(vmem_limit_bytes=VMEM_LIMIT),
        cost_estimate=pl.CostEstimate(
            flops=2 * experts * rows * width * (5 * ff + 3 * n_tok),
            bytes_accessed=6 * experts * width * ff + 8 * n_tok * width,
            transcendentals=0,
        ),
        name="chunk",
    )(first_expert, *[in_vmem(v) for v in (*tokens, *upstream, *weights)])


def halves_of(n, e, side, refs):
    depth = refs[0].shape[2] // 2
    cols = pl.ds(pl.multiple_of(side * depth, depth), depth)
    cat = lambda parts: jnp.concatenate(parts, axis=0)
    x_rows, s_rows = (cat([ref[e, :, cols] for ref in refs[i * n : (i + 1) * n]]) for i in range(2))
    hid = cat([ref[e] for ref in refs[2 * n : 3 * n]])
    ff = hid.shape[1] // 3
    return dot(x_rows, hid[:, : 2 * ff], (0, 0)), dot(hid[:, 2 * ff :], s_rows, (0, 0))


def send_kernel(n, side_ref, *refs):
    out = refs[3 * n]
    for e in range(out.shape[0]):
        gate_up, down = halves_of(n, e, side_ref[0], refs)
        depth = gate_up.shape[0]
        out[e, :depth, :] = gate_up.astype(jnp.bfloat16)
        out[e, depth:, :] = down.astype(jnp.bfloat16)


def keep_kernel(n, side_ref, *refs):
    got, outs = refs[3 * n], refs[3 * n + 1 : 3 * n + 4]
    buffers, sem = refs[3 * n + 4 : 3 * n + 7], refs[3 * n + 7]
    copies = []
    for e in range(got.shape[0]):
        gate_up, down = halves_of(n, e, side_ref[0], refs)
        depth = gate_up.shape[0]
        ff = down.shape[0]
        gate_up = gate_up + got[e, :depth, :].astype(jnp.float32)
        buffers[0][e] = gate_up[:, :ff].astype(jnp.bfloat16)
        buffers[1][e] = gate_up[:, ff:].astype(jnp.bfloat16)
        buffers[2][e] = (down + got[e, depth:, :].astype(jnp.float32)).astype(jnp.bfloat16)
        for i in range(3):
            copy = pltpu.make_async_copy(buffers[i].at[e], outs[i].at[e], sem.at[e, i])
            copy.start()
            copies.append(copy)
    for copy in copies:
        copy.wait()


def weight_call(side, x_rows, s_rows, hids, got=None):
    n = len(x_rows)
    experts, rows, width = x_rows[0].shape
    ff = hids[0].shape[2] // 3
    depth = width // 2
    smem, vmem = (pl.BlockSpec(memory_space=m) for m in (pltpu.SMEM, pltpu.VMEM))
    operands = [*x_rows, *s_rows, *hids]
    scratch = []
    if got is None:
        kernel, out_specs = send_kernel, vmem
        out_shape = pltpu.VMEM((experts, depth + ff, depth), jnp.bfloat16)
    else:
        kernel = keep_kernel
        operands = operands + [got]
        shapes = [(experts, depth, ff), (experts, depth, ff), (experts, ff, depth)]
        out_specs = [pl.BlockSpec(memory_space=pl.ANY)] * 3
        out_shape = [jax.ShapeDtypeStruct(s, jnp.bfloat16) for s in shapes]
        scratch = [pltpu.VMEM(s, jnp.bfloat16) for s in shapes] + [pltpu.SemaphoreType.DMA((experts, 3))]
    return pl.pallas_call(
        functools.partial(kernel, n),
        in_specs=[smem] + [vmem] * len(operands),
        out_specs=out_specs,
        out_shape=out_shape,
        scratch_shapes=scratch,
        compiler_params=pltpu.CompilerParams(vmem_limit_bytes=VMEM_LIMIT),
        cost_estimate=pl.CostEstimate(
            flops=2 * experts * n * rows * 3 * ff * depth,
            bytes_accessed=2 * experts * (n * rows * (width + 3 * ff) + 3 * ff * depth),
            transcendentals=0,
        ),
        name="weight_grads",
    )(side, *[in_vmem(v) for v in operands])


def per_device(tokens, upstream, expert_ids, gate_fixed, slots, w_gate, w_up, w_down):
    local_experts = w_gate.shape[0]
    n_group = lax.axis_size("group")
    n_ingroup = lax.axis_size("ingroup")
    experts_all = local_experts * n_group * n_ingroup
    tok_rows, top_count = expert_ids.shape
    width = tokens.shape[1]
    per_group = top_count // GROUPS_TOK
    capacity = max(2, 3 * tok_rows * top_count // (2 * experts_all))
    rows = -(-n_ingroup * capacity // 16) * 16
    z, x, core = (lax.axis_index(a) for a in ("group", "ingroup", "dp"))
    first_expert = ((z * n_ingroup + x) * local_experts).astype(jnp.int32).reshape(1)
    half = core.astype(jnp.int32).reshape(1)
    weights = load_call((w_gate, w_up, w_down))
    wide = lambda v: v.astype(jnp.float32)
    tie = lambda *trees: lax.optimization_barrier(trees)
    order = ring_order(n_group)
    along = lambda k: [(order[i], order[(i + k) % n_group]) for i in range(n_group)]
    shift = lambda s: [(i, (i + s) % n_ingroup) for i in range(n_ingroup)]

    def spread(column):
        return [column] + [lax.ppermute(column, "ingroup", shift(s)) for s in range(1, n_ingroup)]

    def chunk(blocks, joined=False):
        return chunk_call(*blocks, first_expert, weights, tok_rows, capacity, rows, top_count, per_group, joined)

    def across(others):
        return [
            lax.ppermute(others[(s - 1) * tok_rows : s * tok_rows], "ingroup", shift(-s)) for s in range(1, n_ingroup)
        ]

    def group_sum(part, backs):
        group_part = wide(part)
        for back in backs:
            group_part = group_part + wide(back)
        return group_part.astype(jnp.bfloat16)

    def homeward(group_part, k):
        return lax.ppermute(group_part, "group", along(-k))

    tokens, first_expert, half, other_half = tie(tokens, first_expert, half, 1 - half)
    first_tokens, upstream = pack_call(tokens, upstream, expert_ids, slots, gate_fixed)
    blocks, chunks, backs, sent, near = {}, {}, {}, {}, None
    last = n_group - 1
    for k in range(n_group):
        pair = [spread(tokens), spread(upstream)]
        if k == 0:
            pair[0][0] = first_tokens
        if k < last:
            tokens, upstream = (lax.ppermute(v, "group", along(1)) for v in (tokens, upstream))
        if k > 0:
            chunks[k - 1] = chunk(blocks[k - 1], k - 1 == 1)
        if k == last:
            near = lax.ppermute(chunks[1][0], "group", along(-1))
        tokens, pair[0], chunks, weights = tie(tokens, pair[0], chunks, weights)
        upstream, pair[1] = tie(upstream, pair[1])
        blocks[k] = pair

    for k in range(2, last - 1):
        sent[k] = homeward(group_sum(chunks[k][0], across(chunks[k][1])), k)
    blocks[last], chunks, near = tie(blocks[last], chunks, near)
    backs[last - 1] = across(chunks[last - 1][1])
    chunks[last] = chunk(blocks[last])
    chunks, backs = tie(chunks, backs)

    backs[last] = across(chunks[last][1])
    carried = homeward(group_sum(chunks[last - 1][0], backs[last - 1]), last)
    kept = [[chunks[k][i] for k in range(n_group)] for i in (-3, -2, -1)]
    to_send = weight_call(other_half, *kept)
    to_send, backs[last], carried = tie(to_send, backs[last], carried)

    got = lax.ppermute(to_send, "dp", [(0, 1), (1, 0)])
    sent[last] = homeward(group_sum(chunks[last][0], [*backs[last], carried]), last)
    backs[0] = across((wide(chunks[0][1]) + wide(near[tok_rows:])).astype(jnp.bfloat16))
    grads = weight_call(half, *kept, got)
    grads, sent, backs[0] = tie(grads, sent, backs[0])
    total = wide(chunks[0][0]) + wide(near[:tok_rows])
    for back in backs[0]:
        total = total + wide(back)
    for back in sent.values():
        total = total + wide(back)
    return (total.astype(jnp.bfloat16), *grads)


def solution(mesh):
    rows_spec = P(("parts", "group", "ingroup", "dp"), None)
    weight_spec = P(("group", "ingroup"), None, None)
    out_specs = (
        rows_spec,
        P(("parts", "group", "ingroup"), "dp", None),
        P(("parts", "group", "ingroup"), "dp", None),
        P(("parts", "group", "ingroup"), None, "dp"),
    )
    return jax.shard_map(
        per_device,
        mesh=mesh,
        in_specs=(rows_spec,) * 5 + (weight_spec,) * 3,
        out_specs=out_specs,
        check_vma=False,
    )
```

```python
import functools

import jax
import jax.numpy as jnp
from jax import lax
from jax.experimental import pallas as pl
from jax.experimental.pallas import tpu as pltpu
from jax.sharding import PartitionSpec as P

GROUPS_TOK = 4
ROUTE_ROWS = 16
VMEM_LIMIT = 24 * 1024 * 1024


def dot(a, b, contract):
    return lax.dot_general(a, b, ((contract[:1], contract[1:]), ((), ())), preferred_element_type=jnp.float32)


def in_hbm(v):
    return pltpu.with_memory_space_constraint(v, pltpu.HBM)


def in_vmem(v):
    return pltpu.with_memory_space_constraint(v, pltpu.VMEM)


def gated_parts(pre_gate):
    logistic = jax.nn.sigmoid(pre_gate)
    return (pre_gate * logistic, logistic * (1.0 + pre_gate * (1.0 - logistic)))


def ring_order(size):
    return [0] + list(range(1, size, 2)) + list(range(2, size, 2))[::-1]


def pack_kernel(tokens, upstream, expert_ids, slots, gate_fixed, tokens_out, out, sem):
    top_count, tok_rows = expert_ids.shape
    copies = [
        pltpu.make_async_copy(tokens, tokens_out, sem.at[0]),
        pltpu.make_async_copy(upstream, out.at[pl.ds(0, tok_rows), :], sem.at[1]),
    ]
    for copy in copies:
        copy.start()
    gate = gate_fixed[...]
    out[tok_rows:, :] = jnp.zeros((ROUTE_ROWS, out.shape[1]), jnp.bfloat16)
    for i, field in enumerate((expert_ids[...], slots[...], gate >> 8, gate & 255)):
        empty = jnp.zeros((ROUTE_ROWS - top_count, tok_rows), jnp.float32)
        field = jnp.concatenate([field.astype(jnp.float32), empty], axis=0)
        out[tok_rows:, i * tok_rows : (i + 1) * tok_rows] = field.astype(jnp.bfloat16)
    for copy in copies:
        copy.wait()


def pack_call(tokens, upstream, expert_ids, slots, gate_fixed):
    tok_rows, width = tokens.shape
    vmem, hbm = (pl.BlockSpec(memory_space=m) for m in (pltpu.VMEM, pltpu.HBM))
    operands = [in_hbm(v) for v in (tokens, upstream, expert_ids.T, slots.T, gate_fixed.T)]
    return pl.pallas_call(
        pack_kernel,
        in_specs=[hbm] * 2 + [vmem] * 3,
        out_specs=[vmem] * 2,
        out_shape=[pltpu.VMEM((rows, width), jnp.bfloat16) for rows in (tok_rows, tok_rows + ROUTE_ROWS)],
        scratch_shapes=[pltpu.SemaphoreType.DMA((2,))],
        compiler_params=pltpu.CompilerParams(vmem_limit_bytes=VMEM_LIMIT),
        name="pack",
    )(*operands)


def route_keys(route, first_expert, local_experts, capacity, rows, offset, tok_rows, top_count, per_group):
    field = lambda i: route[:top_count, i * tok_rows : (i + 1) * tok_rows]
    expert = field(0).astype(jnp.int32) - first_expert
    slot = field(1).astype(jnp.int32)
    gate = (field(2) * 256.0 + field(3)) / 65536.0
    valid = (expert >= 0) & (expert < local_experts) & (slot < capacity)
    key = jnp.where(valid, expert * rows + offset + slot, -1)
    gate = jnp.where(valid, gate, 0.0)
    pairs = []
    for i in range(per_group):
        key_out, gate_out = key[i : i + 1, :], gate[i : i + 1, :]
        for j in range(i + per_group, top_count, per_group):
            key_out = jnp.maximum(key_out, key[j : j + 1, :])
            gate_out = jnp.maximum(gate_out, gate[j : j + 1, :])
        pairs.append((key_out, gate_out))
    return pairs


def load_kernel(*refs):
    n = len(refs) // 2
    copies = [pltpu.make_async_copy(refs[i], refs[n + i], refs[-1].at[i]) for i in range(n)]
    for copy in copies:
        copy.start()
    for copy in copies:
        copy.wait()


def load_call(arrays):
    hbm, vmem = (pl.BlockSpec(memory_space=m) for m in (pltpu.HBM, pltpu.VMEM))
    return pl.pallas_call(
        load_kernel,
        in_specs=[hbm] * len(arrays),
        out_specs=[vmem] * len(arrays),
        out_shape=[pltpu.VMEM(v.shape, v.dtype) for v in arrays],
        scratch_shapes=[pltpu.SemaphoreType.DMA((len(arrays),))],
        compiler_params=pltpu.CompilerParams(vmem_limit_bytes=VMEM_LIMIT),
        name="load",
    )(*[in_hbm(v) for v in arrays])


def chunk_kernel(n_blocks, tok_rows, capacity, rows, top_count, per_group, first_ref, *refs):
    tokens, upstream = refs[:n_blocks], refs[n_blocks : 2 * n_blocks]
    w_gate, w_up, w_down = refs[2 * n_blocks : 2 * n_blocks + 3]
    parts = refs[2 * n_blocks + 3 : -4]
    x_rows, s_rows, hids, back_all = refs[-4:]
    experts, width, ff = w_gate.shape

    pairs = []
    for b in range(n_blocks):
        route = upstream[b][tok_rows : tok_rows + ROUTE_ROWS, :].astype(jnp.float32)
        pairs.append(
            route_keys(route, first_ref[0], experts, capacity, rows, b * capacity, tok_rows, top_count, per_group)
        )
    place = lax.broadcasted_iota(jnp.int32, (experts * rows, n_blocks * tok_rows), 0)
    hot = jnp.zeros(place.shape, jnp.float32)
    gate_hot = jnp.zeros(place.shape, jnp.float32)
    for i in range(per_group):
        key = jnp.concatenate([pair[i][0] for pair in pairs], axis=1)
        gate = jnp.concatenate([pair[i][1] for pair in pairs], axis=1)
        match = place == key
        hot = jnp.where(match, 1.0, hot)
        gate_hot = jnp.where(match, gate, gate_hot)
    hot = hot.astype(jnp.bfloat16)
    row_gate = jnp.sum(gate_hot, axis=1, keepdims=True)

    x_all = jnp.concatenate([block[...] for block in tokens], axis=0)
    gathered = dot(hot, x_all, (1, 0)).astype(jnp.bfloat16)
    for e in range(experts):
        x_rows[e] = gathered[e * rows : (e + 1) * rows, :]
    u_all = jnp.concatenate([block[:tok_rows, :] for block in upstream], axis=0)
    scaled = (dot(hot, u_all, (1, 0)) * row_gate).astype(jnp.bfloat16)
    for e in range(experts):
        s_rows[e] = scaled[e * rows : (e + 1) * rows, :]

    for e in range(experts):
        pre_gate = dot(x_rows[e], w_gate[e], (1, 0))
        pre_up = dot(x_rows[e], w_up[e], (1, 0))
        grad_hidden = dot(s_rows[e], w_down[e], (1, 1))
        active, slope = gated_parts(pre_gate)
        grad_gate_pre = (grad_hidden * pre_up * slope).astype(jnp.bfloat16)
        grad_up_pre = (grad_hidden * active).astype(jnp.bfloat16)
        hids[e, :, :ff] = grad_gate_pre
        hids[e, :, ff : 2 * ff] = grad_up_pre
        hids[e, :, 2 * ff :] = (active * pre_up).astype(jnp.bfloat16)
        back = dot(grad_gate_pre, w_gate[e], (1, 1)) + dot(grad_up_pre, w_up[e], (1, 1))
        back_all[e * rows : (e + 1) * rows, :] = back.astype(jnp.bfloat16)

    summed = dot(hot, back_all[...], (0, 0)).astype(jnp.bfloat16)
    start = 0
    for part in parts:
        part[...] = summed[start : start + part.shape[0], :]
        start += part.shape[0]


def chunk_call(tokens, upstream, first_expert, weights, tok_rows, capacity, rows, top_count, per_group, joined):
    n_blocks = len(tokens)
    n_tok = n_blocks * tok_rows
    experts, width, ff = weights[0].shape
    part_shapes = [(n_tok, width)] if joined else [(tok_rows, width), (n_tok - tok_rows, width)]
    kept_shapes = [(experts, rows, width), (experts, rows, width), (experts, rows, 3 * ff)]
    smem, vmem = (pl.BlockSpec(memory_space=m) for m in (pltpu.SMEM, pltpu.VMEM))
    out_shapes = part_shapes + kept_shapes
    return pl.pallas_call(
        functools.partial(chunk_kernel, n_blocks, tok_rows, capacity, rows, top_count, per_group),
        in_specs=[smem] + [vmem] * (2 * n_blocks + 3),
        out_specs=[vmem] * len(out_shapes),
        out_shape=[pltpu.VMEM(shape, jnp.bfloat16) for shape in out_shapes],
        scratch_shapes=[pltpu.VMEM((experts * rows, width), jnp.bfloat16)],
        compiler_params=pltpu.CompilerParams(vmem_limit_bytes=VMEM_LIMIT),
        cost_estimate=pl.CostEstimate(
            flops=2 * experts * rows * width * (5 * ff + 3 * n_tok),
            bytes_accessed=6 * experts * width * ff + 8 * n_tok * width,
            transcendentals=0,
        ),
        name="chunk",
    )(first_expert, *[in_vmem(v) for v in (*tokens, *upstream, *weights)])


def halves_of(n, e, side, refs):
    depth = refs[0].shape[2] // 2
    cols = pl.ds(pl.multiple_of(side * depth, depth), depth)
    cat = lambda parts: jnp.concatenate(parts, axis=0)
    x_rows, s_rows = (cat([ref[e, :, cols] for ref in refs[i * n : (i + 1) * n]]) for i in range(2))
    hid = cat([ref[e] for ref in refs[2 * n : 3 * n]])
    ff = hid.shape[1] // 3
    return dot(x_rows, hid[:, : 2 * ff], (0, 0)), dot(hid[:, 2 * ff :], s_rows, (0, 0))


def send_kernel(n, side_ref, *refs):
    out = refs[3 * n]
    for e in range(out.shape[0]):
        gate_up, down = halves_of(n, e, side_ref[0], refs)
        depth = gate_up.shape[0]
        out[e, :depth, :] = gate_up.astype(jnp.bfloat16)
        out[e, depth:, :] = down.astype(jnp.bfloat16)


def keep_kernel(n, side_ref, *refs):
    got, outs = refs[3 * n], refs[3 * n + 1 : 3 * n + 4]
    buffers, sem = refs[3 * n + 4 : 3 * n + 7], refs[3 * n + 7]
    copies = []
    for e in range(got.shape[0]):
        gate_up, down = halves_of(n, e, side_ref[0], refs)
        depth = gate_up.shape[0]
        ff = down.shape[0]
        gate_up = gate_up + got[e, :depth, :].astype(jnp.float32)
        buffers[0][e] = gate_up[:, :ff].astype(jnp.bfloat16)
        buffers[1][e] = gate_up[:, ff:].astype(jnp.bfloat16)
        buffers[2][e] = (down + got[e, depth:, :].astype(jnp.float32)).astype(jnp.bfloat16)
        for i in range(3):
            copy = pltpu.make_async_copy(buffers[i].at[e], outs[i].at[e], sem.at[e, i])
            copy.start()
            copies.append(copy)
    for copy in copies:
        copy.wait()


def weight_call(side, x_rows, s_rows, hids, got=None):
    n = len(x_rows)
    experts, rows, width = x_rows[0].shape
    ff = hids[0].shape[2] // 3
    depth = width // 2
    smem, vmem = (pl.BlockSpec(memory_space=m) for m in (pltpu.SMEM, pltpu.VMEM))
    operands = [*x_rows, *s_rows, *hids]
    scratch = []
    if got is None:
        kernel, out_specs = send_kernel, vmem
        out_shape = pltpu.VMEM((experts, depth + ff, depth), jnp.bfloat16)
    else:
        kernel = keep_kernel
        operands = operands + [got]
        shapes = [(experts, depth, ff), (experts, depth, ff), (experts, ff, depth)]
        out_specs = [pl.BlockSpec(memory_space=pl.ANY)] * 3
        out_shape = [jax.ShapeDtypeStruct(s, jnp.bfloat16) for s in shapes]
        scratch = [pltpu.VMEM(s, jnp.bfloat16) for s in shapes] + [pltpu.SemaphoreType.DMA((experts, 3))]
    return pl.pallas_call(
        functools.partial(kernel, n),
        in_specs=[smem] + [vmem] * len(operands),
        out_specs=out_specs,
        out_shape=out_shape,
        scratch_shapes=scratch,
        compiler_params=pltpu.CompilerParams(vmem_limit_bytes=VMEM_LIMIT),
        cost_estimate=pl.CostEstimate(
            flops=2 * experts * n * rows * 3 * ff * depth,
            bytes_accessed=2 * experts * (n * rows * (width + 3 * ff) + 3 * ff * depth),
            transcendentals=0,
        ),
        name="weight_grads",
    )(side, *[in_vmem(v) for v in operands])


def per_device(tokens, upstream, expert_ids, gate_fixed, slots, w_gate, w_up, w_down):
    local_experts = w_gate.shape[0]
    n_group = lax.axis_size("group")
    n_ingroup = lax.axis_size("ingroup")
    experts_all = local_experts * n_group * n_ingroup
    tok_rows, top_count = expert_ids.shape
    width = tokens.shape[1]
    per_group = top_count // GROUPS_TOK
    capacity = max(2, 3 * tok_rows * top_count // (2 * experts_all))
    rows = -(-n_ingroup * capacity // 16) * 16
    z, x, core = (lax.axis_index(a) for a in ("group", "ingroup", "dp"))
    first_expert = ((z * n_ingroup + x) * local_experts).astype(jnp.int32).reshape(1)
    half = core.astype(jnp.int32).reshape(1)
    weights = load_call((w_gate, w_up, w_down))
    wide = lambda v: v.astype(jnp.float32)
    tie = lambda *trees: lax.optimization_barrier(trees)
    order = ring_order(n_group)
    along = lambda k: [(order[i], order[(i + k) % n_group]) for i in range(n_group)]
    shift = lambda s: [(i, (i + s) % n_ingroup) for i in range(n_ingroup)]

    def spread(column):
        return [column] + [lax.ppermute(column, "ingroup", shift(s)) for s in range(1, n_ingroup)]

    def chunk(blocks, joined=False):
        return chunk_call(*blocks, first_expert, weights, tok_rows, capacity, rows, top_count, per_group, joined)

    def across(others):
        return [
            lax.ppermute(others[(s - 1) * tok_rows : s * tok_rows], "ingroup", shift(-s)) for s in range(1, n_ingroup)
        ]

    def group_sum(part, backs):
        group_part = wide(part)
        for back in backs:
            group_part = group_part + wide(back)
        return group_part.astype(jnp.bfloat16)

    def homeward(group_part, k):
        return lax.ppermute(group_part, "group", along(-k))

    tokens, first_expert, half, other_half = tie(tokens, first_expert, half, 1 - half)
    first_tokens, upstream = pack_call(tokens, upstream, expert_ids, slots, gate_fixed)
    blocks, chunks, backs, sent = {}, {}, {}, {}
    last = n_group - 1
    for k in range(n_group):
        pair = [spread(tokens), spread(upstream)]
        if k == 0:
            pair[0][0] = first_tokens
        if k < last:
            tokens, upstream = (lax.ppermute(v, "group", along(1)) for v in (tokens, upstream))
        if k > 0:
            chunks[k - 1] = chunk(blocks[k - 1], k - 1 == 1)
        tokens, pair[0], chunks, weights = tie(tokens, pair[0], chunks, weights)
        upstream, pair[1] = tie(upstream, pair[1])
        blocks[k] = pair

    for k in range(2, last - 1):
        sent[k] = homeward(group_sum(chunks[k][0], across(chunks[k][1])), k)
    near = lax.ppermute(chunks[1][0], "group", along(-1))
    blocks[last], chunks = tie(blocks[last], chunks)
    backs[last - 1] = across(chunks[last - 1][1])
    chunks[last] = chunk(blocks[last])
    chunks, backs, near = tie(chunks, backs, near)

    backs[last] = across(chunks[last][1])
    carried = homeward(group_sum(chunks[last - 1][0], backs[last - 1]), last)
    kept = [[chunks[k][i] for k in range(n_group)] for i in (-3, -2, -1)]
    to_send = weight_call(other_half, *kept)
    to_send, backs[last], carried = tie(to_send, backs[last], carried)

    got = lax.ppermute(to_send, "dp", [(0, 1), (1, 0)])
    sent[last] = homeward(group_sum(chunks[last][0], [*backs[last], carried]), last)
    backs[0] = across((wide(chunks[0][1]) + wide(near[tok_rows:])).astype(jnp.bfloat16))
    grads = weight_call(half, *kept, got)
    grads, sent, backs[0] = tie(grads, sent, backs[0])
    total = wide(chunks[0][0]) + wide(near[:tok_rows])
    for back in backs[0]:
        total = total + wide(back)
    for back in sent.values():
        total = total + wide(back)
    return (total.astype(jnp.bfloat16), *grads)


def solution(mesh):
    rows_spec = P(("parts", "group", "ingroup", "dp"), None)
    weight_spec = P(("group", "ingroup"), None, None)
    out_specs = (
        rows_spec,
        P(("parts", "group", "ingroup"), "dp", None),
        P(("parts", "group", "ingroup"), "dp", None),
        P(("parts", "group", "ingroup"), None, "dp"),
    )
    return jax.shard_map(
        per_device,
        mesh=mesh,
        in_specs=(rows_spec,) * 5 + (weight_spec,) * 3,
        out_specs=out_specs,
        check_vma=False,
    )
```

```python
import functools

import jax
import jax.numpy as jnp
from jax import lax
from jax.experimental import pallas as pl
from jax.experimental.pallas import tpu as pltpu
from jax.sharding import PartitionSpec as P

GROUPS_TOK = 4
ROUTE_ROWS = 16
VMEM_LIMIT = 24 * 1024 * 1024


def dot(a, b, contract):
    return lax.dot_general(a, b, ((contract[:1], contract[1:]), ((), ())), preferred_element_type=jnp.float32)


def in_hbm(v):
    return pltpu.with_memory_space_constraint(v, pltpu.HBM)


def in_vmem(v):
    return pltpu.with_memory_space_constraint(v, pltpu.VMEM)


def gated_parts(pre_gate):
    logistic = jax.nn.sigmoid(pre_gate)
    return (pre_gate * logistic, logistic * (1.0 + pre_gate * (1.0 - logistic)))


def ring_order(size):
    return [0] + list(range(1, size, 2)) + list(range(2, size, 2))[::-1]


def pack_kernel(tokens, upstream, expert_ids, slots, gate_fixed, tokens_out, out, sem):
    top_count, tok_rows = expert_ids.shape
    copies = [
        pltpu.make_async_copy(tokens, tokens_out, sem.at[0]),
        pltpu.make_async_copy(upstream, out.at[pl.ds(0, tok_rows), :], sem.at[1]),
    ]
    for copy in copies:
        copy.start()
    gate = gate_fixed[...]
    out[tok_rows:, :] = jnp.zeros((ROUTE_ROWS, out.shape[1]), jnp.bfloat16)
    for i, field in enumerate((expert_ids[...], slots[...], gate >> 8, gate & 255)):
        empty = jnp.zeros((ROUTE_ROWS - top_count, tok_rows), jnp.float32)
        field = jnp.concatenate([field.astype(jnp.float32), empty], axis=0)
        out[tok_rows:, i * tok_rows : (i + 1) * tok_rows] = field.astype(jnp.bfloat16)
    for copy in copies:
        copy.wait()


def pack_call(tokens, upstream, expert_ids, slots, gate_fixed):
    tok_rows, width = tokens.shape
    vmem, hbm = (pl.BlockSpec(memory_space=m) for m in (pltpu.VMEM, pltpu.HBM))
    operands = [in_hbm(v) for v in (tokens, upstream, expert_ids.T, slots.T, gate_fixed.T)]
    return pl.pallas_call(
        pack_kernel,
        in_specs=[hbm] * 2 + [vmem] * 3,
        out_specs=[vmem] * 2,
        out_shape=[pltpu.VMEM((rows, width), jnp.bfloat16) for rows in (tok_rows, tok_rows + ROUTE_ROWS)],
        scratch_shapes=[pltpu.SemaphoreType.DMA((2,))],
        compiler_params=pltpu.CompilerParams(vmem_limit_bytes=VMEM_LIMIT),
        name="pack",
    )(*operands)


def route_keys(route, first_expert, local_experts, capacity, rows, offset, tok_rows, top_count, per_group):
    field = lambda i: route[:top_count, i * tok_rows : (i + 1) * tok_rows]
    expert = field(0).astype(jnp.int32) - first_expert
    slot = field(1).astype(jnp.int32)
    gate = (field(2) * 256.0 + field(3)) / 65536.0
    valid = (expert >= 0) & (expert < local_experts) & (slot < capacity)
    key = jnp.where(valid, expert * rows + offset + slot, -1)
    gate = jnp.where(valid, gate, 0.0)
    pairs = []
    for i in range(per_group):
        key_out, gate_out = key[i : i + 1, :], gate[i : i + 1, :]
        for j in range(i + per_group, top_count, per_group):
            key_out = jnp.maximum(key_out, key[j : j + 1, :])
            gate_out = jnp.maximum(gate_out, gate[j : j + 1, :])
        pairs.append((key_out, gate_out))
    return pairs


def load_kernel(*refs):
    n = len(refs) // 2
    copies = [pltpu.make_async_copy(refs[i], refs[n + i], refs[-1].at[i]) for i in range(n)]
    for copy in copies:
        copy.start()
    for copy in copies:
        copy.wait()


def load_call(arrays):
    hbm, vmem = (pl.BlockSpec(memory_space=m) for m in (pltpu.HBM, pltpu.VMEM))
    return pl.pallas_call(
        load_kernel,
        in_specs=[hbm] * len(arrays),
        out_specs=[vmem] * len(arrays),
        out_shape=[pltpu.VMEM(v.shape, v.dtype) for v in arrays],
        scratch_shapes=[pltpu.SemaphoreType.DMA((len(arrays),))],
        compiler_params=pltpu.CompilerParams(vmem_limit_bytes=VMEM_LIMIT),
        name="load",
    )(*[in_hbm(v) for v in arrays])


def chunk_kernel(n_blocks, tok_rows, capacity, rows, top_count, per_group, first_ref, *refs):
    tokens, upstream = refs[:n_blocks], refs[n_blocks : 2 * n_blocks]
    w_gate, w_up, w_down = refs[2 * n_blocks : 2 * n_blocks + 3]
    parts = refs[2 * n_blocks + 3 : -4]
    x_rows, s_rows, hids, back_all = refs[-4:]
    experts, width, ff = w_gate.shape

    pairs = []
    for b in range(n_blocks):
        route = upstream[b][tok_rows : tok_rows + ROUTE_ROWS, :].astype(jnp.float32)
        pairs.append(
            route_keys(route, first_ref[0], experts, capacity, rows, b * capacity, tok_rows, top_count, per_group)
        )
    place = lax.broadcasted_iota(jnp.int32, (experts * rows, n_blocks * tok_rows), 0)
    hot = jnp.zeros(place.shape, jnp.float32)
    gate_hot = jnp.zeros(place.shape, jnp.float32)
    for i in range(per_group):
        key = jnp.concatenate([pair[i][0] for pair in pairs], axis=1)
        gate = jnp.concatenate([pair[i][1] for pair in pairs], axis=1)
        match = place == key
        hot = jnp.where(match, 1.0, hot)
        gate_hot = jnp.where(match, gate, gate_hot)
    hot = hot.astype(jnp.bfloat16)
    row_gate = jnp.sum(gate_hot, axis=1, keepdims=True)

    x_all = jnp.concatenate([block[...] for block in tokens], axis=0)
    gathered = dot(hot, x_all, (1, 0)).astype(jnp.bfloat16)
    for e in range(experts):
        x_rows[e] = gathered[e * rows : (e + 1) * rows, :]
    u_all = jnp.concatenate([block[:tok_rows, :] for block in upstream], axis=0)
    scaled = (dot(hot, u_all, (1, 0)) * row_gate).astype(jnp.bfloat16)
    for e in range(experts):
        s_rows[e] = scaled[e * rows : (e + 1) * rows, :]

    for e in range(experts):
        pre_gate = dot(x_rows[e], w_gate[e], (1, 0))
        pre_up = dot(x_rows[e], w_up[e], (1, 0))
        grad_hidden = dot(s_rows[e], w_down[e], (1, 1))
        active, slope = gated_parts(pre_gate)
        grad_gate_pre = (grad_hidden * pre_up * slope).astype(jnp.bfloat16)
        grad_up_pre = (grad_hidden * active).astype(jnp.bfloat16)
        hids[e, :, :ff] = grad_gate_pre
        hids[e, :, ff : 2 * ff] = grad_up_pre
        hids[e, :, 2 * ff :] = (active * pre_up).astype(jnp.bfloat16)
        back = dot(grad_gate_pre, w_gate[e], (1, 1)) + dot(grad_up_pre, w_up[e], (1, 1))
        back_all[e * rows : (e + 1) * rows, :] = back.astype(jnp.bfloat16)

    summed = dot(hot, back_all[...], (0, 0)).astype(jnp.bfloat16)
    start = 0
    for part in parts:
        part[...] = summed[start : start + part.shape[0], :]
        start += part.shape[0]


def chunk_call(tokens, upstream, first_expert, weights, tok_rows, capacity, rows, top_count, per_group):
    n_blocks = len(tokens)
    n_tok = n_blocks * tok_rows
    experts, width, ff = weights[0].shape
    part_shapes = [(tok_rows, width), (n_tok - tok_rows, width)]
    kept_shapes = [(experts, rows, width), (experts, rows, width), (experts, rows, 3 * ff)]
    smem, vmem = (pl.BlockSpec(memory_space=m) for m in (pltpu.SMEM, pltpu.VMEM))
    out_shapes = part_shapes + kept_shapes
    return pl.pallas_call(
        functools.partial(chunk_kernel, n_blocks, tok_rows, capacity, rows, top_count, per_group),
        in_specs=[smem] + [vmem] * (2 * n_blocks + 3),
        out_specs=[vmem] * len(out_shapes),
        out_shape=[pltpu.VMEM(shape, jnp.bfloat16) for shape in out_shapes],
        scratch_shapes=[pltpu.VMEM((experts * rows, width), jnp.bfloat16)],
        compiler_params=pltpu.CompilerParams(vmem_limit_bytes=VMEM_LIMIT),
        cost_estimate=pl.CostEstimate(
            flops=2 * experts * rows * width * (5 * ff + 3 * n_tok),
            bytes_accessed=6 * experts * width * ff + 8 * n_tok * width,
            transcendentals=0,
        ),
        name="chunk",
    )(first_expert, *[in_vmem(v) for v in (*tokens, *upstream, *weights)])


def halves_of(n, e, side, refs):
    depth = refs[0].shape[2] // 2
    cols = pl.ds(pl.multiple_of(side * depth, depth), depth)
    cat = lambda parts: jnp.concatenate(parts, axis=0)
    x_rows, s_rows = (cat([ref[e, :, cols] for ref in refs[i * n : (i + 1) * n]]) for i in range(2))
    hid = cat([ref[e] for ref in refs[2 * n : 3 * n]])
    ff = hid.shape[1] // 3
    return dot(x_rows, hid[:, : 2 * ff], (0, 0)), dot(hid[:, 2 * ff :], s_rows, (0, 0))


def send_kernel(n, side_ref, *refs):
    out = refs[3 * n]
    for e in range(out.shape[0]):
        gate_up, down = halves_of(n, e, side_ref[0], refs)
        depth = gate_up.shape[0]
        out[e, :depth, :] = gate_up.astype(jnp.bfloat16)
        out[e, depth:, :] = down.astype(jnp.bfloat16)


def keep_kernel(n, side_ref, *refs):
    got, outs = refs[3 * n], refs[3 * n + 1 : 3 * n + 4]
    buffers, sem = refs[3 * n + 4 : 3 * n + 7], refs[3 * n + 7]
    copies = []
    for e in range(got.shape[0]):
        gate_up, down = halves_of(n, e, side_ref[0], refs)
        depth = gate_up.shape[0]
        ff = down.shape[0]
        gate_up = gate_up + got[e, :depth, :].astype(jnp.float32)
        buffers[0][e] = gate_up[:, :ff].astype(jnp.bfloat16)
        buffers[1][e] = gate_up[:, ff:].astype(jnp.bfloat16)
        buffers[2][e] = (down + got[e, depth:, :].astype(jnp.float32)).astype(jnp.bfloat16)
        for i in range(3):
            copy = pltpu.make_async_copy(buffers[i].at[e], outs[i].at[e], sem.at[e, i])
            copy.start()
            copies.append(copy)
    for copy in copies:
        copy.wait()


def weight_call(side, x_rows, s_rows, hids, got=None):
    n = len(x_rows)
    experts, rows, width = x_rows[0].shape
    ff = hids[0].shape[2] // 3
    depth = width // 2
    smem, vmem = (pl.BlockSpec(memory_space=m) for m in (pltpu.SMEM, pltpu.VMEM))
    operands = [*x_rows, *s_rows, *hids]
    scratch = []
    if got is None:
        kernel, out_specs = send_kernel, vmem
        out_shape = pltpu.VMEM((experts, depth + ff, depth), jnp.bfloat16)
    else:
        kernel = keep_kernel
        operands = operands + [got]
        shapes = [(experts, depth, ff), (experts, depth, ff), (experts, ff, depth)]
        out_specs = [pl.BlockSpec(memory_space=pl.ANY)] * 3
        out_shape = [jax.ShapeDtypeStruct(s, jnp.bfloat16) for s in shapes]
        scratch = [pltpu.VMEM(s, jnp.bfloat16) for s in shapes] + [pltpu.SemaphoreType.DMA((experts, 3))]
    return pl.pallas_call(
        functools.partial(kernel, n),
        in_specs=[smem] + [vmem] * len(operands),
        out_specs=out_specs,
        out_shape=out_shape,
        scratch_shapes=scratch,
        compiler_params=pltpu.CompilerParams(vmem_limit_bytes=VMEM_LIMIT),
        cost_estimate=pl.CostEstimate(
            flops=2 * experts * n * rows * 3 * ff * depth,
            bytes_accessed=2 * experts * (n * rows * (width + 3 * ff) + 3 * ff * depth),
            transcendentals=0,
        ),
        name="weight_grads",
    )(side, *[in_vmem(v) for v in operands])


def per_device(tokens, upstream, expert_ids, gate_fixed, slots, w_gate, w_up, w_down):
    local_experts = w_gate.shape[0]
    n_group = lax.axis_size("group")
    n_ingroup = lax.axis_size("ingroup")
    experts_all = local_experts * n_group * n_ingroup
    tok_rows, top_count = expert_ids.shape
    width = tokens.shape[1]
    per_group = top_count // GROUPS_TOK
    capacity = max(2, 3 * tok_rows * top_count // (2 * experts_all))
    rows = -(-n_ingroup * capacity // 16) * 16
    z, x, core = (lax.axis_index(a) for a in ("group", "ingroup", "dp"))
    first_expert = ((z * n_ingroup + x) * local_experts).astype(jnp.int32).reshape(1)
    half = core.astype(jnp.int32).reshape(1)
    weights = load_call((w_gate, w_up, w_down))
    wide = lambda v: v.astype(jnp.float32)
    tie = lambda *trees: lax.optimization_barrier(trees)
    order = ring_order(n_group)
    along = lambda k: [(order[i], order[(i + k) % n_group]) for i in range(n_group)]
    shift = lambda s: [(i, (i + s) % n_ingroup) for i in range(n_ingroup)]

    def spread(column):
        return [column] + [lax.ppermute(column, "ingroup", shift(s)) for s in range(1, n_ingroup)]

    def chunk(blocks):
        return chunk_call(*blocks, first_expert, weights, tok_rows, capacity, rows, top_count, per_group)

    def across(others):
        return [
            lax.ppermute(others[(s - 1) * tok_rows : s * tok_rows], "ingroup", shift(-s)) for s in range(1, n_ingroup)
        ]

    def group_sum(part, backs):
        group_part = wide(part)
        for back in backs:
            group_part = group_part + wide(back)
        return group_part.astype(jnp.bfloat16)

    def homeward(group_part, k):
        return lax.ppermute(group_part, "group", along(-k))

    tokens, first_expert, half, other_half = tie(tokens, first_expert, half, 1 - half)
    first_tokens, upstream = pack_call(tokens, upstream, expert_ids, slots, gate_fixed)
    blocks, chunks, backs, sent = {}, {}, {}, {}
    last = n_group - 1
    for k in range(n_group):
        pair = [spread(tokens), spread(upstream) if k < last else [upstream]]
        if k == last:
            pair[1] += [lax.ppermute(block, "group", along(1)) for block in blocks[k - 1][1][1:]]
        if k == 0:
            pair[0][0] = first_tokens
        if k < last:
            tokens, upstream = (lax.ppermute(v, "group", along(1)) for v in (tokens, upstream))
        if k > 0:
            chunks[k - 1] = chunk(blocks[k - 1])
        tokens, pair[0], chunks, weights = tie(tokens, pair[0], chunks, weights)
        upstream, pair[1] = tie(upstream, pair[1])
        blocks[k] = pair

    for k in range(2, last - 1):
        sent[k] = homeward(group_sum(chunks[k][0], across(chunks[k][1])), k)
    backs[last - 1] = across(chunks[last - 1][1])
    near_other, blocks[last] = tie(chunks[1][1], blocks[last])
    near_other = homeward(near_other, 1)
    chunks[last] = chunk(blocks[last])
    chunks, backs = tie(chunks, backs)

    backs[last] = across(chunks[last][1])
    carried = homeward(group_sum(chunks[last - 1][0], backs[last - 1]), last)
    sent[1] = homeward(chunks[1][0], 1)
    kept = [[chunks[k][i] for k in range(n_group)] for i in (-3, -2, -1)]
    to_send = weight_call(other_half, *kept)
    other = (wide(chunks[0][1]) + wide(near_other)).astype(jnp.bfloat16)
    to_send, backs[last], carried, other = tie(to_send, backs[last], carried, other)

    got = lax.ppermute(to_send, "dp", [(0, 1), (1, 0)])
    sent[last] = homeward(group_sum(chunks[last][0], [*backs[last], carried]), last)
    backs[0] = across(other)
    got, sent[1] = tie(got, sent[1])
    grads = weight_call(half, *kept, got)
    grads, sent, backs[0] = tie(grads, sent, backs[0])
    total = wide(chunks[0][0])
    for back in backs[0]:
        total = total + wide(back)
    for back in sent.values():
        total = total + wide(back)
    return (total.astype(jnp.bfloat16), *grads)


def solution(mesh):
    rows_spec = P(("parts", "group", "ingroup", "dp"), None)
    weight_spec = P(("group", "ingroup"), None, None)
    out_specs = (
        rows_spec,
        P(("parts", "group", "ingroup"), "dp", None),
        P(("parts", "group", "ingroup"), "dp", None),
        P(("parts", "group", "ingroup"), None, "dp"),
    )
    return jax.shard_map(
        per_device,
        mesh=mesh,
        in_specs=(rows_spec,) * 5 + (weight_spec,) * 3,
        out_specs=out_specs,
        check_vma=False,
    )
```

```python
import functools

import jax
import jax.numpy as jnp
from jax import lax
from jax.experimental import pallas as pl
from jax.experimental.pallas import tpu as pltpu
from jax.sharding import PartitionSpec as P

GROUPS_TOK = 4
ROUTE_ROWS = 16
VMEM_LIMIT = 24 * 1024 * 1024


def dot(a, b, contract):
    return lax.dot_general(a, b, ((contract[:1], contract[1:]), ((), ())), preferred_element_type=jnp.float32)


def in_hbm(v):
    return pltpu.with_memory_space_constraint(v, pltpu.HBM)


def in_vmem(v):
    return pltpu.with_memory_space_constraint(v, pltpu.VMEM)


def gated_parts(pre_gate):
    logistic = jax.nn.sigmoid(pre_gate)
    return (pre_gate * logistic, logistic * (1.0 + pre_gate * (1.0 - logistic)))


def ring_order(size):
    return [0] + list(range(1, size, 2)) + list(range(2, size, 2))[::-1]


def pack_kernel(tokens, upstream, expert_ids, slots, gate_fixed, tokens_out, out, sem):
    top_count, tok_rows = expert_ids.shape
    copies = [
        pltpu.make_async_copy(tokens, tokens_out, sem.at[0]),
        pltpu.make_async_copy(upstream, out.at[pl.ds(0, tok_rows), :], sem.at[1]),
    ]
    for copy in copies:
        copy.start()
    gate = gate_fixed[...]
    out[tok_rows:, :] = jnp.zeros((ROUTE_ROWS, out.shape[1]), jnp.bfloat16)
    for i, field in enumerate((expert_ids[...], slots[...], gate >> 8, gate & 255)):
        empty = jnp.zeros((ROUTE_ROWS - top_count, tok_rows), jnp.float32)
        field = jnp.concatenate([field.astype(jnp.float32), empty], axis=0)
        out[tok_rows:, i * tok_rows : (i + 1) * tok_rows] = field.astype(jnp.bfloat16)
    for copy in copies:
        copy.wait()


def pack_call(tokens, upstream, expert_ids, slots, gate_fixed):
    tok_rows, width = tokens.shape
    vmem, hbm = (pl.BlockSpec(memory_space=m) for m in (pltpu.VMEM, pltpu.HBM))
    operands = [in_hbm(v) for v in (tokens, upstream, expert_ids.T, slots.T, gate_fixed.T)]
    return pl.pallas_call(
        pack_kernel,
        in_specs=[hbm] * 2 + [vmem] * 3,
        out_specs=[vmem] * 2,
        out_shape=[pltpu.VMEM((rows, width), jnp.bfloat16) for rows in (tok_rows, tok_rows + ROUTE_ROWS)],
        scratch_shapes=[pltpu.SemaphoreType.DMA((2,))],
        compiler_params=pltpu.CompilerParams(vmem_limit_bytes=VMEM_LIMIT),
        cost_estimate=pl.CostEstimate(flops=0, bytes_accessed=8 * tokens.size, transcendentals=0),
        name="pack",
    )(*operands)


def route_keys(route, first_expert, local_experts, capacity, rows, offset, tok_rows, top_count, per_group):
    field = lambda i: route[:top_count, i * tok_rows : (i + 1) * tok_rows]
    expert = field(0).astype(jnp.int32) - first_expert
    slot = field(1).astype(jnp.int32)
    gate = (field(2) * 256.0 + field(3)) / 65536.0
    valid = (expert >= 0) & (expert < local_experts) & (slot < capacity)
    key = jnp.where(valid, expert * rows + offset + slot, -1)
    gate = jnp.where(valid, gate, 0.0)
    pairs = []
    for i in range(per_group):
        key_out, gate_out = key[i : i + 1, :], gate[i : i + 1, :]
        for j in range(i + per_group, top_count, per_group):
            key_out = jnp.maximum(key_out, key[j : j + 1, :])
            gate_out = jnp.maximum(gate_out, gate[j : j + 1, :])
        pairs.append((key_out, gate_out))
    return pairs


def load_kernel(*refs):
    n = len(refs) // 2
    copies = [pltpu.make_async_copy(refs[i], refs[n + i], refs[-1].at[i]) for i in range(n)]
    for copy in copies:
        copy.start()
    for copy in copies:
        copy.wait()


def load_call(arrays):
    hbm, vmem = (pl.BlockSpec(memory_space=m) for m in (pltpu.HBM, pltpu.VMEM))
    return pl.pallas_call(
        load_kernel,
        in_specs=[hbm] * len(arrays),
        out_specs=[vmem] * len(arrays),
        out_shape=[pltpu.VMEM(v.shape, v.dtype) for v in arrays],
        scratch_shapes=[pltpu.SemaphoreType.DMA((len(arrays),))],
        compiler_params=pltpu.CompilerParams(vmem_limit_bytes=VMEM_LIMIT),
        cost_estimate=pl.CostEstimate(
            flops=0, bytes_accessed=sum(4 * v.size for v in arrays), transcendentals=0
        ),
        name="load",
    )(*[in_hbm(v) for v in arrays])


def chunk_kernel(n_blocks, tok_rows, capacity, rows, top_count, per_group, first_ref, *refs):
    tokens, upstream = refs[:n_blocks], refs[n_blocks : 2 * n_blocks]
    w_gate, w_up, w_down = refs[2 * n_blocks : 2 * n_blocks + 3]
    parts = refs[2 * n_blocks + 3 : -4]
    x_rows, s_rows, hids, back_all = refs[-4:]
    experts, width, ff = w_gate.shape

    pairs = []
    for b in range(n_blocks):
        route = upstream[b][tok_rows : tok_rows + ROUTE_ROWS, :].astype(jnp.float32)
        pairs.append(
            route_keys(route, first_ref[0], experts, capacity, rows, b * capacity, tok_rows, top_count, per_group)
        )
    place = lax.broadcasted_iota(jnp.int32, (experts * rows, n_blocks * tok_rows), 0)
    hot = jnp.zeros(place.shape, jnp.float32)
    gate_hot = jnp.zeros(place.shape, jnp.float32)
    for i in range(per_group):
        key = jnp.concatenate([pair[i][0] for pair in pairs], axis=1)
        gate = jnp.concatenate([pair[i][1] for pair in pairs], axis=1)
        match = place == key
        hot = jnp.where(match, 1.0, hot)
        gate_hot = jnp.where(match, gate, gate_hot)
    hot = hot.astype(jnp.bfloat16)
    row_gate = jnp.sum(gate_hot, axis=1, keepdims=True)

    x_all = jnp.concatenate([block[...] for block in tokens], axis=0)
    gathered = dot(hot, x_all, (1, 0)).astype(jnp.bfloat16)
    for e in range(experts):
        x_rows[e] = gathered[e * rows : (e + 1) * rows, :]
    u_all = jnp.concatenate([block[:tok_rows, :] for block in upstream], axis=0)
    scaled = (dot(hot, u_all, (1, 0)) * row_gate).astype(jnp.bfloat16)
    for e in range(experts):
        s_rows[e] = scaled[e * rows : (e + 1) * rows, :]

    for e in range(experts):
        pre_gate = dot(x_rows[e], w_gate[e], (1, 0))
        pre_up = dot(x_rows[e], w_up[e], (1, 0))
        grad_hidden = dot(s_rows[e], w_down[e], (1, 1))
        active, slope = gated_parts(pre_gate)
        grad_gate_pre = (grad_hidden * pre_up * slope).astype(jnp.bfloat16)
        grad_up_pre = (grad_hidden * active).astype(jnp.bfloat16)
        hids[e, :, :ff] = grad_gate_pre
        hids[e, :, ff : 2 * ff] = grad_up_pre
        hids[e, :, 2 * ff :] = (active * pre_up).astype(jnp.bfloat16)
        back = dot(grad_gate_pre, w_gate[e], (1, 1)) + dot(grad_up_pre, w_up[e], (1, 1))
        back_all[e * rows : (e + 1) * rows, :] = back.astype(jnp.bfloat16)

    summed = dot(hot, back_all[...], (0, 0)).astype(jnp.bfloat16)
    start = 0
    for part in parts:
        part[...] = summed[start : start + part.shape[0], :]
        start += part.shape[0]


def chunk_call(tokens, upstream, first_expert, weights, tok_rows, capacity, rows, top_count, per_group):
    n_blocks = len(tokens)
    n_tok = n_blocks * tok_rows
    experts, width, ff = weights[0].shape
    part_shapes = [(tok_rows, width), (n_tok - tok_rows, width)]
    kept_shapes = [(experts, rows, width), (experts, rows, width), (experts, rows, 3 * ff)]
    smem, vmem = (pl.BlockSpec(memory_space=m) for m in (pltpu.SMEM, pltpu.VMEM))
    out_shapes = part_shapes + kept_shapes
    return pl.pallas_call(
        functools.partial(chunk_kernel, n_blocks, tok_rows, capacity, rows, top_count, per_group),
        in_specs=[smem] + [vmem] * (2 * n_blocks + 3),
        out_specs=[vmem] * len(out_shapes),
        out_shape=[pltpu.VMEM(shape, jnp.bfloat16) for shape in out_shapes],
        scratch_shapes=[pltpu.VMEM((experts * rows, width), jnp.bfloat16)],
        compiler_params=pltpu.CompilerParams(vmem_limit_bytes=VMEM_LIMIT),
        cost_estimate=pl.CostEstimate(
            flops=2 * experts * rows * width * (5 * ff + 3 * n_tok),
            bytes_accessed=6 * experts * width * ff + 8 * n_tok * width,
            transcendentals=0,
        ),
        name="chunk",
    )(first_expert, *[in_vmem(v) for v in (*tokens, *upstream, *weights)])


def halves_of(n, e, side, refs):
    depth = refs[0].shape[2] // 2
    cols = pl.ds(pl.multiple_of(side * depth, depth), depth)
    cat = lambda parts: jnp.concatenate(parts, axis=0)
    x_rows, s_rows = (cat([ref[e, :, cols] for ref in refs[i * n : (i + 1) * n]]) for i in range(2))
    hid = cat([ref[e] for ref in refs[2 * n : 3 * n]])
    ff = hid.shape[1] // 3
    return dot(x_rows, hid[:, : 2 * ff], (0, 0)), dot(hid[:, 2 * ff :], s_rows, (0, 0))


def send_kernel(n, side_ref, *refs):
    out = refs[3 * n]
    for e in range(out.shape[0]):
        gate_up, down = halves_of(n, e, side_ref[0], refs)
        depth = gate_up.shape[0]
        out[e, :depth, :] = gate_up.astype(jnp.bfloat16)
        out[e, depth:, :] = down.astype(jnp.bfloat16)


def keep_kernel(n, side_ref, *refs):
    got, outs = refs[3 * n], refs[3 * n + 1 : 3 * n + 4]
    buffers, sem = refs[3 * n + 4 : 3 * n + 7], refs[3 * n + 7]
    copies = []
    for e in range(got.shape[0]):
        gate_up, down = halves_of(n, e, side_ref[0], refs)
        depth = gate_up.shape[0]
        ff = down.shape[0]
        gate_up = gate_up + got[e, :depth, :].astype(jnp.float32)
        buffers[0][e] = gate_up[:, :ff].astype(jnp.bfloat16)
        buffers[1][e] = gate_up[:, ff:].astype(jnp.bfloat16)
        buffers[2][e] = (down + got[e, depth:, :].astype(jnp.float32)).astype(jnp.bfloat16)
        for i in range(3):
            copy = pltpu.make_async_copy(buffers[i].at[e], outs[i].at[e], sem.at[e, i])
            copy.start()
            copies.append(copy)
    for copy in copies:
        copy.wait()


def weight_call(side, x_rows, s_rows, hids, got=None):
    n = len(x_rows)
    experts, rows, width = x_rows[0].shape
    ff = hids[0].shape[2] // 3
    depth = width // 2
    smem, vmem = (pl.BlockSpec(memory_space=m) for m in (pltpu.SMEM, pltpu.VMEM))
    operands = [*x_rows, *s_rows, *hids]
    scratch = []
    if got is None:
        kernel, out_specs = send_kernel, vmem
        out_shape = pltpu.VMEM((experts, depth + ff, depth), jnp.bfloat16)
    else:
        kernel = keep_kernel
        operands = operands + [got]
        shapes = [(experts, depth, ff), (experts, depth, ff), (experts, ff, depth)]
        out_specs = [pl.BlockSpec(memory_space=pl.ANY)] * 3
        out_shape = [jax.ShapeDtypeStruct(s, jnp.bfloat16) for s in shapes]
        scratch = [pltpu.VMEM(s, jnp.bfloat16) for s in shapes] + [pltpu.SemaphoreType.DMA((experts, 3))]
    return pl.pallas_call(
        functools.partial(kernel, n),
        in_specs=[smem] + [vmem] * len(operands),
        out_specs=out_specs,
        out_shape=out_shape,
        scratch_shapes=scratch,
        compiler_params=pltpu.CompilerParams(vmem_limit_bytes=VMEM_LIMIT),
        cost_estimate=pl.CostEstimate(
            flops=2 * experts * n * rows * 3 * ff * depth,
            bytes_accessed=2 * experts * (n * rows * (width + 3 * ff) + 3 * ff * depth),
            transcendentals=0,
        ),
        name="weight_grads",
    )(side, *[in_vmem(v) for v in operands])


def per_device(tokens, upstream, expert_ids, gate_fixed, slots, w_gate, w_up, w_down):
    local_experts = w_gate.shape[0]
    n_group = lax.axis_size("group")
    n_ingroup = lax.axis_size("ingroup")
    experts_all = local_experts * n_group * n_ingroup
    tok_rows, top_count = expert_ids.shape
    width = tokens.shape[1]
    per_group = top_count // GROUPS_TOK
    capacity = max(2, 3 * tok_rows * top_count // (2 * experts_all))
    rows = -(-n_ingroup * capacity // 16) * 16
    z, x, core = (lax.axis_index(a) for a in ("group", "ingroup", "dp"))
    first_expert = ((z * n_ingroup + x) * local_experts).astype(jnp.int32).reshape(1)
    half = core.astype(jnp.int32).reshape(1)
    wide = lambda v: v.astype(jnp.float32)
    tie = lambda *trees: lax.optimization_barrier(trees)
    order = ring_order(n_group)
    along = lambda k: [(order[i], order[(i + k) % n_group]) for i in range(n_group)]
    shift = lambda s: [(i, (i + s) % n_ingroup) for i in range(n_ingroup)]

    def spread(column):
        return [column] + [lax.ppermute(column, "ingroup", shift(s)) for s in range(1, n_ingroup)]

    def chunk(blocks):
        return chunk_call(*blocks, first_expert, weights, tok_rows, capacity, rows, top_count, per_group)

    def across(others):
        return [
            lax.ppermute(others[(s - 1) * tok_rows : s * tok_rows], "ingroup", shift(-s)) for s in range(1, n_ingroup)
        ]

    def group_sum(part, backs):
        group_part = wide(part)
        for back in backs:
            group_part = group_part + wide(back)
        return group_part.astype(jnp.bfloat16)

    def homeward(group_part, k):
        return lax.ppermute(group_part, "group", along(-k))

    tokens, first_expert, half, other_half = tie(tokens, first_expert, half, 1 - half)
    weights = load_call((w_gate, w_up, w_down))
    first_tokens, upstream = pack_call(tokens, upstream, expert_ids, slots, gate_fixed)
    blocks, chunks, backs, sent = {}, {}, {}, {}
    last = n_group - 1
    for k in range(n_group):
        pair = [spread(tokens), spread(upstream) if k < last else [upstream]]
        if k == last:
            pair[1] += [lax.ppermute(block, "group", along(1)) for block in blocks[k - 1][1][1:]]
        if k == 0:
            pair[0][0] = first_tokens
        if k < last:
            tokens, upstream = (lax.ppermute(v, "group", along(1)) for v in (tokens, upstream))
        if k > 0:
            chunks[k - 1] = chunk(blocks[k - 1])
        upstream, pair[1], chunks, weights = tie(upstream, pair[1], chunks, weights)
        tokens, pair[0] = tie(tokens, pair[0])
        blocks[k] = pair

    for k in range(2, last - 1):
        sent[k] = homeward(group_sum(chunks[k][0], across(chunks[k][1])), k)
    backs[1] = across(chunks[1][1])
    backs[last - 1] = across(chunks[last - 1][1])
    chunks[last] = chunk(blocks[last])
    chunks, backs[1] = tie(chunks, backs[1])

    backs[last] = across(chunks[last][1])
    sent[1] = homeward(group_sum(chunks[1][0], backs[1]), 1)
    carried = homeward(group_sum(chunks[last - 1][0], backs[last - 1]), last)
    kept = [[chunks[k][i] for k in range(n_group)] for i in (-3, -2, -1)]
    kept, backs[last - 1] = tie(kept, backs[last - 1])
    to_send = weight_call(other_half, *kept)
    got = lax.ppermute(to_send, "dp", [(0, 1), (1, 0)])
    other, to_send = tie(chunks[0][1], to_send)
    backs[0] = across(other)
    sent[last] = homeward(group_sum(chunks[last][0], [*backs[last], carried]), last)
    got, carried, backs[last] = tie(got, carried, backs[last])
    grads = weight_call(half, *kept, got)
    grads, sent, backs[0] = tie(grads, sent, backs[0])
    total = wide(chunks[0][0])
    for back in backs[0]:
        total = total + wide(back)
    for back in sent.values():
        total = total + wide(back)
    return (total.astype(jnp.bfloat16), *grads)


def solution(mesh):
    rows_spec = P(("parts", "group", "ingroup", "dp"), None)
    weight_spec = P(("group", "ingroup"), None, None)
    out_specs = (
        rows_spec,
        P(("parts", "group", "ingroup"), "dp", None),
        P(("parts", "group", "ingroup"), "dp", None),
        P(("parts", "group", "ingroup"), None, "dp"),
    )
    return jax.shard_map(
        per_device,
        mesh=mesh,
        in_specs=(rows_spec,) * 5 + (weight_spec,) * 3,
        out_specs=out_specs,
        check_vma=False,
    )
```

```python
import functools

import jax
import jax.numpy as jnp
from jax import lax
from jax.experimental import pallas as pl
from jax.experimental.pallas import tpu as pltpu
from jax.sharding import PartitionSpec as P

GROUPS_TOK = 4
ROUTE_ROWS = 16
VMEM_LIMIT = 24 * 1024 * 1024


def dot(a, b, contract):
    return lax.dot_general(a, b, ((contract[:1], contract[1:]), ((), ())), preferred_element_type=jnp.float32)


def in_hbm(v):
    return pltpu.with_memory_space_constraint(v, pltpu.HBM)


def in_vmem(v):
    return pltpu.with_memory_space_constraint(v, pltpu.VMEM)


def gated_parts(pre_gate):
    logistic = jax.nn.sigmoid(pre_gate)
    return (pre_gate * logistic, logistic * (1.0 + pre_gate * (1.0 - logistic)))


def ring_order(size):
    return [0] + list(range(1, size, 2)) + list(range(2, size, 2))[::-1]


def pack_kernel(tokens, upstream, expert_ids, slots, gate_fixed, tokens_out, out, sem):
    top_count, tok_rows = expert_ids.shape
    copies = [
        pltpu.make_async_copy(tokens, tokens_out, sem.at[0]),
        pltpu.make_async_copy(upstream, out.at[pl.ds(0, tok_rows), :], sem.at[1]),
    ]
    for copy in copies:
        copy.start()
    gate = gate_fixed[...]
    out[tok_rows:, :] = jnp.zeros((ROUTE_ROWS, out.shape[1]), jnp.bfloat16)
    for i, field in enumerate((expert_ids[...], slots[...], gate >> 8, gate & 255)):
        empty = jnp.zeros((ROUTE_ROWS - top_count, tok_rows), jnp.float32)
        field = jnp.concatenate([field.astype(jnp.float32), empty], axis=0)
        out[tok_rows:, i * tok_rows : (i + 1) * tok_rows] = field.astype(jnp.bfloat16)
    for copy in copies:
        copy.wait()


def pack_call(tokens, upstream, expert_ids, slots, gate_fixed):
    tok_rows, width = tokens.shape
    vmem, hbm = (pl.BlockSpec(memory_space=m) for m in (pltpu.VMEM, pltpu.HBM))
    operands = [in_hbm(v) for v in (tokens, upstream, expert_ids.T, slots.T, gate_fixed.T)]
    return pl.pallas_call(
        pack_kernel,
        in_specs=[hbm] * 2 + [vmem] * 3,
        out_specs=[vmem] * 2,
        out_shape=[pltpu.VMEM((rows, width), jnp.bfloat16) for rows in (tok_rows, tok_rows + ROUTE_ROWS)],
        scratch_shapes=[pltpu.SemaphoreType.DMA((2,))],
        compiler_params=pltpu.CompilerParams(vmem_limit_bytes=VMEM_LIMIT),
        cost_estimate=pl.CostEstimate(flops=0, bytes_accessed=8 * tokens.size, transcendentals=0),
        name="pack",
    )(*operands)


def route_keys(route, first_expert, local_experts, capacity, rows, offset, tok_rows, top_count, per_group):
    field = lambda i: route[:top_count, i * tok_rows : (i + 1) * tok_rows]
    expert = field(0).astype(jnp.int32) - first_expert
    slot = field(1).astype(jnp.int32)
    gate = (field(2) * 256.0 + field(3)) / 65536.0
    valid = (expert >= 0) & (expert < local_experts) & (slot < capacity)
    key = jnp.where(valid, expert * rows + offset + slot, -1)
    gate = jnp.where(valid, gate, 0.0)
    pairs = []
    for i in range(per_group):
        key_out, gate_out = key[i : i + 1, :], gate[i : i + 1, :]
        for j in range(i + per_group, top_count, per_group):
            key_out = jnp.maximum(key_out, key[j : j + 1, :])
            gate_out = jnp.maximum(gate_out, gate[j : j + 1, :])
        pairs.append((key_out, gate_out))
    return pairs


def load_kernel(*refs):
    n = len(refs) // 2
    copies = [pltpu.make_async_copy(refs[i], refs[n + i], refs[-1].at[i]) for i in range(n)]
    for copy in copies:
        copy.start()
    for copy in copies:
        copy.wait()


def load_call(arrays):
    hbm, vmem = (pl.BlockSpec(memory_space=m) for m in (pltpu.HBM, pltpu.VMEM))
    return pl.pallas_call(
        load_kernel,
        in_specs=[hbm] * len(arrays),
        out_specs=[vmem] * len(arrays),
        out_shape=[pltpu.VMEM(v.shape, v.dtype) for v in arrays],
        scratch_shapes=[pltpu.SemaphoreType.DMA((len(arrays),))],
        compiler_params=pltpu.CompilerParams(vmem_limit_bytes=VMEM_LIMIT),
        cost_estimate=pl.CostEstimate(
            flops=0, bytes_accessed=sum(4 * v.size for v in arrays), transcendentals=0
        ),
        name="load",
    )(*[in_hbm(v) for v in arrays])


def chunk_kernel(n_blocks, tok_rows, capacity, rows, top_count, per_group, first_ref, *refs):
    tokens, upstream = refs[:n_blocks], refs[n_blocks : 2 * n_blocks]
    w_gate, w_up, w_down = refs[2 * n_blocks : 2 * n_blocks + 3]
    parts = refs[2 * n_blocks + 3 : -4]
    x_rows, s_rows, hids, back_all = refs[-4:]
    experts, width, ff = w_gate.shape

    pairs = []
    for b in range(n_blocks):
        route = upstream[b][tok_rows : tok_rows + ROUTE_ROWS, :].astype(jnp.float32)
        pairs.append(
            route_keys(route, first_ref[0], experts, capacity, rows, b * capacity, tok_rows, top_count, per_group)
        )
    place = lax.broadcasted_iota(jnp.int32, (experts * rows, n_blocks * tok_rows), 0)
    hot = jnp.zeros(place.shape, jnp.float32)
    gate_hot = jnp.zeros(place.shape, jnp.float32)
    for i in range(per_group):
        key = jnp.concatenate([pair[i][0] for pair in pairs], axis=1)
        gate = jnp.concatenate([pair[i][1] for pair in pairs], axis=1)
        match = place == key
        hot = jnp.where(match, 1.0, hot)
        gate_hot = jnp.where(match, gate, gate_hot)
    hot = hot.astype(jnp.bfloat16)
    row_gate = jnp.sum(gate_hot, axis=1, keepdims=True)

    x_all = jnp.concatenate([block[...] for block in tokens], axis=0)
    gathered = dot(hot, x_all, (1, 0)).astype(jnp.bfloat16)
    for e in range(experts):
        x_rows[e] = gathered[e * rows : (e + 1) * rows, :]
    u_all = jnp.concatenate([block[:tok_rows, :] for block in upstream], axis=0)
    scaled = (dot(hot, u_all, (1, 0)) * row_gate).astype(jnp.bfloat16)
    for e in range(experts):
        s_rows[e] = scaled[e * rows : (e + 1) * rows, :]

    for e in range(experts):
        pre_gate = dot(x_rows[e], w_gate[e], (1, 0))
        pre_up = dot(x_rows[e], w_up[e], (1, 0))
        grad_hidden = dot(s_rows[e], w_down[e], (1, 1))
        active, slope = gated_parts(pre_gate)
        grad_gate_pre = (grad_hidden * pre_up * slope).astype(jnp.bfloat16)
        grad_up_pre = (grad_hidden * active).astype(jnp.bfloat16)
        hids[e, :, :ff] = grad_gate_pre
        hids[e, :, ff : 2 * ff] = grad_up_pre
        hids[e, :, 2 * ff :] = (active * pre_up).astype(jnp.bfloat16)
        back = dot(grad_gate_pre, w_gate[e], (1, 1)) + dot(grad_up_pre, w_up[e], (1, 1))
        back_all[e * rows : (e + 1) * rows, :] = back.astype(jnp.bfloat16)

    summed = dot(hot, back_all[...], (0, 0)).astype(jnp.bfloat16)
    start = 0
    for part in parts:
        part[...] = summed[start : start + part.shape[0], :]
        start += part.shape[0]


def chunk_call(tokens, upstream, first_expert, weights, tok_rows, capacity, rows, top_count, per_group, joined):
    n_blocks = len(tokens)
    n_tok = n_blocks * tok_rows
    experts, width, ff = weights[0].shape
    part_shapes = [(n_tok, width)] if joined else [(tok_rows, width), (n_tok - tok_rows, width)]
    kept_shapes = [(experts, rows, width), (experts, rows, width), (experts, rows, 3 * ff)]
    smem, vmem = (pl.BlockSpec(memory_space=m) for m in (pltpu.SMEM, pltpu.VMEM))
    out_shapes = part_shapes + kept_shapes
    return pl.pallas_call(
        functools.partial(chunk_kernel, n_blocks, tok_rows, capacity, rows, top_count, per_group),
        in_specs=[smem] + [vmem] * (2 * n_blocks + 3),
        out_specs=[vmem] * len(out_shapes),
        out_shape=[pltpu.VMEM(shape, jnp.bfloat16) for shape in out_shapes],
        scratch_shapes=[pltpu.VMEM((experts * rows, width), jnp.bfloat16)],
        compiler_params=pltpu.CompilerParams(vmem_limit_bytes=VMEM_LIMIT),
        cost_estimate=pl.CostEstimate(
            flops=2 * experts * rows * width * (5 * ff + 3 * n_tok),
            bytes_accessed=6 * experts * width * ff + 8 * n_tok * width,
            transcendentals=0,
        ),
        name="chunk",
    )(first_expert, *[in_vmem(v) for v in (*tokens, *upstream, *weights)])


def halves_of(n, e, side, refs):
    depth = refs[0].shape[2] // 2
    cols = pl.ds(pl.multiple_of(side * depth, depth), depth)
    cat = lambda parts: jnp.concatenate(parts, axis=0)
    x_rows, s_rows = (cat([ref[e, :, cols] for ref in refs[i * n : (i + 1) * n]]) for i in range(2))
    hid = cat([ref[e] for ref in refs[2 * n : 3 * n]])
    ff = hid.shape[1] // 3
    return dot(x_rows, hid[:, : 2 * ff], (0, 0)), dot(hid[:, 2 * ff :], s_rows, (0, 0))


def send_kernel(n, side_ref, *refs):
    out = refs[3 * n]
    for e in range(out.shape[0]):
        gate_up, down = halves_of(n, e, side_ref[0], refs)
        depth = gate_up.shape[0]
        out[e, :depth, :] = gate_up.astype(jnp.bfloat16)
        out[e, depth:, :] = down.astype(jnp.bfloat16)


def keep_kernel(n, side_ref, *refs):
    got, outs = refs[3 * n], refs[3 * n + 1 : 3 * n + 4]
    buffers, sem = refs[3 * n + 4 : 3 * n + 7], refs[3 * n + 7]
    copies = []
    for e in range(got.shape[0]):
        gate_up, down = halves_of(n, e, side_ref[0], refs)
        depth = gate_up.shape[0]
        ff = down.shape[0]
        gate_up = gate_up + got[e, :depth, :].astype(jnp.float32)
        buffers[0][e] = gate_up[:, :ff].astype(jnp.bfloat16)
        buffers[1][e] = gate_up[:, ff:].astype(jnp.bfloat16)
        buffers[2][e] = (down + got[e, depth:, :].astype(jnp.float32)).astype(jnp.bfloat16)
        for i in range(3):
            copy = pltpu.make_async_copy(buffers[i].at[e], outs[i].at[e], sem.at[e, i])
            copy.start()
            copies.append(copy)
    for copy in copies:
        copy.wait()


def weight_call(side, x_rows, s_rows, hids, got=None):
    n = len(x_rows)
    experts, rows, width = x_rows[0].shape
    ff = hids[0].shape[2] // 3
    depth = width // 2
    smem, vmem = (pl.BlockSpec(memory_space=m) for m in (pltpu.SMEM, pltpu.VMEM))
    operands = [*x_rows, *s_rows, *hids]
    scratch = []
    if got is None:
        kernel, out_specs = send_kernel, vmem
        out_shape = pltpu.VMEM((experts, depth + ff, depth), jnp.bfloat16)
    else:
        kernel = keep_kernel
        operands = operands + [got]
        shapes = [(experts, depth, ff), (experts, depth, ff), (experts, ff, depth)]
        out_specs = [pl.BlockSpec(memory_space=pl.ANY)] * 3
        out_shape = [jax.ShapeDtypeStruct(s, jnp.bfloat16) for s in shapes]
        scratch = [pltpu.VMEM(s, jnp.bfloat16) for s in shapes] + [pltpu.SemaphoreType.DMA((experts, 3))]
    return pl.pallas_call(
        functools.partial(kernel, n),
        in_specs=[smem] + [vmem] * len(operands),
        out_specs=out_specs,
        out_shape=out_shape,
        scratch_shapes=scratch,
        compiler_params=pltpu.CompilerParams(vmem_limit_bytes=VMEM_LIMIT),
        cost_estimate=pl.CostEstimate(
            flops=2 * experts * n * rows * 3 * ff * depth,
            bytes_accessed=2 * experts * (n * rows * (width + 3 * ff) + 3 * ff * depth),
            transcendentals=0,
        ),
        name="weight_grads",
    )(side, *[in_vmem(v) for v in operands])


def per_device(tokens, upstream, expert_ids, gate_fixed, slots, w_gate, w_up, w_down):
    local_experts = w_gate.shape[0]
    n_group = lax.axis_size("group")
    n_ingroup = lax.axis_size("ingroup")
    experts_all = local_experts * n_group * n_ingroup
    tok_rows, top_count = expert_ids.shape
    width = tokens.shape[1]
    per_group = top_count // GROUPS_TOK
    capacity = max(2, 3 * tok_rows * top_count // (2 * experts_all))
    rows = -(-n_ingroup * capacity // 16) * 16
    z, x, core = (lax.axis_index(a) for a in ("group", "ingroup", "dp"))
    first_expert = ((z * n_ingroup + x) * local_experts).astype(jnp.int32).reshape(1)
    half = core.astype(jnp.int32).reshape(1)
    wide = lambda v: v.astype(jnp.float32)
    tie = lambda *trees: lax.optimization_barrier(trees)
    order = ring_order(n_group)
    along = lambda k: [(order[i], order[(i + k) % n_group]) for i in range(n_group)]
    shift = lambda s: [(i, (i + s) % n_ingroup) for i in range(n_ingroup)]

    def spread(column):
        return [column] + [lax.ppermute(column, "ingroup", shift(s)) for s in range(1, n_ingroup)]

    def chunk(blocks, joined=False):
        return chunk_call(*blocks, first_expert, weights, tok_rows, capacity, rows, top_count, per_group, joined)

    def across(others):
        return [
            lax.ppermute(others[(s - 1) * tok_rows : s * tok_rows], "ingroup", shift(-s)) for s in range(1, n_ingroup)
        ]

    def group_sum(part, backs):
        group_part = wide(part)
        for back in backs:
            group_part = group_part + wide(back)
        return group_part.astype(jnp.bfloat16)

    def homeward(group_part, k):
        return lax.ppermute(group_part, "group", along(-k))

    tokens, first_expert, half, other_half = tie(tokens, first_expert, half, 1 - half)
    weights = load_call((w_gate, w_up, w_down))
    first_tokens, upstream = pack_call(tokens, upstream, expert_ids, slots, gate_fixed)
    blocks, chunks, backs, sent = {}, {}, {}, {}
    last = n_group - 1
    for k in range(n_group):
        pair = [spread(tokens) if k < last else [tokens], spread(upstream)]
        if k == last:
            pair[0] += [lax.ppermute(block, "group", along(1)) for block in blocks[k - 1][0][1:]]
        if k == 0:
            pair[0][0] = first_tokens
        if k < last:
            tokens, upstream = (lax.ppermute(v, "group", along(1)) for v in (tokens, upstream))
        if k > 0:
            chunks[k - 1] = chunk(blocks[k - 1], k - 1 == 1)
        upstream, pair[1], chunks, weights = tie(upstream, pair[1], chunks, weights)
        tokens, pair[0] = tie(tokens, pair[0])
        blocks[k] = pair

    for k in range(2, last - 1):
        sent[k] = homeward(group_sum(chunks[k][0], across(chunks[k][1])), k)
    backs[last - 1] = across(chunks[last - 1][1])
    near, blocks[last] = tie(chunks[1][0], blocks[last])
    near = homeward(near, 1)
    chunks[last] = chunk(blocks[last])
    backs[last] = across(chunks[last][1])
    chunks, backs[last - 1], near = tie(chunks, backs[last - 1], near)

    carried = homeward(group_sum(chunks[last - 1][0], backs[last - 1]), last)
    kept = [[chunks[k][i] for k in range(n_group)] for i in (-3, -2, -1)]
    to_send = weight_call(other_half, *kept)
    other = (wide(chunks[0][1]) + wide(near[tok_rows:])).astype(jnp.bfloat16)
    to_send, backs[last], carried, other = tie(to_send, backs[last], carried, other)

    got = lax.ppermute(to_send, "dp", [(0, 1), (1, 0)])
    sent[last] = homeward(group_sum(chunks[last][0], [*backs[last], carried]), last)
    backs[0] = across(other)
    grads = weight_call(half, *kept, got)
    grads, sent, backs[0] = tie(grads, sent, backs[0])
    total = wide(chunks[0][0]) + wide(near[:tok_rows])
    for back in backs[0]:
        total = total + wide(back)
    for back in sent.values():
        total = total + wide(back)
    return (total.astype(jnp.bfloat16), *grads)


def solution(mesh):
    rows_spec = P(("parts", "group", "ingroup", "dp"), None)
    weight_spec = P(("group", "ingroup"), None, None)
    out_specs = (
        rows_spec,
        P(("parts", "group", "ingroup"), "dp", None),
        P(("parts", "group", "ingroup"), "dp", None),
        P(("parts", "group", "ingroup"), None, "dp"),
    )
    return jax.shard_map(
        per_device,
        mesh=mesh,
        in_specs=(rows_spec,) * 5 + (weight_spec,) * 3,
        out_specs=out_specs,
        check_vma=False,
    )
```

```python
import functools

import jax
import jax.numpy as jnp
from jax import lax
from jax.experimental import pallas as pl
from jax.experimental.pallas import tpu as pltpu
from jax.sharding import PartitionSpec as P

GROUPS_TOK = 4
ROUTE_ROWS = 16
VMEM_LIMIT = 24 * 1024 * 1024


def dot(a, b, contract):
    return lax.dot_general(a, b, ((contract[:1], contract[1:]), ((), ())), preferred_element_type=jnp.float32)


def in_hbm(v):
    return pltpu.with_memory_space_constraint(v, pltpu.HBM)


def in_vmem(v):
    return pltpu.with_memory_space_constraint(v, pltpu.VMEM)


def gated_parts(pre_gate):
    logistic = jax.nn.sigmoid(pre_gate)
    return (pre_gate * logistic, logistic * (1.0 + pre_gate * (1.0 - logistic)))


def ring_order(size):
    return [0] + list(range(1, size, 2)) + list(range(2, size, 2))[::-1]


def pack_kernel(tokens, upstream, expert_ids, slots, gate_fixed, tokens_out, out, sem):
    top_count, tok_rows = expert_ids.shape
    copies = [
        pltpu.make_async_copy(tokens, tokens_out, sem.at[0]),
        pltpu.make_async_copy(upstream, out.at[pl.ds(0, tok_rows), :], sem.at[1]),
    ]
    for copy in copies:
        copy.start()
    gate = gate_fixed[...]
    out[tok_rows:, :] = jnp.zeros((ROUTE_ROWS, out.shape[1]), jnp.bfloat16)
    for i, field in enumerate((expert_ids[...], slots[...], gate >> 8, gate & 255)):
        empty = jnp.zeros((ROUTE_ROWS - top_count, tok_rows), jnp.float32)
        field = jnp.concatenate([field.astype(jnp.float32), empty], axis=0)
        out[tok_rows:, i * tok_rows : (i + 1) * tok_rows] = field.astype(jnp.bfloat16)
    for copy in copies:
        copy.wait()


def pack_call(tokens, upstream, expert_ids, slots, gate_fixed):
    tok_rows, width = tokens.shape
    vmem, hbm = (pl.BlockSpec(memory_space=m) for m in (pltpu.VMEM, pltpu.HBM))
    operands = [in_hbm(v) for v in (tokens, upstream, expert_ids.T, slots.T, gate_fixed.T)]
    return pl.pallas_call(
        pack_kernel,
        in_specs=[hbm] * 2 + [vmem] * 3,
        out_specs=[vmem] * 2,
        out_shape=[pltpu.VMEM((rows, width), jnp.bfloat16) for rows in (tok_rows, tok_rows + ROUTE_ROWS)],
        scratch_shapes=[pltpu.SemaphoreType.DMA((2,))],
        compiler_params=pltpu.CompilerParams(vmem_limit_bytes=VMEM_LIMIT),
        cost_estimate=pl.CostEstimate(flops=0, bytes_accessed=8 * tokens.size, transcendentals=0),
        name="pack",
    )(*operands)


def route_keys(route, first_expert, local_experts, capacity, rows, offset, tok_rows, top_count, per_group):
    field = lambda i: route[:top_count, i * tok_rows : (i + 1) * tok_rows]
    expert = field(0).astype(jnp.int32) - first_expert
    slot = field(1).astype(jnp.int32)
    gate = (field(2) * 256.0 + field(3)) / 65536.0
    valid = (expert >= 0) & (expert < local_experts) & (slot < capacity)
    key = jnp.where(valid, expert * rows + offset + slot, -1)
    gate = jnp.where(valid, gate, 0.0)
    pairs = []
    for i in range(per_group):
        key_out, gate_out = key[i : i + 1, :], gate[i : i + 1, :]
        for j in range(i + per_group, top_count, per_group):
            key_out = jnp.maximum(key_out, key[j : j + 1, :])
            gate_out = jnp.maximum(gate_out, gate[j : j + 1, :])
        pairs.append((key_out, gate_out))
    return pairs


def load_kernel(*refs):
    n = len(refs) // 2
    copies = [pltpu.make_async_copy(refs[i], refs[n + i], refs[-1].at[i]) for i in range(n)]
    for copy in copies:
        copy.start()
    for copy in copies:
        copy.wait()


def load_call(arrays):
    hbm, vmem = (pl.BlockSpec(memory_space=m) for m in (pltpu.HBM, pltpu.VMEM))
    return pl.pallas_call(
        load_kernel,
        in_specs=[hbm] * len(arrays),
        out_specs=[vmem] * len(arrays),
        out_shape=[pltpu.VMEM(v.shape, v.dtype) for v in arrays],
        scratch_shapes=[pltpu.SemaphoreType.DMA((len(arrays),))],
        compiler_params=pltpu.CompilerParams(vmem_limit_bytes=VMEM_LIMIT),
        cost_estimate=pl.CostEstimate(
            flops=0, bytes_accessed=sum(4 * v.size for v in arrays), transcendentals=0
        ),
        name="load",
    )(*[in_hbm(v) for v in arrays])


def chunk_kernel(n_blocks, tok_rows, capacity, rows, top_count, per_group, first_ref, *refs):
    tokens, upstream = refs[:n_blocks], refs[n_blocks : 2 * n_blocks]
    w_gate, w_up, w_down = refs[2 * n_blocks : 2 * n_blocks + 3]
    parts = refs[2 * n_blocks + 3 : -4]
    x_rows, s_rows, hids, back_all = refs[-4:]
    experts, width, ff = w_gate.shape

    pairs = []
    for b in range(n_blocks):
        route = upstream[b][tok_rows : tok_rows + ROUTE_ROWS, :].astype(jnp.float32)
        pairs.append(
            route_keys(route, first_ref[0], experts, capacity, rows, b * capacity, tok_rows, top_count, per_group)
        )
    place = lax.broadcasted_iota(jnp.int32, (experts * rows, n_blocks * tok_rows), 0)
    hot = jnp.zeros(place.shape, jnp.float32)
    gate_hot = jnp.zeros(place.shape, jnp.float32)
    for i in range(per_group):
        key = jnp.concatenate([pair[i][0] for pair in pairs], axis=1)
        gate = jnp.concatenate([pair[i][1] for pair in pairs], axis=1)
        match = place == key
        hot = jnp.where(match, 1.0, hot)
        gate_hot = jnp.where(match, gate, gate_hot)
    hot = hot.astype(jnp.bfloat16)
    row_gate = jnp.sum(gate_hot, axis=1, keepdims=True)

    x_all = jnp.concatenate([block[...] for block in tokens], axis=0)
    gathered = dot(hot, x_all, (1, 0)).astype(jnp.bfloat16)
    for e in range(experts):
        x_rows[e] = gathered[e * rows : (e + 1) * rows, :]
    u_all = jnp.concatenate([block[:tok_rows, :] for block in upstream], axis=0)
    scaled = (dot(hot, u_all, (1, 0)) * row_gate).astype(jnp.bfloat16)
    for e in range(experts):
        s_rows[e] = scaled[e * rows : (e + 1) * rows, :]

    for e in range(experts):
        pre_gate = dot(x_rows[e], w_gate[e], (1, 0))
        pre_up = dot(x_rows[e], w_up[e], (1, 0))
        grad_hidden = dot(s_rows[e], w_down[e], (1, 1))
        active, slope = gated_parts(pre_gate)
        grad_gate_pre = (grad_hidden * pre_up * slope).astype(jnp.bfloat16)
        grad_up_pre = (grad_hidden * active).astype(jnp.bfloat16)
        hids[e, :, :ff] = grad_gate_pre
        hids[e, :, ff : 2 * ff] = grad_up_pre
        hids[e, :, 2 * ff :] = (active * pre_up).astype(jnp.bfloat16)
        back = dot(grad_gate_pre, w_gate[e], (1, 1)) + dot(grad_up_pre, w_up[e], (1, 1))
        back_all[e * rows : (e + 1) * rows, :] = back.astype(jnp.bfloat16)

    summed = dot(hot, back_all[...], (0, 0)).astype(jnp.bfloat16)
    start = 0
    for part in parts:
        part[...] = summed[start : start + part.shape[0], :]
        start += part.shape[0]


def chunk_call(tokens, upstream, first_expert, weights, tok_rows, capacity, rows, top_count, per_group):
    n_blocks = len(tokens)
    n_tok = n_blocks * tok_rows
    experts, width, ff = weights[0].shape
    part_shapes = [(tok_rows, width), (n_tok - tok_rows, width)]
    kept_shapes = [(experts, rows, width), (experts, rows, width), (experts, rows, 3 * ff)]
    smem, vmem = (pl.BlockSpec(memory_space=m) for m in (pltpu.SMEM, pltpu.VMEM))
    out_shapes = part_shapes + kept_shapes
    return pl.pallas_call(
        functools.partial(chunk_kernel, n_blocks, tok_rows, capacity, rows, top_count, per_group),
        in_specs=[smem] + [vmem] * (2 * n_blocks + 3),
        out_specs=[vmem] * len(out_shapes),
        out_shape=[pltpu.VMEM(shape, jnp.bfloat16) for shape in out_shapes],
        scratch_shapes=[pltpu.VMEM((experts * rows, width), jnp.bfloat16)],
        compiler_params=pltpu.CompilerParams(vmem_limit_bytes=VMEM_LIMIT),
        cost_estimate=pl.CostEstimate(
            flops=2 * experts * rows * width * (5 * ff + 3 * n_tok),
            bytes_accessed=6 * experts * width * ff + 8 * n_tok * width,
            transcendentals=0,
        ),
        name="chunk",
    )(first_expert, *[in_vmem(v) for v in (*tokens, *upstream, *weights)])


def halves_of(n, e, side, refs):
    depth = refs[0].shape[2] // 2
    cols = pl.ds(pl.multiple_of(side * depth, depth), depth)
    cat = lambda parts: jnp.concatenate(parts, axis=0)
    x_rows, s_rows = (cat([ref[e, :, cols] for ref in refs[i * n : (i + 1) * n]]) for i in range(2))
    hid = cat([ref[e] for ref in refs[2 * n : 3 * n]])
    ff = hid.shape[1] // 3
    return dot(x_rows, hid[:, : 2 * ff], (0, 0)), dot(hid[:, 2 * ff :], s_rows, (0, 0))


def send_kernel(n, side_ref, *refs):
    out = refs[3 * n]
    for e in range(out.shape[0]):
        gate_up, down = halves_of(n, e, side_ref[0], refs)
        depth = gate_up.shape[0]
        out[e, :depth, :] = gate_up.astype(jnp.bfloat16)
        out[e, depth:, :] = down.astype(jnp.bfloat16)


def keep_kernel(n, side_ref, *refs):
    got, outs = refs[3 * n], refs[3 * n + 1 : 3 * n + 4]
    buffers, sem = refs[3 * n + 4 : 3 * n + 7], refs[3 * n + 7]
    copies = []
    for e in range(got.shape[0]):
        gate_up, down = halves_of(n, e, side_ref[0], refs)
        depth = gate_up.shape[0]
        ff = down.shape[0]
        gate_up = gate_up + got[e, :depth, :].astype(jnp.float32)
        buffers[0][e] = gate_up[:, :ff].astype(jnp.bfloat16)
        buffers[1][e] = gate_up[:, ff:].astype(jnp.bfloat16)
        buffers[2][e] = (down + got[e, depth:, :].astype(jnp.float32)).astype(jnp.bfloat16)
        for i in range(3):
            copy = pltpu.make_async_copy(buffers[i].at[e], outs[i].at[e], sem.at[e, i])
            copy.start()
            copies.append(copy)
    for copy in copies:
        copy.wait()


def weight_call(side, x_rows, s_rows, hids, got=None):
    n = len(x_rows)
    experts, rows, width = x_rows[0].shape
    ff = hids[0].shape[2] // 3
    depth = width // 2
    smem, vmem = (pl.BlockSpec(memory_space=m) for m in (pltpu.SMEM, pltpu.VMEM))
    operands = [*x_rows, *s_rows, *hids]
    scratch = []
    if got is None:
        kernel, out_specs = send_kernel, vmem
        out_shape = pltpu.VMEM((experts, depth + ff, depth), jnp.bfloat16)
    else:
        kernel = keep_kernel
        operands = operands + [got]
        shapes = [(experts, depth, ff), (experts, depth, ff), (experts, ff, depth)]
        out_specs = [pl.BlockSpec(memory_space=pl.ANY)] * 3
        out_shape = [jax.ShapeDtypeStruct(s, jnp.bfloat16) for s in shapes]
        scratch = [pltpu.VMEM(s, jnp.bfloat16) for s in shapes] + [pltpu.SemaphoreType.DMA((experts, 3))]
    return pl.pallas_call(
        functools.partial(kernel, n),
        in_specs=[smem] + [vmem] * len(operands),
        out_specs=out_specs,
        out_shape=out_shape,
        scratch_shapes=scratch,
        compiler_params=pltpu.CompilerParams(vmem_limit_bytes=VMEM_LIMIT),
        cost_estimate=pl.CostEstimate(
            flops=2 * experts * n * rows * 3 * ff * depth,
            bytes_accessed=2 * experts * (n * rows * (width + 3 * ff) + 3 * ff * depth),
            transcendentals=0,
        ),
        name="weight_grads",
    )(side, *[in_vmem(v) for v in operands])


def per_device(tokens, upstream, expert_ids, gate_fixed, slots, w_gate, w_up, w_down):
    local_experts = w_gate.shape[0]
    n_group = lax.axis_size("group")
    n_ingroup = lax.axis_size("ingroup")
    experts_all = local_experts * n_group * n_ingroup
    tok_rows, top_count = expert_ids.shape
    width = tokens.shape[1]
    per_group = top_count // GROUPS_TOK
    capacity = max(2, 3 * tok_rows * top_count // (2 * experts_all))
    rows = -(-n_ingroup * capacity // 16) * 16
    z, x, core = (lax.axis_index(a) for a in ("group", "ingroup", "dp"))
    first_expert = ((z * n_ingroup + x) * local_experts).astype(jnp.int32).reshape(1)
    half = core.astype(jnp.int32).reshape(1)
    wide = lambda v: v.astype(jnp.float32)
    tie = lambda *trees: lax.optimization_barrier(trees)
    order = ring_order(n_group)
    along = lambda k: [(order[i], order[(i + k) % n_group]) for i in range(n_group)]
    shift = lambda s: [(i, (i + s) % n_ingroup) for i in range(n_ingroup)]

    def spread(column):
        return [column] + [lax.ppermute(column, "ingroup", shift(s)) for s in range(1, n_ingroup)]

    def chunk(blocks):
        return chunk_call(*blocks, first_expert, weights, tok_rows, capacity, rows, top_count, per_group)

    def across(others):
        return [
            lax.ppermute(others[(s - 1) * tok_rows : s * tok_rows], "ingroup", shift(-s)) for s in range(1, n_ingroup)
        ]

    def group_sum(part, backs):
        group_part = wide(part)
        for back in backs:
            group_part = group_part + wide(back)
        return group_part.astype(jnp.bfloat16)

    def homeward(group_part, k):
        return lax.ppermute(group_part, "group", along(-k))

    tokens, first_expert, half, other_half = tie(tokens, first_expert, half, 1 - half)
    weights = load_call((w_gate, w_up, w_down))
    first_tokens, upstream = pack_call(tokens, upstream, expert_ids, slots, gate_fixed)
    blocks, chunks, backs, sent = {}, {}, {}, {}
    last = n_group - 1
    for k in range(n_group):
        pair = [spread(tokens) if k < last else [tokens], spread(upstream)]
        if k == last:
            other, *held = tie(chunks[1][1], *blocks[k - 1][0])
            backs[1] = across(other)
            blocks[k - 1][0] = held
            pair[0] += [lax.ppermute(block, "group", along(1)) for block in held[1:]]
        if k == 0:
            pair[0][0] = first_tokens
        if k < last:
            tokens, upstream = (lax.ppermute(v, "group", along(1)) for v in (tokens, upstream))
        if k > 0:
            chunks[k - 1] = chunk(blocks[k - 1])
        if k == last:
            backs[k - 1] = across(chunks[k - 1][1])
            backs[1], chunks = tie(backs[1], chunks)
        upstream, pair[1], chunks, weights = tie(upstream, pair[1], chunks, weights)
        tokens, pair[0] = tie(tokens, pair[0])
        blocks[k] = pair

    for k in range(2, last - 1):
        sent[k] = homeward(group_sum(chunks[k][0], across(chunks[k][1])), k)
    chunks[last] = chunk(blocks[last])
    backs[last] = across(chunks[last][1])
    sent[1] = homeward(group_sum(chunks[1][0], backs[1]), 1)
    chunks, backs[last - 1] = tie(chunks, backs[last - 1])

    carried = homeward(group_sum(chunks[last - 1][0], backs[last - 1]), last)
    kept = [[chunks[k][i] for k in range(n_group)] for i in (-3, -2, -1)]
    to_send = weight_call(other_half, *kept)
    to_send, backs[last], carried, other, sent = tie(to_send, backs[last], carried, chunks[0][1], sent)

    got = lax.ppermute(to_send, "dp", [(0, 1), (1, 0)])
    sent[last] = homeward(group_sum(chunks[last][0], [*backs[last], carried]), last)
    backs[0] = across(other)
    grads = weight_call(half, *kept, got)
    grads, sent, backs[0] = tie(grads, sent, backs[0])
    total = wide(chunks[0][0])
    for back in backs[0]:
        total = total + wide(back)
    for back in sent.values():
        total = total + wide(back)
    return (total.astype(jnp.bfloat16), *grads)


def solution(mesh):
    rows_spec = P(("parts", "group", "ingroup", "dp"), None)
    weight_spec = P(("group", "ingroup"), None, None)
    out_specs = (
        rows_spec,
        P(("parts", "group", "ingroup"), "dp", None),
        P(("parts", "group", "ingroup"), "dp", None),
        P(("parts", "group", "ingroup"), None, "dp"),
    )
    return jax.shard_map(
        per_device,
        mesh=mesh,
        in_specs=(rows_spec,) * 5 + (weight_spec,) * 3,
        out_specs=out_specs,
        check_vma=False,
    )
```

```python
import functools

import jax
import jax.numpy as jnp
from jax import lax
from jax.experimental import pallas as pl
from jax.experimental.pallas import tpu as pltpu
from jax.sharding import PartitionSpec as P

GROUPS_TOK = 4
ROUTE_ROWS = 16
VMEM_LIMIT = 24 * 1024 * 1024


def dot(a, b, contract):
    return lax.dot_general(a, b, ((contract[:1], contract[1:]), ((), ())), preferred_element_type=jnp.float32)


def in_hbm(v):
    return pltpu.with_memory_space_constraint(v, pltpu.HBM)


def in_vmem(v):
    return pltpu.with_memory_space_constraint(v, pltpu.VMEM)


def gated_parts(pre_gate):
    logistic = jax.nn.sigmoid(pre_gate)
    return (pre_gate * logistic, logistic * (1.0 + pre_gate * (1.0 - logistic)))


def ring_order(size):
    return [0] + list(range(1, size, 2)) + list(range(2, size, 2))[::-1]


def pack_kernel(tokens, upstream, expert_ids, slots, gate_fixed, tokens_out, out, sem):
    top_count, tok_rows = expert_ids.shape
    copies = [
        pltpu.make_async_copy(tokens, tokens_out, sem.at[0]),
        pltpu.make_async_copy(upstream, out.at[pl.ds(0, tok_rows), :], sem.at[1]),
    ]
    for copy in copies:
        copy.start()
    gate = gate_fixed[...]
    out[tok_rows:, :] = jnp.zeros((ROUTE_ROWS, out.shape[1]), jnp.bfloat16)
    for i, field in enumerate((expert_ids[...], slots[...], gate >> 8, gate & 255)):
        empty = jnp.zeros((ROUTE_ROWS - top_count, tok_rows), jnp.float32)
        field = jnp.concatenate([field.astype(jnp.float32), empty], axis=0)
        out[tok_rows:, i * tok_rows : (i + 1) * tok_rows] = field.astype(jnp.bfloat16)
    for copy in copies:
        copy.wait()


def pack_call(tokens, upstream, expert_ids, slots, gate_fixed):
    tok_rows, width = tokens.shape
    vmem, hbm = (pl.BlockSpec(memory_space=m) for m in (pltpu.VMEM, pltpu.HBM))
    operands = [in_hbm(v) for v in (tokens, upstream, expert_ids.T, slots.T, gate_fixed.T)]
    return pl.pallas_call(
        pack_kernel,
        in_specs=[hbm] * 2 + [vmem] * 3,
        out_specs=[vmem] * 2,
        out_shape=[pltpu.VMEM((rows, width), jnp.bfloat16) for rows in (tok_rows, tok_rows + ROUTE_ROWS)],
        scratch_shapes=[pltpu.SemaphoreType.DMA((2,))],
        compiler_params=pltpu.CompilerParams(vmem_limit_bytes=VMEM_LIMIT),
        cost_estimate=pl.CostEstimate(flops=0, bytes_accessed=8 * tokens.size, transcendentals=0),
        name="pack",
    )(*operands)


def route_keys(route, first_expert, local_experts, capacity, rows, offset, tok_rows, top_count, per_group):
    field = lambda i: route[:top_count, i * tok_rows : (i + 1) * tok_rows]
    expert = field(0).astype(jnp.int32) - first_expert
    slot = field(1).astype(jnp.int32)
    gate = (field(2) * 256.0 + field(3)) / 65536.0
    valid = (expert >= 0) & (expert < local_experts) & (slot < capacity)
    key = jnp.where(valid, expert * rows + offset + slot, -1)
    gate = jnp.where(valid, gate, 0.0)
    pairs = []
    for i in range(per_group):
        key_out, gate_out = key[i : i + 1, :], gate[i : i + 1, :]
        for j in range(i + per_group, top_count, per_group):
            key_out = jnp.maximum(key_out, key[j : j + 1, :])
            gate_out = jnp.maximum(gate_out, gate[j : j + 1, :])
        pairs.append((key_out, gate_out))
    return pairs


def load_kernel(*refs):
    n = len(refs) // 2
    copies = [pltpu.make_async_copy(refs[i], refs[n + i], refs[-1].at[i]) for i in range(n)]
    for copy in copies:
        copy.start()
    for copy in copies:
        copy.wait()


def load_call(arrays):
    hbm, vmem = (pl.BlockSpec(memory_space=m) for m in (pltpu.HBM, pltpu.VMEM))
    return pl.pallas_call(
        load_kernel,
        in_specs=[hbm] * len(arrays),
        out_specs=[vmem] * len(arrays),
        out_shape=[pltpu.VMEM(v.shape, v.dtype) for v in arrays],
        scratch_shapes=[pltpu.SemaphoreType.DMA((len(arrays),))],
        compiler_params=pltpu.CompilerParams(vmem_limit_bytes=VMEM_LIMIT),
        cost_estimate=pl.CostEstimate(
            flops=0, bytes_accessed=sum(4 * v.size for v in arrays), transcendentals=0
        ),
        name="load",
    )(*[in_hbm(v) for v in arrays])


def chunk_kernel(n_blocks, tok_rows, capacity, rows, top_count, per_group, first_ref, *refs):
    tokens, upstream = refs[:n_blocks], refs[n_blocks : 2 * n_blocks]
    w_gate, w_up, w_down = refs[2 * n_blocks : 2 * n_blocks + 3]
    parts = refs[2 * n_blocks + 3 : -4]
    x_rows, s_rows, hids, back_all = refs[-4:]
    experts, width, ff = w_gate.shape

    pairs = []
    for b in range(n_blocks):
        route = upstream[b][tok_rows : tok_rows + ROUTE_ROWS, :].astype(jnp.float32)
        pairs.append(
            route_keys(route, first_ref[0], experts, capacity, rows, b * capacity, tok_rows, top_count, per_group)
        )
    place = lax.broadcasted_iota(jnp.int32, (experts * rows, n_blocks * tok_rows), 0)
    hot = jnp.zeros(place.shape, jnp.float32)
    gate_hot = jnp.zeros(place.shape, jnp.float32)
    for i in range(per_group):
        key = jnp.concatenate([pair[i][0] for pair in pairs], axis=1)
        gate = jnp.concatenate([pair[i][1] for pair in pairs], axis=1)
        match = place == key
        hot = jnp.where(match, 1.0, hot)
        gate_hot = jnp.where(match, gate, gate_hot)
    hot = hot.astype(jnp.bfloat16)
    row_gate = jnp.sum(gate_hot, axis=1, keepdims=True)

    x_all = jnp.concatenate([block[...] for block in tokens], axis=0)
    gathered = dot(hot, x_all, (1, 0)).astype(jnp.bfloat16)
    for e in range(experts):
        x_rows[e] = gathered[e * rows : (e + 1) * rows, :]
    u_all = jnp.concatenate([block[:tok_rows, :] for block in upstream], axis=0)
    scaled = (dot(hot, u_all, (1, 0)) * row_gate).astype(jnp.bfloat16)
    for e in range(experts):
        s_rows[e] = scaled[e * rows : (e + 1) * rows, :]

    for e in range(experts):
        pre_gate = dot(x_rows[e], w_gate[e], (1, 0))
        pre_up = dot(x_rows[e], w_up[e], (1, 0))
        grad_hidden = dot(s_rows[e], w_down[e], (1, 1))
        active, slope = gated_parts(pre_gate)
        grad_gate_pre = (grad_hidden * pre_up * slope).astype(jnp.bfloat16)
        grad_up_pre = (grad_hidden * active).astype(jnp.bfloat16)
        hids[e, :, :ff] = grad_gate_pre
        hids[e, :, ff : 2 * ff] = grad_up_pre
        hids[e, :, 2 * ff :] = (active * pre_up).astype(jnp.bfloat16)
        back = dot(grad_gate_pre, w_gate[e], (1, 1)) + dot(grad_up_pre, w_up[e], (1, 1))
        back_all[e * rows : (e + 1) * rows, :] = back.astype(jnp.bfloat16)

    summed = dot(hot, back_all[...], (0, 0)).astype(jnp.bfloat16)
    start = 0
    for part in parts:
        part[...] = summed[start : start + part.shape[0], :]
        start += part.shape[0]


def chunk_call(tokens, upstream, first_expert, weights, tok_rows, capacity, rows, top_count, per_group):
    n_blocks = len(tokens)
    n_tok = n_blocks * tok_rows
    experts, width, ff = weights[0].shape
    part_shapes = [(tok_rows, width), (n_tok - tok_rows, width)]
    kept_shapes = [(experts, rows, width), (experts, rows, width), (experts, rows, 3 * ff)]
    smem, vmem = (pl.BlockSpec(memory_space=m) for m in (pltpu.SMEM, pltpu.VMEM))
    out_shapes = part_shapes + kept_shapes
    return pl.pallas_call(
        functools.partial(chunk_kernel, n_blocks, tok_rows, capacity, rows, top_count, per_group),
        in_specs=[smem] + [vmem] * (2 * n_blocks + 3),
        out_specs=[vmem] * len(out_shapes),
        out_shape=[pltpu.VMEM(shape, jnp.bfloat16) for shape in out_shapes],
        scratch_shapes=[pltpu.VMEM((experts * rows, width), jnp.bfloat16)],
        compiler_params=pltpu.CompilerParams(vmem_limit_bytes=VMEM_LIMIT),
        cost_estimate=pl.CostEstimate(
            flops=2 * experts * rows * width * (5 * ff + 3 * n_tok),
            bytes_accessed=6 * experts * width * ff + 8 * n_tok * width,
            transcendentals=0,
        ),
        name="chunk",
    )(first_expert, *[in_vmem(v) for v in (*tokens, *upstream, *weights)])


def halves_of(n, e, side, refs):
    depth = refs[0].shape[2] // 2
    cols = pl.ds(pl.multiple_of(side * depth, depth), depth)
    cat = lambda parts: jnp.concatenate(parts, axis=0)
    x_rows, s_rows = (cat([ref[e, :, cols] for ref in refs[i * n : (i + 1) * n]]) for i in range(2))
    hid = cat([ref[e] for ref in refs[2 * n : 3 * n]])
    ff = hid.shape[1] // 3
    return dot(x_rows, hid[:, : 2 * ff], (0, 0)), dot(hid[:, 2 * ff :], s_rows, (0, 0))


def send_kernel(n, side_ref, *refs):
    out = refs[3 * n]
    for e in range(out.shape[0]):
        gate_up, down = halves_of(n, e, side_ref[0], refs)
        depth = gate_up.shape[0]
        out[e, :depth, :] = gate_up.astype(jnp.bfloat16)
        out[e, depth:, :] = down.astype(jnp.bfloat16)


def keep_kernel(n, side_ref, *refs):
    got, outs = refs[3 * n], refs[3 * n + 1 : 3 * n + 4]
    buffers, sem = refs[3 * n + 4 : 3 * n + 7], refs[3 * n + 7]
    copies = []
    for e in range(got.shape[0]):
        gate_up, down = halves_of(n, e, side_ref[0], refs)
        depth = gate_up.shape[0]
        ff = down.shape[0]
        gate_up = gate_up + got[e, :depth, :].astype(jnp.float32)
        buffers[0][e] = gate_up[:, :ff].astype(jnp.bfloat16)
        buffers[1][e] = gate_up[:, ff:].astype(jnp.bfloat16)
        buffers[2][e] = (down + got[e, depth:, :].astype(jnp.float32)).astype(jnp.bfloat16)
        for i in range(3):
            copy = pltpu.make_async_copy(buffers[i].at[e], outs[i].at[e], sem.at[e, i])
            copy.start()
            copies.append(copy)
    for copy in copies:
        copy.wait()


def weight_call(side, x_rows, s_rows, hids, got=None):
    n = len(x_rows)
    experts, rows, width = x_rows[0].shape
    ff = hids[0].shape[2] // 3
    depth = width // 2
    smem, vmem = (pl.BlockSpec(memory_space=m) for m in (pltpu.SMEM, pltpu.VMEM))
    operands = [*x_rows, *s_rows, *hids]
    scratch = []
    if got is None:
        kernel, out_specs = send_kernel, vmem
        out_shape = pltpu.VMEM((experts, depth + ff, depth), jnp.bfloat16)
    else:
        kernel = keep_kernel
        operands = operands + [got]
        shapes = [(experts, depth, ff), (experts, depth, ff), (experts, ff, depth)]
        out_specs = [pl.BlockSpec(memory_space=pl.ANY)] * 3
        out_shape = [jax.ShapeDtypeStruct(s, jnp.bfloat16) for s in shapes]
        scratch = [pltpu.VMEM(s, jnp.bfloat16) for s in shapes] + [pltpu.SemaphoreType.DMA((experts, 3))]
    return pl.pallas_call(
        functools.partial(kernel, n),
        in_specs=[smem] + [vmem] * len(operands),
        out_specs=out_specs,
        out_shape=out_shape,
        scratch_shapes=scratch,
        compiler_params=pltpu.CompilerParams(vmem_limit_bytes=VMEM_LIMIT),
        cost_estimate=pl.CostEstimate(
            flops=2 * experts * n * rows * 3 * ff * depth,
            bytes_accessed=2 * experts * (n * rows * (width + 3 * ff) + 3 * ff * depth),
            transcendentals=0,
        ),
        name="weight_grads",
    )(side, *[in_vmem(v) for v in operands])


def per_device(tokens, upstream, expert_ids, gate_fixed, slots, w_gate, w_up, w_down):
    local_experts = w_gate.shape[0]
    n_group = lax.axis_size("group")
    n_ingroup = lax.axis_size("ingroup")
    experts_all = local_experts * n_group * n_ingroup
    tok_rows, top_count = expert_ids.shape
    width = tokens.shape[1]
    per_group = top_count // GROUPS_TOK
    capacity = max(2, 3 * tok_rows * top_count // (2 * experts_all))
    rows = -(-n_ingroup * capacity // 16) * 16
    z, x, core = (lax.axis_index(a) for a in ("group", "ingroup", "dp"))
    first_expert = ((z * n_ingroup + x) * local_experts).astype(jnp.int32).reshape(1)
    half = core.astype(jnp.int32).reshape(1)
    wide = lambda v: v.astype(jnp.float32)
    tie = lambda *trees: lax.optimization_barrier(trees)
    order = ring_order(n_group)
    along = lambda k: [(order[i], order[(i + k) % n_group]) for i in range(n_group)]
    shift = lambda s: [(i, (i + s) % n_ingroup) for i in range(n_ingroup)]

    def spread(column):
        return [column] + [lax.ppermute(column, "ingroup", shift(s)) for s in range(1, n_ingroup)]

    def chunk(blocks):
        return chunk_call(*blocks, first_expert, weights, tok_rows, capacity, rows, top_count, per_group)

    def across(others):
        return [
            lax.ppermute(others[(s - 1) * tok_rows : s * tok_rows], "ingroup", shift(-s)) for s in range(1, n_ingroup)
        ]

    def group_sum(part, backs):
        group_part = wide(part)
        for back in backs:
            group_part = group_part + wide(back)
        return group_part.astype(jnp.bfloat16)

    def homeward(group_part, k):
        return lax.ppermute(group_part, "group", along(-k))

    tokens, first_expert, half, other_half = tie(tokens, first_expert, half, 1 - half)
    weights = load_call((w_gate, w_up, w_down))
    first_tokens, upstream = pack_call(tokens, upstream, expert_ids, slots, gate_fixed)
    blocks, chunks, backs, sent = {}, {}, {}, {}
    last = n_group - 1
    for k in range(n_group):
        pair = [spread(tokens) if k < last else [tokens], spread(upstream)]
        if k == last:
            other, *held = tie(chunks[1][1], *blocks[k - 1][0])
            backs[1] = across(other)
            blocks[k - 1][0] = held
            pair[0] += [lax.ppermute(block, "group", along(1)) for block in held[1:]]
        if k == 0:
            pair[0][0] = first_tokens
        if k < last:
            tokens, upstream = (lax.ppermute(v, "group", along(1)) for v in (tokens, upstream))
        if k > 0:
            chunks[k - 1] = chunk(blocks[k - 1])
        if k == last:
            backs[k - 1] = across(chunks[k - 1][1])
        upstream, pair[1], chunks, weights = tie(upstream, pair[1], chunks, weights)
        tokens, pair[0] = tie(tokens, pair[0])
        blocks[k] = pair

    for k in range(2, last - 1):
        sent[k] = homeward(group_sum(chunks[k][0], across(chunks[k][1])), k)
    chunks[last] = chunk(blocks[last])
    backs[last] = across(chunks[last][1])
    chunks, backs[last - 1], backs[1] = tie(chunks, backs[last - 1], backs[1])

    sent[1] = homeward(group_sum(chunks[1][0], backs[1]), 1)
    carried = homeward(group_sum(chunks[last - 1][0], backs[last - 1]), last)
    kept = [[chunks[k][i] for k in range(n_group)] for i in (-3, -2, -1)]
    to_send = weight_call(other_half, *kept)
    to_send, backs[last], other = tie(to_send, backs[last], chunks[0][1])
    to_send, carried, sent = tie(to_send, carried, sent)

    got = lax.ppermute(to_send, "dp", [(0, 1), (1, 0)])
    sent[last] = homeward(group_sum(chunks[last][0], [*backs[last], carried]), last)
    backs[0] = across(other)
    grads = weight_call(half, *kept, got)
    grads, sent, backs[0] = tie(grads, sent, backs[0])
    total = wide(chunks[0][0])
    for back in backs[0]:
        total = total + wide(back)
    for back in sent.values():
        total = total + wide(back)
    return (total.astype(jnp.bfloat16), *grads)


def solution(mesh):
    rows_spec = P(("parts", "group", "ingroup", "dp"), None)
    weight_spec = P(("group", "ingroup"), None, None)
    out_specs = (
        rows_spec,
        P(("parts", "group", "ingroup"), "dp", None),
        P(("parts", "group", "ingroup"), "dp", None),
        P(("parts", "group", "ingroup"), None, "dp"),
    )
    return jax.shard_map(
        per_device,
        mesh=mesh,
        in_specs=(rows_spec,) * 5 + (weight_spec,) * 3,
        out_specs=out_specs,
        check_vma=False,
    )
```

```python
import functools

import jax
import jax.numpy as jnp
from jax import lax
from jax.experimental import pallas as pl
from jax.experimental.pallas import tpu as pltpu
from jax.sharding import PartitionSpec as P

GROUPS_TOK = 4
ROUTE_ROWS = 16
VMEM_LIMIT = 24 * 1024 * 1024


def dot(a, b, contract):
    return lax.dot_general(a, b, ((contract[:1], contract[1:]), ((), ())), preferred_element_type=jnp.float32)


def in_hbm(v):
    return pltpu.with_memory_space_constraint(v, pltpu.HBM)


def in_vmem(v):
    return pltpu.with_memory_space_constraint(v, pltpu.VMEM)


def gated_parts(pre_gate):
    logistic = jax.nn.sigmoid(pre_gate)
    return (pre_gate * logistic, logistic * (1.0 + pre_gate * (1.0 - logistic)))


def ring_order(size):
    return [0] + list(range(1, size, 2)) + list(range(2, size, 2))[::-1]


def pack_kernel(tokens, upstream, expert_ids, slots, gate_fixed, tokens_out, out, sem):
    top_count, tok_rows = expert_ids.shape
    copies = [
        pltpu.make_async_copy(tokens, tokens_out, sem.at[0]),
        pltpu.make_async_copy(upstream, out.at[pl.ds(0, tok_rows), :], sem.at[1]),
    ]
    for copy in copies:
        copy.start()
    gate = gate_fixed[...]
    out[tok_rows:, :] = jnp.zeros((ROUTE_ROWS, out.shape[1]), jnp.bfloat16)
    for i, field in enumerate((expert_ids[...], slots[...], gate >> 8, gate & 255)):
        empty = jnp.zeros((ROUTE_ROWS - top_count, tok_rows), jnp.float32)
        field = jnp.concatenate([field.astype(jnp.float32), empty], axis=0)
        out[tok_rows:, i * tok_rows : (i + 1) * tok_rows] = field.astype(jnp.bfloat16)
    for copy in copies:
        copy.wait()


def pack_call(tokens, upstream, expert_ids, slots, gate_fixed):
    tok_rows, width = tokens.shape
    vmem, hbm = (pl.BlockSpec(memory_space=m) for m in (pltpu.VMEM, pltpu.HBM))
    operands = [in_hbm(v) for v in (tokens, upstream, expert_ids.T, slots.T, gate_fixed.T)]
    return pl.pallas_call(
        pack_kernel,
        in_specs=[hbm] * 2 + [vmem] * 3,
        out_specs=[vmem] * 2,
        out_shape=[pltpu.VMEM((rows, width), jnp.bfloat16) for rows in (tok_rows, tok_rows + ROUTE_ROWS)],
        scratch_shapes=[pltpu.SemaphoreType.DMA((2,))],
        compiler_params=pltpu.CompilerParams(vmem_limit_bytes=VMEM_LIMIT),
        cost_estimate=pl.CostEstimate(flops=0, bytes_accessed=8 * tokens.size, transcendentals=0),
        name="pack",
    )(*operands)


def route_keys(route, first_expert, local_experts, capacity, rows, offset, tok_rows, top_count, per_group):
    field = lambda i: route[:top_count, i * tok_rows : (i + 1) * tok_rows]
    expert = field(0).astype(jnp.int32) - first_expert
    slot = field(1).astype(jnp.int32)
    gate = (field(2) * 256.0 + field(3)) / 65536.0
    valid = (expert >= 0) & (expert < local_experts) & (slot < capacity)
    key = jnp.where(valid, expert * rows + offset + slot, -1)
    gate = jnp.where(valid, gate, 0.0)
    pairs = []
    for i in range(per_group):
        key_out, gate_out = key[i : i + 1, :], gate[i : i + 1, :]
        for j in range(i + per_group, top_count, per_group):
            key_out = jnp.maximum(key_out, key[j : j + 1, :])
            gate_out = jnp.maximum(gate_out, gate[j : j + 1, :])
        pairs.append((key_out, gate_out))
    return pairs


def load_kernel(*refs):
    n = len(refs) // 2
    copies = [pltpu.make_async_copy(refs[i], refs[n + i], refs[-1].at[i]) for i in range(n)]
    for copy in copies:
        copy.start()
    for copy in copies:
        copy.wait()


def load_call(arrays):
    hbm, vmem = (pl.BlockSpec(memory_space=m) for m in (pltpu.HBM, pltpu.VMEM))
    return pl.pallas_call(
        load_kernel,
        in_specs=[hbm] * len(arrays),
        out_specs=[vmem] * len(arrays),
        out_shape=[pltpu.VMEM(v.shape, v.dtype) for v in arrays],
        scratch_shapes=[pltpu.SemaphoreType.DMA((len(arrays),))],
        compiler_params=pltpu.CompilerParams(vmem_limit_bytes=VMEM_LIMIT),
        cost_estimate=pl.CostEstimate(
            flops=0, bytes_accessed=sum(4 * v.size for v in arrays), transcendentals=0
        ),
        name="load",
    )(*[in_hbm(v) for v in arrays])


def chunk_kernel(n_blocks, tok_rows, capacity, rows, top_count, per_group, first_ref, *refs):
    tokens, upstream = refs[:n_blocks], refs[n_blocks : 2 * n_blocks]
    w_gate, w_up, w_down = refs[2 * n_blocks : 2 * n_blocks + 3]
    parts = refs[2 * n_blocks + 3 : -4]
    x_rows, s_rows, hids, back_all = refs[-4:]
    experts, width, ff = w_gate.shape

    pairs = []
    for b in range(n_blocks):
        route = upstream[b][tok_rows : tok_rows + ROUTE_ROWS, :].astype(jnp.float32)
        pairs.append(
            route_keys(route, first_ref[0], experts, capacity, rows, b * capacity, tok_rows, top_count, per_group)
        )
    place = lax.broadcasted_iota(jnp.int32, (experts * rows, n_blocks * tok_rows), 0)
    hot = jnp.zeros(place.shape, jnp.float32)
    gate_hot = jnp.zeros(place.shape, jnp.float32)
    for i in range(per_group):
        key = jnp.concatenate([pair[i][0] for pair in pairs], axis=1)
        gate = jnp.concatenate([pair[i][1] for pair in pairs], axis=1)
        match = place == key
        hot = jnp.where(match, 1.0, hot)
        gate_hot = jnp.where(match, gate, gate_hot)
    hot = hot.astype(jnp.bfloat16)
    row_gate = jnp.sum(gate_hot, axis=1, keepdims=True)

    x_all = jnp.concatenate([block[...] for block in tokens], axis=0)
    gathered = dot(hot, x_all, (1, 0)).astype(jnp.bfloat16)
    for e in range(experts):
        x_rows[e] = gathered[e * rows : (e + 1) * rows, :]
    u_all = jnp.concatenate([block[:tok_rows, :] for block in upstream], axis=0)
    scaled = (dot(hot, u_all, (1, 0)) * row_gate).astype(jnp.bfloat16)
    for e in range(experts):
        s_rows[e] = scaled[e * rows : (e + 1) * rows, :]

    for e in range(experts):
        pre_gate = dot(x_rows[e], w_gate[e], (1, 0))
        pre_up = dot(x_rows[e], w_up[e], (1, 0))
        grad_hidden = dot(s_rows[e], w_down[e], (1, 1))
        active, slope = gated_parts(pre_gate)
        grad_gate_pre = (grad_hidden * pre_up * slope).astype(jnp.bfloat16)
        grad_up_pre = (grad_hidden * active).astype(jnp.bfloat16)
        hids[e, :, :ff] = grad_gate_pre
        hids[e, :, ff : 2 * ff] = grad_up_pre
        hids[e, :, 2 * ff :] = (active * pre_up).astype(jnp.bfloat16)
        back = dot(grad_gate_pre, w_gate[e], (1, 1)) + dot(grad_up_pre, w_up[e], (1, 1))
        back_all[e * rows : (e + 1) * rows, :] = back.astype(jnp.bfloat16)

    summed = dot(hot, back_all[...], (0, 0)).astype(jnp.bfloat16)
    start = 0
    for part in parts:
        part[...] = summed[start : start + part.shape[0], :]
        start += part.shape[0]


def chunk_call(tokens, upstream, first_expert, weights, tok_rows, capacity, rows, top_count, per_group):
    n_blocks = len(tokens)
    n_tok = n_blocks * tok_rows
    experts, width, ff = weights[0].shape
    part_shapes = [(tok_rows, width), (n_tok - tok_rows, width)]
    kept_shapes = [(experts, rows, width), (experts, rows, width), (experts, rows, 3 * ff)]
    smem, vmem = (pl.BlockSpec(memory_space=m) for m in (pltpu.SMEM, pltpu.VMEM))
    out_shapes = part_shapes + kept_shapes
    return pl.pallas_call(
        functools.partial(chunk_kernel, n_blocks, tok_rows, capacity, rows, top_count, per_group),
        in_specs=[smem] + [vmem] * (2 * n_blocks + 3),
        out_specs=[vmem] * len(out_shapes),
        out_shape=[pltpu.VMEM(shape, jnp.bfloat16) for shape in out_shapes],
        scratch_shapes=[pltpu.VMEM((experts * rows, width), jnp.bfloat16)],
        compiler_params=pltpu.CompilerParams(vmem_limit_bytes=VMEM_LIMIT),
        cost_estimate=pl.CostEstimate(
            flops=2 * experts * rows * width * (5 * ff + 3 * n_tok),
            bytes_accessed=6 * experts * width * ff + 8 * n_tok * width,
            transcendentals=0,
        ),
        name="chunk",
    )(first_expert, *[in_vmem(v) for v in (*tokens, *upstream, *weights)])


def halves_of(n, e, side, refs):
    depth = refs[0].shape[2] // 2
    cols = pl.ds(pl.multiple_of(side * depth, depth), depth)
    cat = lambda parts: jnp.concatenate(parts, axis=0)
    x_rows, s_rows = (cat([ref[e, :, cols] for ref in refs[i * n : (i + 1) * n]]) for i in range(2))
    hid = cat([ref[e] for ref in refs[2 * n : 3 * n]])
    ff = hid.shape[1] // 3
    return dot(x_rows, hid[:, : 2 * ff], (0, 0)), dot(hid[:, 2 * ff :], s_rows, (0, 0))


def send_kernel(n, side_ref, *refs):
    out = refs[3 * n]
    for e in range(out.shape[0]):
        gate_up, down = halves_of(n, e, side_ref[0], refs)
        depth = gate_up.shape[0]
        out[e, :depth, :] = gate_up.astype(jnp.bfloat16)
        out[e, depth:, :] = down.astype(jnp.bfloat16)


def keep_kernel(n, side_ref, *refs):
    got, outs = refs[3 * n], refs[3 * n + 1 : 3 * n + 4]
    buffers, sem = refs[3 * n + 4 : 3 * n + 7], refs[3 * n + 7]
    copies = []
    for e in range(got.shape[0]):
        gate_up, down = halves_of(n, e, side_ref[0], refs)
        depth = gate_up.shape[0]
        ff = down.shape[0]
        gate_up = gate_up + got[e, :depth, :].astype(jnp.float32)
        buffers[0][e] = gate_up[:, :ff].astype(jnp.bfloat16)
        buffers[1][e] = gate_up[:, ff:].astype(jnp.bfloat16)
        buffers[2][e] = (down + got[e, depth:, :].astype(jnp.float32)).astype(jnp.bfloat16)
        for i in range(3):
            copy = pltpu.make_async_copy(buffers[i].at[e], outs[i].at[e], sem.at[e, i])
            copy.start()
            copies.append(copy)
    for copy in copies:
        copy.wait()


def weight_call(side, x_rows, s_rows, hids, got=None):
    n = len(x_rows)
    experts, rows, width = x_rows[0].shape
    ff = hids[0].shape[2] // 3
    depth = width // 2
    smem, vmem = (pl.BlockSpec(memory_space=m) for m in (pltpu.SMEM, pltpu.VMEM))
    operands = [*x_rows, *s_rows, *hids]
    scratch = []
    if got is None:
        kernel, out_specs = send_kernel, vmem
        out_shape = pltpu.VMEM((experts, depth + ff, depth), jnp.bfloat16)
    else:
        kernel = keep_kernel
        operands = operands + [got]
        shapes = [(experts, depth, ff), (experts, depth, ff), (experts, ff, depth)]
        out_specs = [pl.BlockSpec(memory_space=pl.ANY)] * 3
        out_shape = [jax.ShapeDtypeStruct(s, jnp.bfloat16) for s in shapes]
        scratch = [pltpu.VMEM(s, jnp.bfloat16) for s in shapes] + [pltpu.SemaphoreType.DMA((experts, 3))]
    return pl.pallas_call(
        functools.partial(kernel, n),
        in_specs=[smem] + [vmem] * len(operands),
        out_specs=out_specs,
        out_shape=out_shape,
        scratch_shapes=scratch,
        compiler_params=pltpu.CompilerParams(vmem_limit_bytes=VMEM_LIMIT),
        cost_estimate=pl.CostEstimate(
            flops=2 * experts * n * rows * 3 * ff * depth,
            bytes_accessed=2 * experts * (n * rows * (width + 3 * ff) + 3 * ff * depth),
            transcendentals=0,
        ),
        name="weight_grads",
    )(side, *[in_vmem(v) for v in operands])


def per_device(tokens, upstream, expert_ids, gate_fixed, slots, w_gate, w_up, w_down):
    local_experts = w_gate.shape[0]
    n_group = lax.axis_size("group")
    n_ingroup = lax.axis_size("ingroup")
    experts_all = local_experts * n_group * n_ingroup
    tok_rows, top_count = expert_ids.shape
    width = tokens.shape[1]
    per_group = top_count // GROUPS_TOK
    capacity = max(2, 3 * tok_rows * top_count // (2 * experts_all))
    rows = -(-n_ingroup * capacity // 16) * 16
    z, x, core = (lax.axis_index(a) for a in ("group", "ingroup", "dp"))
    first_expert = ((z * n_ingroup + x) * local_experts).astype(jnp.int32).reshape(1)
    half = core.astype(jnp.int32).reshape(1)
    wide = lambda v: v.astype(jnp.float32)
    tie = lambda *trees: lax.optimization_barrier(trees)
    order = ring_order(n_group)
    along = lambda k: [(order[i], order[(i + k) % n_group]) for i in range(n_group)]
    shift = lambda s: [(i, (i + s) % n_ingroup) for i in range(n_ingroup)]

    def spread(column):
        return [column] + [lax.ppermute(column, "ingroup", shift(s)) for s in range(1, n_ingroup)]

    def chunk(blocks):
        return chunk_call(*blocks, first_expert, weights, tok_rows, capacity, rows, top_count, per_group)

    def across(others):
        return [
            lax.ppermute(others[(s - 1) * tok_rows : s * tok_rows], "ingroup", shift(-s)) for s in range(1, n_ingroup)
        ]

    def group_sum(part, backs):
        group_part = wide(part)
        for back in backs:
            group_part = group_part + wide(back)
        return group_part.astype(jnp.bfloat16)

    def homeward(group_part, k):
        return lax.ppermute(group_part, "group", along(-k))

    tokens, first_expert, half, other_half = tie(tokens, first_expert, half, 1 - half)
    weights = load_call((w_gate, w_up, w_down))
    first_tokens, upstream = pack_call(tokens, upstream, expert_ids, slots, gate_fixed)
    blocks, chunks, backs, sent = {}, {}, {}, {}
    last = n_group - 1
    for k in range(n_group):
        pair = [spread(tokens) if k < last else [tokens], spread(upstream)]
        if k == last:
            other, *held = tie(chunks[1][1], *blocks[k - 1][0])
            backs[1] = across(other)
            blocks[k - 1][0] = held
            pair[0] += [lax.ppermute(block, "group", along(1)) for block in held[1:]]
        if k == 0:
            pair[0][0] = first_tokens
        if k < last:
            tokens, upstream = (lax.ppermute(v, "group", along(1)) for v in (tokens, upstream))
        if k > 0:
            chunks[k - 1] = chunk(blocks[k - 1])
        if k == last:
            backs[k - 1] = across(chunks[k - 1][1])
        upstream, pair[1], chunks, weights = tie(upstream, pair[1], chunks, weights)
        tokens, pair[0] = tie(tokens, pair[0])
        blocks[k] = pair

    for k in range(2, last - 1):
        sent[k] = homeward(group_sum(chunks[k][0], across(chunks[k][1])), k)
    chunks[last] = chunk(blocks[last])
    backs[last] = across(chunks[last][1])
    chunks, backs[1] = tie(chunks, backs[1])

    sent[1] = homeward(group_sum(chunks[1][0], backs[1]), 1)
    carried = homeward(group_sum(chunks[last - 1][0], backs[last - 1]), last)
    kept = [[chunks[k][i] for k in range(n_group)] for i in (-3, -2, -1)]
    kept, backs[last - 1], sent = tie(kept, backs[last - 1], sent)
    to_send = weight_call(other_half, *kept)
    to_send, backs[last], other = tie(to_send, backs[last], chunks[0][1])
    to_send, carried = tie(to_send, carried)

    got = lax.ppermute(to_send, "dp", [(0, 1), (1, 0)])
    sent[last] = homeward(group_sum(chunks[last][0], [*backs[last], carried]), last)
    backs[0] = across(other)
    grads = weight_call(half, *kept, got)
    grads, sent, backs[0] = tie(grads, sent, backs[0])
    total = wide(chunks[0][0])
    for back in backs[0]:
        total = total + wide(back)
    for back in sent.values():
        total = total + wide(back)
    return (total.astype(jnp.bfloat16), *grads)


def solution(mesh):
    rows_spec = P(("parts", "group", "ingroup", "dp"), None)
    weight_spec = P(("group", "ingroup"), None, None)
    out_specs = (
        rows_spec,
        P(("parts", "group", "ingroup"), "dp", None),
        P(("parts", "group", "ingroup"), "dp", None),
        P(("parts", "group", "ingroup"), None, "dp"),
    )
    return jax.shard_map(
        per_device,
        mesh=mesh,
        in_specs=(rows_spec,) * 5 + (weight_spec,) * 3,
        out_specs=out_specs,
        check_vma=False,
    )
```

```python
import functools

import jax
import jax.numpy as jnp
from jax import lax
from jax.experimental import pallas as pl
from jax.experimental.pallas import tpu as pltpu
from jax.sharding import PartitionSpec as P

GROUPS_TOK = 4
ROUTE_ROWS = 16
VMEM_LIMIT = 24 * 1024 * 1024


def dot(a, b, contract):
    return lax.dot_general(a, b, ((contract[:1], contract[1:]), ((), ())), preferred_element_type=jnp.float32)


def in_hbm(v):
    return pltpu.with_memory_space_constraint(v, pltpu.HBM)


def in_vmem(v):
    return pltpu.with_memory_space_constraint(v, pltpu.VMEM)


def gated_parts(pre_gate):
    logistic = jax.nn.sigmoid(pre_gate)
    return (pre_gate * logistic, logistic * (1.0 + pre_gate * (1.0 - logistic)))


def ring_order(size):
    return [0] + list(range(1, size, 2)) + list(range(2, size, 2))[::-1]


def pack_kernel(tokens, upstream, expert_ids, slots, gate_fixed, tokens_out, out, sem):
    top_count, tok_rows = expert_ids.shape
    copies = [
        pltpu.make_async_copy(tokens, tokens_out, sem.at[0]),
        pltpu.make_async_copy(upstream, out.at[pl.ds(0, tok_rows), :], sem.at[1]),
    ]
    for copy in copies:
        copy.start()
    gate = gate_fixed[...]
    out[tok_rows:, :] = jnp.zeros((ROUTE_ROWS, out.shape[1]), jnp.bfloat16)
    for i, field in enumerate((expert_ids[...], slots[...], gate >> 8, gate & 255)):
        empty = jnp.zeros((ROUTE_ROWS - top_count, tok_rows), jnp.float32)
        field = jnp.concatenate([field.astype(jnp.float32), empty], axis=0)
        out[tok_rows:, i * tok_rows : (i + 1) * tok_rows] = field.astype(jnp.bfloat16)
    for copy in copies:
        copy.wait()


def pack_call(tokens, upstream, expert_ids, slots, gate_fixed):
    tok_rows, width = tokens.shape
    vmem, hbm = (pl.BlockSpec(memory_space=m) for m in (pltpu.VMEM, pltpu.HBM))
    operands = [in_hbm(v) for v in (tokens, upstream, expert_ids.T, slots.T, gate_fixed.T)]
    return pl.pallas_call(
        pack_kernel,
        in_specs=[hbm] * 2 + [vmem] * 3,
        out_specs=[vmem] * 2,
        out_shape=[pltpu.VMEM((rows, width), jnp.bfloat16) for rows in (tok_rows, tok_rows + ROUTE_ROWS)],
        scratch_shapes=[pltpu.SemaphoreType.DMA((2,))],
        compiler_params=pltpu.CompilerParams(vmem_limit_bytes=VMEM_LIMIT),
        cost_estimate=pl.CostEstimate(flops=0, bytes_accessed=8 * tokens.size, transcendentals=0),
        name="pack",
    )(*operands)


def route_keys(route, first_expert, local_experts, capacity, rows, offset, tok_rows, top_count, per_group):
    field = lambda i: route[:top_count, i * tok_rows : (i + 1) * tok_rows]
    expert = field(0).astype(jnp.int32) - first_expert
    slot = field(1).astype(jnp.int32)
    gate = (field(2) * 256.0 + field(3)) / 65536.0
    valid = (expert >= 0) & (expert < local_experts) & (slot < capacity)
    key = jnp.where(valid, expert * rows + offset + slot, -1)
    gate = jnp.where(valid, gate, 0.0)
    pairs = []
    for i in range(per_group):
        key_out, gate_out = key[i : i + 1, :], gate[i : i + 1, :]
        for j in range(i + per_group, top_count, per_group):
            key_out = jnp.maximum(key_out, key[j : j + 1, :])
            gate_out = jnp.maximum(gate_out, gate[j : j + 1, :])
        pairs.append((key_out, gate_out))
    return pairs


def load_kernel(*refs):
    n = len(refs) // 2
    copies = [pltpu.make_async_copy(refs[i], refs[n + i], refs[-1].at[i]) for i in range(n)]
    for copy in copies:
        copy.start()
    for copy in copies:
        copy.wait()


def load_call(arrays):
    hbm, vmem = (pl.BlockSpec(memory_space=m) for m in (pltpu.HBM, pltpu.VMEM))
    return pl.pallas_call(
        load_kernel,
        in_specs=[hbm] * len(arrays),
        out_specs=[vmem] * len(arrays),
        out_shape=[pltpu.VMEM(v.shape, v.dtype) for v in arrays],
        scratch_shapes=[pltpu.SemaphoreType.DMA((len(arrays),))],
        compiler_params=pltpu.CompilerParams(vmem_limit_bytes=VMEM_LIMIT),
        cost_estimate=pl.CostEstimate(
            flops=0, bytes_accessed=sum(4 * v.size for v in arrays), transcendentals=0
        ),
        name="load",
    )(*[in_hbm(v) for v in arrays])


def chunk_kernel(n_blocks, tok_rows, capacity, rows, top_count, per_group, first_ref, *refs):
    tokens, upstream = refs[:n_blocks], refs[n_blocks : 2 * n_blocks]
    w_gate, w_up, w_down = refs[2 * n_blocks : 2 * n_blocks + 3]
    parts = refs[2 * n_blocks + 3 : -4]
    x_rows, s_rows, hids, back_all = refs[-4:]
    experts, width, ff = w_gate.shape

    pairs = []
    for b in range(n_blocks):
        route = upstream[b][tok_rows : tok_rows + ROUTE_ROWS, :].astype(jnp.float32)
        pairs.append(
            route_keys(route, first_ref[0], experts, capacity, rows, b * capacity, tok_rows, top_count, per_group)
        )
    place = lax.broadcasted_iota(jnp.int32, (experts * rows, n_blocks * tok_rows), 0)
    hot = jnp.zeros(place.shape, jnp.float32)
    gate_hot = jnp.zeros(place.shape, jnp.float32)
    for i in range(per_group):
        key = jnp.concatenate([pair[i][0] for pair in pairs], axis=1)
        gate = jnp.concatenate([pair[i][1] for pair in pairs], axis=1)
        match = place == key
        hot = jnp.where(match, 1.0, hot)
        gate_hot = jnp.where(match, gate, gate_hot)
    hot = hot.astype(jnp.bfloat16)
    row_gate = jnp.sum(gate_hot, axis=1, keepdims=True)

    x_all = jnp.concatenate([block[...] for block in tokens], axis=0)
    gathered = dot(hot, x_all, (1, 0)).astype(jnp.bfloat16)
    for e in range(experts):
        x_rows[e] = gathered[e * rows : (e + 1) * rows, :]
    u_all = jnp.concatenate([block[:tok_rows, :] for block in upstream], axis=0)
    scaled = (dot(hot, u_all, (1, 0)) * row_gate).astype(jnp.bfloat16)
    for e in range(experts):
        s_rows[e] = scaled[e * rows : (e + 1) * rows, :]

    for e in range(experts):
        pre_gate = dot(x_rows[e], w_gate[e], (1, 0))
        pre_up = dot(x_rows[e], w_up[e], (1, 0))
        grad_hidden = dot(s_rows[e], w_down[e], (1, 1))
        active, slope = gated_parts(pre_gate)
        grad_gate_pre = (grad_hidden * pre_up * slope).astype(jnp.bfloat16)
        grad_up_pre = (grad_hidden * active).astype(jnp.bfloat16)
        hids[e, :, :ff] = grad_gate_pre
        hids[e, :, ff : 2 * ff] = grad_up_pre
        hids[e, :, 2 * ff :] = (active * pre_up).astype(jnp.bfloat16)
        back = dot(grad_gate_pre, w_gate[e], (1, 1)) + dot(grad_up_pre, w_up[e], (1, 1))
        back_all[e * rows : (e + 1) * rows, :] = back.astype(jnp.bfloat16)

    summed = dot(hot, back_all[...], (0, 0)).astype(jnp.bfloat16)
    start = 0
    for part in parts:
        part[...] = summed[start : start + part.shape[0], :]
        start += part.shape[0]


def chunk_call(tokens, upstream, first_expert, weights, tok_rows, capacity, rows, top_count, per_group):
    n_blocks = len(tokens)
    n_tok = n_blocks * tok_rows
    experts, width, ff = weights[0].shape
    part_shapes = [(tok_rows, width), (n_tok - tok_rows, width)]
    kept_shapes = [(experts, rows, width), (experts, rows, width), (experts, rows, 3 * ff)]
    smem, vmem = (pl.BlockSpec(memory_space=m) for m in (pltpu.SMEM, pltpu.VMEM))
    out_shapes = part_shapes + kept_shapes
    return pl.pallas_call(
        functools.partial(chunk_kernel, n_blocks, tok_rows, capacity, rows, top_count, per_group),
        in_specs=[smem] + [vmem] * (2 * n_blocks + 3),
        out_specs=[vmem] * len(out_shapes),
        out_shape=[pltpu.VMEM(shape, jnp.bfloat16) for shape in out_shapes],
        scratch_shapes=[pltpu.VMEM((experts * rows, width), jnp.bfloat16)],
        compiler_params=pltpu.CompilerParams(vmem_limit_bytes=VMEM_LIMIT),
        cost_estimate=pl.CostEstimate(
            flops=2 * experts * rows * width * (5 * ff + 3 * n_tok),
            bytes_accessed=6 * experts * width * ff + 8 * n_tok * width,
            transcendentals=0,
        ),
        name="chunk",
    )(first_expert, *[in_vmem(v) for v in (*tokens, *upstream, *weights)])


def halves_of(n, e, side, refs):
    depth = refs[0].shape[2] // 2
    cols = pl.ds(pl.multiple_of(side * depth, depth), depth)
    cat = lambda parts: jnp.concatenate(parts, axis=0)
    x_rows, s_rows = (cat([ref[e, :, cols] for ref in refs[i * n : (i + 1) * n]]) for i in range(2))
    hid = cat([ref[e] for ref in refs[2 * n : 3 * n]])
    ff = hid.shape[1] // 3
    return dot(x_rows, hid[:, : 2 * ff], (0, 0)), dot(hid[:, 2 * ff :], s_rows, (0, 0))


def send_kernel(n, side_ref, *refs):
    out = refs[3 * n]
    for e in range(out.shape[0]):
        gate_up, down = halves_of(n, e, side_ref[0], refs)
        depth = gate_up.shape[0]
        out[e, :depth, :] = gate_up.astype(jnp.bfloat16)
        out[e, depth:, :] = down.astype(jnp.bfloat16)


def keep_kernel(n, side_ref, *refs):
    got, outs = refs[3 * n], refs[3 * n + 2 : 3 * n + 5]
    buffers, sem = refs[3 * n + 5 : 3 * n + 8], refs[3 * n + 8]
    copies = []
    for e in range(got.shape[0]):
        gate_up, down = halves_of(n, e, side_ref[0], refs)
        depth = gate_up.shape[0]
        ff = down.shape[0]
        gate_up = gate_up + got[e, :depth, :].astype(jnp.float32)
        buffers[0][e] = gate_up[:, :ff].astype(jnp.bfloat16)
        buffers[1][e] = gate_up[:, ff:].astype(jnp.bfloat16)
        buffers[2][e] = (down + got[e, depth:, :].astype(jnp.float32)).astype(jnp.bfloat16)
        for i in range(3):
            copy = pltpu.make_async_copy(buffers[i].at[e], outs[i].at[e], sem.at[e, i])
            copy.start()
            copies.append(copy)
    for copy in copies:
        copy.wait()


def weight_call(side, x_rows, s_rows, hids, got=None, pace=None):
    n = len(x_rows)
    experts, rows, width = x_rows[0].shape
    ff = hids[0].shape[2] // 3
    depth = width // 2
    smem, vmem = (pl.BlockSpec(memory_space=m) for m in (pltpu.SMEM, pltpu.VMEM))
    operands = [*x_rows, *s_rows, *hids]
    scratch = []
    if got is None:
        kernel, out_specs = send_kernel, vmem
        out_shape = pltpu.VMEM((experts, depth + ff, depth), jnp.bfloat16)
    else:
        kernel = keep_kernel
        operands = operands + [got, pace]
        shapes = [(experts, depth, ff), (experts, depth, ff), (experts, ff, depth)]
        out_specs = [pl.BlockSpec(memory_space=pl.ANY)] * 3
        out_shape = [jax.ShapeDtypeStruct(s, jnp.bfloat16) for s in shapes]
        scratch = [pltpu.VMEM(s, jnp.bfloat16) for s in shapes] + [pltpu.SemaphoreType.DMA((experts, 3))]
    return pl.pallas_call(
        functools.partial(kernel, n),
        in_specs=[smem] + [vmem] * len(operands),
        out_specs=out_specs,
        out_shape=out_shape,
        scratch_shapes=scratch,
        compiler_params=pltpu.CompilerParams(vmem_limit_bytes=VMEM_LIMIT),
        cost_estimate=pl.CostEstimate(
            flops=2 * experts * n * rows * 3 * ff * depth,
            bytes_accessed=2 * experts * (n * rows * (width + 3 * ff) + 3 * ff * depth),
            transcendentals=0,
        ),
        name="weight_grads",
    )(side, *[in_vmem(v) for v in operands])


def per_device(tokens, upstream, expert_ids, gate_fixed, slots, w_gate, w_up, w_down):
    local_experts = w_gate.shape[0]
    n_group = lax.axis_size("group")
    n_ingroup = lax.axis_size("ingroup")
    experts_all = local_experts * n_group * n_ingroup
    tok_rows, top_count = expert_ids.shape
    width = tokens.shape[1]
    per_group = top_count // GROUPS_TOK
    capacity = max(2, 3 * tok_rows * top_count // (2 * experts_all))
    rows = -(-n_ingroup * capacity // 16) * 16
    z, x, core = (lax.axis_index(a) for a in ("group", "ingroup", "dp"))
    first_expert = ((z * n_ingroup + x) * local_experts).astype(jnp.int32).reshape(1)
    half = core.astype(jnp.int32).reshape(1)
    wide = lambda v: v.astype(jnp.float32)
    tie = lambda *trees: lax.optimization_barrier(trees)
    order = ring_order(n_group)
    along = lambda k: [(order[i], order[(i + k) % n_group]) for i in range(n_group)]
    shift = lambda s: [(i, (i + s) % n_ingroup) for i in range(n_ingroup)]

    def spread(column):
        return [column] + [lax.ppermute(column, "ingroup", shift(s)) for s in range(1, n_ingroup)]

    def chunk(blocks):
        return chunk_call(*blocks, first_expert, weights, tok_rows, capacity, rows, top_count, per_group)

    def across(others):
        return [
            lax.ppermute(others[(s - 1) * tok_rows : s * tok_rows], "ingroup", shift(-s)) for s in range(1, n_ingroup)
        ]

    def group_sum(part, backs):
        group_part = wide(part)
        for back in backs:
            group_part = group_part + wide(back)
        return group_part.astype(jnp.bfloat16)

    def homeward(group_part, k):
        return lax.ppermute(group_part, "group", along(-k))

    tokens, first_expert, half, other_half = tie(tokens, first_expert, half, 1 - half)
    weights = load_call((w_gate, w_up, w_down))
    first_tokens, upstream = pack_call(tokens, upstream, expert_ids, slots, gate_fixed)
    pace = lax.slice(upstream, (tok_rows, 0), (tok_rows + 8, 128))
    blocks, chunks, backs, sent = {}, {}, {}, {}
    last = n_group - 1
    for k in range(n_group):
        pair = [spread(tokens) if k < last else [tokens], spread(upstream)]
        if k == last:
            other, *held = tie(chunks[1][1], *blocks[k - 1][0])
            backs[1] = across(other)
            blocks[k - 1][0] = held
            pair[0] += [lax.ppermute(block, "group", along(1)) for block in held[1:]]
        if k == 0:
            pair[0][0] = first_tokens
        if k < last:
            tokens, upstream = (lax.ppermute(v, "group", along(1)) for v in (tokens, upstream))
        if k > 0:
            chunks[k - 1] = chunk(blocks[k - 1])
        if k == last:
            backs[k - 1] = across(chunks[k - 1][1])
        if k > 0:
            pace = lax.ppermute(pace, "dp", [(0, 1), (1, 0)])
        upstream, pair[1], chunks, weights, pace = tie(upstream, pair[1], chunks, weights, pace)
        tokens, pair[0] = tie(tokens, pair[0])
        blocks[k] = pair

    for k in range(2, last - 1):
        sent[k] = homeward(group_sum(chunks[k][0], across(chunks[k][1])), k)
    chunks[last] = chunk(blocks[last])
    backs[last] = across(chunks[last][1])
    chunks, backs[1] = tie(chunks, backs[1])

    sent[1] = homeward(group_sum(chunks[1][0], backs[1]), 1)
    carried = homeward(group_sum(chunks[last - 1][0], backs[last - 1]), last)
    kept = [[chunks[k][i] for k in range(n_group)] for i in (-3, -2, -1)]
    kept, backs[last - 1], sent = tie(kept, backs[last - 1], sent)
    to_send = weight_call(other_half, *kept)
    to_send, backs[last], other = tie(to_send, backs[last], chunks[0][1])
    to_send, carried = tie(to_send, carried)

    got = lax.ppermute(to_send, "dp", [(0, 1), (1, 0)])
    sent[last] = homeward(group_sum(chunks[last][0], [*backs[last], carried]), last)
    backs[0] = across(other)
    grads = weight_call(half, *kept, got, pace)
    grads, sent, backs[0] = tie(grads, sent, backs[0])
    total = wide(chunks[0][0])
    for back in backs[0]:
        total = total + wide(back)
    for back in sent.values():
        total = total + wide(back)
    return (total.astype(jnp.bfloat16), *grads)


def solution(mesh):
    rows_spec = P(("parts", "group", "ingroup", "dp"), None)
    weight_spec = P(("group", "ingroup"), None, None)
    out_specs = (
        rows_spec,
        P(("parts", "group", "ingroup"), "dp", None),
        P(("parts", "group", "ingroup"), "dp", None),
        P(("parts", "group", "ingroup"), None, "dp"),
    )
    return jax.shard_map(
        per_device,
        mesh=mesh,
        in_specs=(rows_spec,) * 5 + (weight_spec,) * 3,
        out_specs=out_specs,
        check_vma=False,
    )
```

```python
import functools

import jax
import jax.numpy as jnp
from jax import lax
from jax.experimental import pallas as pl
from jax.experimental.pallas import tpu as pltpu
from jax.sharding import PartitionSpec as P

GROUPS_TOK = 4
ROUTE_ROWS = 16
VMEM_LIMIT = 24 * 1024 * 1024


def dot(a, b, contract):
    return lax.dot_general(a, b, ((contract[:1], contract[1:]), ((), ())), preferred_element_type=jnp.float32)


def in_hbm(v):
    return pltpu.with_memory_space_constraint(v, pltpu.HBM)


def in_vmem(v):
    return pltpu.with_memory_space_constraint(v, pltpu.VMEM)


def gated_parts(pre_gate):
    logistic = jax.nn.sigmoid(pre_gate)
    return (pre_gate * logistic, logistic * (1.0 + pre_gate * (1.0 - logistic)))


def ring_order(size):
    return [0] + list(range(1, size, 2)) + list(range(2, size, 2))[::-1]


def pack_kernel(tokens, upstream, expert_ids, slots, gate_fixed, tokens_out, out, sem):
    top_count, tok_rows = expert_ids.shape
    copies = [
        pltpu.make_async_copy(tokens, tokens_out, sem.at[0]),
        pltpu.make_async_copy(upstream, out.at[pl.ds(0, tok_rows), :], sem.at[1]),
    ]
    for copy in copies:
        copy.start()
    gate = gate_fixed[...]
    out[tok_rows:, :] = jnp.zeros((ROUTE_ROWS, out.shape[1]), jnp.bfloat16)
    for i, field in enumerate((expert_ids[...], slots[...], gate >> 8, gate & 255)):
        empty = jnp.zeros((ROUTE_ROWS - top_count, tok_rows), jnp.float32)
        field = jnp.concatenate([field.astype(jnp.float32), empty], axis=0)
        out[tok_rows:, i * tok_rows : (i + 1) * tok_rows] = field.astype(jnp.bfloat16)
    for copy in copies:
        copy.wait()


def pack_call(tokens, upstream, expert_ids, slots, gate_fixed):
    tok_rows, width = tokens.shape
    vmem, hbm = (pl.BlockSpec(memory_space=m) for m in (pltpu.VMEM, pltpu.HBM))
    operands = [in_hbm(v) for v in (tokens, upstream, expert_ids.T, slots.T, gate_fixed.T)]
    return pl.pallas_call(
        pack_kernel,
        in_specs=[hbm] * 2 + [vmem] * 3,
        out_specs=[vmem] * 2,
        out_shape=[pltpu.VMEM((rows, width), jnp.bfloat16) for rows in (tok_rows, tok_rows + ROUTE_ROWS)],
        scratch_shapes=[pltpu.SemaphoreType.DMA((2,))],
        compiler_params=pltpu.CompilerParams(vmem_limit_bytes=VMEM_LIMIT),
        name="pack",
    )(*operands)


def route_keys(route, first_expert, local_experts, capacity, rows, offset, tok_rows, top_count, per_group):
    field = lambda i: route[:top_count, i * tok_rows : (i + 1) * tok_rows]
    expert = field(0).astype(jnp.int32) - first_expert
    slot = field(1).astype(jnp.int32)
    gate = (field(2) * 256.0 + field(3)) / 65536.0
    valid = (expert >= 0) & (expert < local_experts) & (slot < capacity)
    key = jnp.where(valid, expert * rows + offset + slot, -1)
    gate = jnp.where(valid, gate, 0.0)
    pairs = []
    for i in range(per_group):
        key_out, gate_out = key[i : i + 1, :], gate[i : i + 1, :]
        for j in range(i + per_group, top_count, per_group):
            key_out = jnp.maximum(key_out, key[j : j + 1, :])
            gate_out = jnp.maximum(gate_out, gate[j : j + 1, :])
        pairs.append((key_out, gate_out))
    return pairs


def load_kernel(*refs):
    n = len(refs) // 2
    copies = [pltpu.make_async_copy(refs[i], refs[n + i], refs[-1].at[i]) for i in range(n)]
    for copy in copies:
        copy.start()
    for copy in copies:
        copy.wait()


def load_call(arrays):
    hbm, vmem = (pl.BlockSpec(memory_space=m) for m in (pltpu.HBM, pltpu.VMEM))
    return pl.pallas_call(
        load_kernel,
        in_specs=[hbm] * len(arrays),
        out_specs=[vmem] * len(arrays),
        out_shape=[pltpu.VMEM(v.shape, v.dtype) for v in arrays],
        scratch_shapes=[pltpu.SemaphoreType.DMA((len(arrays),))],
        compiler_params=pltpu.CompilerParams(vmem_limit_bytes=VMEM_LIMIT),
        name="load",
    )(*[in_hbm(v) for v in arrays])


def chunk_kernel(n_blocks, tok_rows, capacity, rows, top_count, per_group, first_ref, *refs):
    tokens, upstream = refs[:n_blocks], refs[n_blocks : 2 * n_blocks]
    w_gate, w_up, w_down = refs[2 * n_blocks : 2 * n_blocks + 3]
    parts = refs[2 * n_blocks + 3 : -4]
    x_rows, s_rows, hids, back_all = refs[-4:]
    experts, width, ff = w_gate.shape

    pairs = []
    for b in range(n_blocks):
        route = upstream[b][tok_rows : tok_rows + ROUTE_ROWS, :].astype(jnp.float32)
        pairs.append(
            route_keys(route, first_ref[0], experts, capacity, rows, b * capacity, tok_rows, top_count, per_group)
        )
    place = lax.broadcasted_iota(jnp.int32, (experts * rows, n_blocks * tok_rows), 0)
    hot = jnp.zeros(place.shape, jnp.float32)
    gate_hot = jnp.zeros(place.shape, jnp.float32)
    for i in range(per_group):
        key = jnp.concatenate([pair[i][0] for pair in pairs], axis=1)
        gate = jnp.concatenate([pair[i][1] for pair in pairs], axis=1)
        match = place == key
        hot = jnp.where(match, 1.0, hot)
        gate_hot = jnp.where(match, gate, gate_hot)
    hot = hot.astype(jnp.bfloat16)
    row_gate = jnp.sum(gate_hot, axis=1, keepdims=True)

    x_all = jnp.concatenate([block[...] for block in tokens], axis=0)
    gathered = dot(hot, x_all, (1, 0)).astype(jnp.bfloat16)
    for e in range(experts):
        x_rows[e] = gathered[e * rows : (e + 1) * rows, :]
    u_all = jnp.concatenate([block[:tok_rows, :] for block in upstream], axis=0)
    scaled = (dot(hot, u_all, (1, 0)) * row_gate).astype(jnp.bfloat16)
    for e in range(experts):
        s_rows[e] = scaled[e * rows : (e + 1) * rows, :]

    for e in range(experts):
        pre_gate = dot(x_rows[e], w_gate[e], (1, 0))
        pre_up = dot(x_rows[e], w_up[e], (1, 0))
        grad_hidden = dot(s_rows[e], w_down[e], (1, 1))
        active, slope = gated_parts(pre_gate)
        grad_gate_pre = (grad_hidden * pre_up * slope).astype(jnp.bfloat16)
        grad_up_pre = (grad_hidden * active).astype(jnp.bfloat16)
        hids[e, :, :ff] = grad_gate_pre
        hids[e, :, ff : 2 * ff] = grad_up_pre
        hids[e, :, 2 * ff :] = (active * pre_up).astype(jnp.bfloat16)
        back = dot(grad_gate_pre, w_gate[e], (1, 1)) + dot(grad_up_pre, w_up[e], (1, 1))
        back_all[e * rows : (e + 1) * rows, :] = back.astype(jnp.bfloat16)

    summed = dot(hot, back_all[...], (0, 0)).astype(jnp.bfloat16)
    start = 0
    for part in parts:
        part[...] = summed[start : start + part.shape[0], :]
        start += part.shape[0]


def chunk_call(tokens, upstream, first_expert, weights, tok_rows, capacity, rows, top_count, per_group, joined):
    n_blocks = len(tokens)
    n_tok = n_blocks * tok_rows
    experts, width, ff = weights[0].shape
    part_shapes = [(n_tok, width)] if joined else [(tok_rows, width), (n_tok - tok_rows, width)]
    kept_shapes = [(experts, rows, width), (experts, rows, width), (experts, rows, 3 * ff)]
    smem, vmem = (pl.BlockSpec(memory_space=m) for m in (pltpu.SMEM, pltpu.VMEM))
    out_shapes = part_shapes + kept_shapes
    return pl.pallas_call(
        functools.partial(chunk_kernel, n_blocks, tok_rows, capacity, rows, top_count, per_group),
        in_specs=[smem] + [vmem] * (2 * n_blocks + 3),
        out_specs=[vmem] * len(out_shapes),
        out_shape=[pltpu.VMEM(shape, jnp.bfloat16) for shape in out_shapes],
        scratch_shapes=[pltpu.VMEM((experts * rows, width), jnp.bfloat16)],
        compiler_params=pltpu.CompilerParams(vmem_limit_bytes=VMEM_LIMIT),
        cost_estimate=pl.CostEstimate(
            flops=2 * experts * rows * width * (5 * ff + 3 * n_tok),
            bytes_accessed=6 * experts * width * ff + 8 * n_tok * width,
            transcendentals=0,
        ),
        name="chunk",
    )(first_expert, *[in_vmem(v) for v in (*tokens, *upstream, *weights)])


def halves_of(n, e, side, refs):
    depth = refs[0].shape[2] // 2
    cols = pl.ds(pl.multiple_of(side * depth, depth), depth)
    cat = lambda parts: jnp.concatenate(parts, axis=0)
    x_rows, s_rows = (cat([ref[e, :, cols] for ref in refs[i * n : (i + 1) * n]]) for i in range(2))
    hid = cat([ref[e] for ref in refs[2 * n : 3 * n]])
    ff = hid.shape[1] // 3
    return dot(x_rows, hid[:, : 2 * ff], (0, 0)), dot(hid[:, 2 * ff :], s_rows, (0, 0))


def send_kernel(n, side_ref, *refs):
    out = refs[3 * n]
    for e in range(out.shape[0]):
        gate_up, down = halves_of(n, e, side_ref[0], refs)
        depth = gate_up.shape[0]
        out[e, :depth, :] = gate_up.astype(jnp.bfloat16)
        out[e, depth:, :] = down.astype(jnp.bfloat16)


def keep_kernel(n, side_ref, *refs):
    got, outs = refs[3 * n], refs[3 * n + 1 : 3 * n + 4]
    buffers, sem = refs[3 * n + 4 : 3 * n + 7], refs[3 * n + 7]
    copies = []
    for e in range(got.shape[0]):
        gate_up, down = halves_of(n, e, side_ref[0], refs)
        depth = gate_up.shape[0]
        ff = down.shape[0]
        gate_up = gate_up + got[e, :depth, :].astype(jnp.float32)
        buffers[0][e] = gate_up[:, :ff].astype(jnp.bfloat16)
        buffers[1][e] = gate_up[:, ff:].astype(jnp.bfloat16)
        buffers[2][e] = (down + got[e, depth:, :].astype(jnp.float32)).astype(jnp.bfloat16)
        for i in range(3):
            copy = pltpu.make_async_copy(buffers[i].at[e], outs[i].at[e], sem.at[e, i])
            copy.start()
            copies.append(copy)
    for copy in copies:
        copy.wait()


def weight_call(side, x_rows, s_rows, hids, got=None):
    n = len(x_rows)
    experts, rows, width = x_rows[0].shape
    ff = hids[0].shape[2] // 3
    depth = width // 2
    smem, vmem = (pl.BlockSpec(memory_space=m) for m in (pltpu.SMEM, pltpu.VMEM))
    operands = [*x_rows, *s_rows, *hids]
    scratch = []
    if got is None:
        kernel, out_specs = send_kernel, vmem
        out_shape = pltpu.VMEM((experts, depth + ff, depth), jnp.bfloat16)
    else:
        kernel = keep_kernel
        operands = operands + [got]
        shapes = [(experts, depth, ff), (experts, depth, ff), (experts, ff, depth)]
        out_specs = [pl.BlockSpec(memory_space=pl.ANY)] * 3
        out_shape = [jax.ShapeDtypeStruct(s, jnp.bfloat16) for s in shapes]
        scratch = [pltpu.VMEM(s, jnp.bfloat16) for s in shapes] + [pltpu.SemaphoreType.DMA((experts, 3))]
    return pl.pallas_call(
        functools.partial(kernel, n),
        in_specs=[smem] + [vmem] * len(operands),
        out_specs=out_specs,
        out_shape=out_shape,
        scratch_shapes=scratch,
        compiler_params=pltpu.CompilerParams(vmem_limit_bytes=VMEM_LIMIT),
        cost_estimate=pl.CostEstimate(
            flops=2 * experts * n * rows * 3 * ff * depth,
            bytes_accessed=2 * experts * (n * rows * (width + 3 * ff) + 3 * ff * depth),
            transcendentals=0,
        ),
        name="weight_grads",
    )(side, *[in_vmem(v) for v in operands])


def per_device(tokens, upstream, expert_ids, gate_fixed, slots, w_gate, w_up, w_down):
    local_experts = w_gate.shape[0]
    n_group = lax.axis_size("group")
    n_ingroup = lax.axis_size("ingroup")
    experts_all = local_experts * n_group * n_ingroup
    tok_rows, top_count = expert_ids.shape
    width = tokens.shape[1]
    per_group = top_count // GROUPS_TOK
    capacity = max(2, 3 * tok_rows * top_count // (2 * experts_all))
    rows = -(-n_ingroup * capacity // 16) * 16
    z, x, core = (lax.axis_index(a) for a in ("group", "ingroup", "dp"))
    first_expert = ((z * n_ingroup + x) * local_experts).astype(jnp.int32).reshape(1)
    half = core.astype(jnp.int32).reshape(1)
    weights = load_call((w_gate, w_up, w_down))
    wide = lambda v: v.astype(jnp.float32)
    tie = lambda *trees: lax.optimization_barrier(trees)
    order = ring_order(n_group)
    along = lambda k: [(order[i], order[(i + k) % n_group]) for i in range(n_group)]
    shift = lambda s: [(i, (i + s) % n_ingroup) for i in range(n_ingroup)]

    def spread(column):
        return [column] + [lax.ppermute(column, "ingroup", shift(s)) for s in range(1, n_ingroup)]

    def chunk(blocks, joined=False):
        return chunk_call(*blocks, first_expert, weights, tok_rows, capacity, rows, top_count, per_group, joined)

    def across(others):
        return [
            lax.ppermute(others[(s - 1) * tok_rows : s * tok_rows], "ingroup", shift(-s)) for s in range(1, n_ingroup)
        ]

    def group_sum(part, backs):
        group_part = wide(part)
        for back in backs:
            group_part = group_part + wide(back)
        return group_part.astype(jnp.bfloat16)

    def homeward(group_part, k):
        return lax.ppermute(group_part, "group", along(-k))

    tokens, first_expert, half, other_half = tie(tokens, first_expert, half, 1 - half)
    first_tokens, upstream = pack_call(tokens, upstream, expert_ids, slots, gate_fixed)
    blocks, chunks, backs, sent = {}, {}, {}, {}
    last = n_group - 1
    for k in range(n_group):
        pair = [spread(tokens), spread(upstream)]
        if k == 0:
            pair[0][0] = first_tokens
        if k < last:
            tokens, upstream = (lax.ppermute(v, "group", along(1)) for v in (tokens, upstream))
        if k > 0:
            chunks[k - 1] = chunk(blocks[k - 1], k - 1 == 1)
        upstream, pair[1], chunks, weights = tie(upstream, pair[1], chunks, weights)
        tokens, pair[0] = tie(tokens, pair[0])
        blocks[k] = pair

    for k in range(2, last - 1):
        sent[k] = homeward(group_sum(chunks[k][0], across(chunks[k][1])), k)
    near = homeward(chunks[1][0], 1)
    blocks[last], chunks = tie(blocks[last], chunks)
    backs[last - 1] = across(chunks[last - 1][1])
    chunks[last] = chunk(blocks[last])
    backs[last] = across(chunks[last][1])
    chunks, backs[last - 1] = tie(chunks, backs[last - 1])

    carried = homeward(group_sum(chunks[last - 1][0], backs[last - 1]), last)
    kept = [[chunks[k][i] for k in range(n_group)] for i in (-3, -2, -1)]
    kept, near = tie(kept, near)
    to_send = weight_call(other_half, *kept)
    other = (wide(chunks[0][1]) + wide(near[tok_rows:])).astype(jnp.bfloat16)
    to_send, backs[last], other = tie(to_send, backs[last], other)
    to_send, carried = tie(to_send, carried)

    got = lax.ppermute(to_send, "dp", [(0, 1), (1, 0)])
    sent[last] = homeward(group_sum(chunks[last][0], [*backs[last], carried]), last)
    backs[0] = across(other)
    grads = weight_call(half, *kept, got)
    grads, sent, backs[0] = tie(grads, sent, backs[0])
    total = wide(chunks[0][0]) + wide(near[:tok_rows])
    for back in backs[0]:
        total = total + wide(back)
    for back in sent.values():
        total = total + wide(back)
    return (total.astype(jnp.bfloat16), *grads)


def solution(mesh):
    rows_spec = P(("parts", "group", "ingroup", "dp"), None)
    weight_spec = P(("group", "ingroup"), None, None)
    out_specs = (
        rows_spec,
        P(("parts", "group", "ingroup"), "dp", None),
        P(("parts", "group", "ingroup"), "dp", None),
        P(("parts", "group", "ingroup"), None, "dp"),
    )
    return jax.shard_map(
        per_device,
        mesh=mesh,
        in_specs=(rows_spec,) * 5 + (weight_spec,) * 3,
        out_specs=out_specs,
        check_vma=False,
    )
```

```python
import functools

import jax
import jax.numpy as jnp
from jax import lax
from jax.experimental import pallas as pl
from jax.experimental.pallas import tpu as pltpu
from jax.sharding import PartitionSpec as P

GROUPS_TOK = 4
ROUTE_ROWS = 8
VMEM_LIMIT = 24 * 1024 * 1024


def dot(a, b, contract):
    return lax.dot_general(a, b, ((contract[:1], contract[1:]), ((), ())), preferred_element_type=jnp.float32)


def in_hbm(v):
    return pltpu.with_memory_space_constraint(v, pltpu.HBM)


def in_vmem(v):
    return pltpu.with_memory_space_constraint(v, pltpu.VMEM)


def gated_parts(pre_gate):
    logistic = jax.nn.sigmoid(pre_gate)
    return (pre_gate * logistic, logistic * (1.0 + pre_gate * (1.0 - logistic)))


def ring_order(size):
    return [0] + list(range(1, size, 2)) + list(range(2, size, 2))[::-1]


def pack_kernel(tokens, upstream, expert_ids, slots, gate_fixed, tokens_out, out, sem):
    top_count, tok_rows = expert_ids.shape
    copies = [
        pltpu.make_async_copy(tokens, tokens_out, sem.at[0]),
        pltpu.make_async_copy(upstream, out.at[pl.ds(0, tok_rows), :], sem.at[1]),
    ]
    for copy in copies:
        copy.start()
    gate = gate_fixed[...]
    out[tok_rows:, :] = jnp.zeros((ROUTE_ROWS, out.shape[1]), jnp.bfloat16)
    for i, field in enumerate((expert_ids[...], slots[...], gate >> 8, gate & 255)):
        out[tok_rows : tok_rows + top_count, i * tok_rows : (i + 1) * tok_rows] = field.astype(jnp.float32).astype(
            jnp.bfloat16
        )
    for copy in copies:
        copy.wait()


def pack_call(tokens, upstream, expert_ids, slots, gate_fixed):
    tok_rows, width = tokens.shape
    vmem, hbm = (pl.BlockSpec(memory_space=m) for m in (pltpu.VMEM, pltpu.HBM))
    operands = [in_hbm(v) for v in (tokens, upstream, expert_ids.T, slots.T, gate_fixed.T)]
    return pl.pallas_call(
        pack_kernel,
        in_specs=[hbm] * 2 + [vmem] * 3,
        out_specs=[vmem] * 2,
        out_shape=[pltpu.VMEM((rows, width), jnp.bfloat16) for rows in (tok_rows, tok_rows + ROUTE_ROWS)],
        scratch_shapes=[pltpu.SemaphoreType.DMA((2,))],
        compiler_params=pltpu.CompilerParams(vmem_limit_bytes=VMEM_LIMIT),
        name="pack",
    )(*operands)


def route_keys(route, first_expert, local_experts, capacity, rows, offset, tok_rows, top_count, per_group):
    field = lambda i: route[:top_count, i * tok_rows : (i + 1) * tok_rows]
    expert = field(0).astype(jnp.int32) - first_expert
    slot = field(1).astype(jnp.int32)
    gate = (field(2) * 256.0 + field(3)) / 65536.0
    valid = (expert >= 0) & (expert < local_experts) & (slot < capacity)
    key = jnp.where(valid, expert * rows + offset + slot, -1)
    gate = jnp.where(valid, gate, 0.0)
    pairs = []
    for i in range(per_group):
        key_out, gate_out = key[i : i + 1, :], gate[i : i + 1, :]
        for j in range(i + per_group, top_count, per_group):
            key_out = jnp.maximum(key_out, key[j : j + 1, :])
            gate_out = jnp.maximum(gate_out, gate[j : j + 1, :])
        pairs.append((key_out, gate_out))
    return pairs


def load_kernel(*refs):
    n = len(refs) // 2
    copies = [pltpu.make_async_copy(refs[i], refs[n + i], refs[-1].at[i]) for i in range(n)]
    for copy in copies:
        copy.start()
    for copy in copies:
        copy.wait()


def load_call(arrays):
    hbm, vmem = (pl.BlockSpec(memory_space=m) for m in (pltpu.HBM, pltpu.VMEM))
    return pl.pallas_call(
        load_kernel,
        in_specs=[hbm] * len(arrays),
        out_specs=[vmem] * len(arrays),
        out_shape=[pltpu.VMEM(v.shape, v.dtype) for v in arrays],
        scratch_shapes=[pltpu.SemaphoreType.DMA((len(arrays),))],
        compiler_params=pltpu.CompilerParams(vmem_limit_bytes=VMEM_LIMIT),
        name="load",
    )(*[in_hbm(v) for v in arrays])


def chunk_kernel(n_blocks, tok_rows, capacity, rows, top_count, per_group, first_ref, *refs):
    tokens, upstream = refs[:n_blocks], refs[n_blocks : 2 * n_blocks]
    w_gate, w_up, w_down = refs[2 * n_blocks : 2 * n_blocks + 3]
    parts = refs[2 * n_blocks + 3 : -4]
    x_rows, s_rows, hids, back_all = refs[-4:]
    experts, width, ff = w_gate.shape

    pairs = []
    for b in range(n_blocks):
        route = upstream[b][tok_rows : tok_rows + ROUTE_ROWS, :].astype(jnp.float32)
        pairs.append(
            route_keys(route, first_ref[0], experts, capacity, rows, b * capacity, tok_rows, top_count, per_group)
        )
    place = lax.broadcasted_iota(jnp.int32, (experts * rows, n_blocks * tok_rows), 0)
    hot = jnp.zeros(place.shape, jnp.float32)
    gate_hot = jnp.zeros(place.shape, jnp.float32)
    for i in range(per_group):
        key = jnp.concatenate([pair[i][0] for pair in pairs], axis=1)
        gate = jnp.concatenate([pair[i][1] for pair in pairs], axis=1)
        match = place == key
        hot = jnp.where(match, 1.0, hot)
        gate_hot = jnp.where(match, gate, gate_hot)
    hot = hot.astype(jnp.bfloat16)
    row_gate = jnp.sum(gate_hot, axis=1, keepdims=True)

    x_all = jnp.concatenate([block[...] for block in tokens], axis=0)
    gathered = dot(hot, x_all, (1, 0)).astype(jnp.bfloat16)
    for e in range(experts):
        x_rows[e] = gathered[e * rows : (e + 1) * rows, :]
    u_all = jnp.concatenate([block[:tok_rows, :] for block in upstream], axis=0)
    scaled = (dot(hot, u_all, (1, 0)) * row_gate).astype(jnp.bfloat16)
    for e in range(experts):
        s_rows[e] = scaled[e * rows : (e + 1) * rows, :]

    for e in range(experts):
        pre_gate = dot(x_rows[e], w_gate[e], (1, 0))
        pre_up = dot(x_rows[e], w_up[e], (1, 0))
        grad_hidden = dot(s_rows[e], w_down[e], (1, 1))
        active, slope = gated_parts(pre_gate)
        grad_gate_pre = (grad_hidden * pre_up * slope).astype(jnp.bfloat16)
        grad_up_pre = (grad_hidden * active).astype(jnp.bfloat16)
        hids[e, :, :ff] = grad_gate_pre
        hids[e, :, ff : 2 * ff] = grad_up_pre
        hids[e, :, 2 * ff :] = (active * pre_up).astype(jnp.bfloat16)
        back = dot(grad_gate_pre, w_gate[e], (1, 1)) + dot(grad_up_pre, w_up[e], (1, 1))
        back_all[e * rows : (e + 1) * rows, :] = back.astype(jnp.bfloat16)

    summed = dot(hot, back_all[...], (0, 0)).astype(jnp.bfloat16)
    start = 0
    for part in parts:
        part[...] = summed[start : start + part.shape[0], :]
        start += part.shape[0]


def chunk_call(tokens, upstream, first_expert, weights, tok_rows, capacity, rows, top_count, per_group, joined):
    n_blocks = len(tokens)
    n_tok = n_blocks * tok_rows
    experts, width, ff = weights[0].shape
    part_shapes = [(n_tok, width)] if joined else [(tok_rows, width), (n_tok - tok_rows, width)]
    kept_shapes = [(experts, rows, width), (experts, rows, width), (experts, rows, 3 * ff)]
    smem, vmem = (pl.BlockSpec(memory_space=m) for m in (pltpu.SMEM, pltpu.VMEM))
    out_shapes = part_shapes + kept_shapes
    return pl.pallas_call(
        functools.partial(chunk_kernel, n_blocks, tok_rows, capacity, rows, top_count, per_group),
        in_specs=[smem] + [vmem] * (2 * n_blocks + 3),
        out_specs=[vmem] * len(out_shapes),
        out_shape=[pltpu.VMEM(shape, jnp.bfloat16) for shape in out_shapes],
        scratch_shapes=[pltpu.VMEM((experts * rows, width), jnp.bfloat16)],
        compiler_params=pltpu.CompilerParams(vmem_limit_bytes=VMEM_LIMIT),
        cost_estimate=pl.CostEstimate(
            flops=2 * experts * rows * width * (5 * ff + 3 * n_tok),
            bytes_accessed=6 * experts * width * ff + 8 * n_tok * width,
            transcendentals=0,
        ),
        name="chunk",
    )(first_expert, *[in_vmem(v) for v in (*tokens, *upstream, *weights)])


def halves_of(n, e, side, refs):
    depth = refs[0].shape[2] // 2
    cols = pl.ds(pl.multiple_of(side * depth, depth), depth)
    cat = lambda parts: jnp.concatenate(parts, axis=0)
    x_rows, s_rows = (cat([ref[e, :, cols] for ref in refs[i * n : (i + 1) * n]]) for i in range(2))
    hid = cat([ref[e] for ref in refs[2 * n : 3 * n]])
    ff = hid.shape[1] // 3
    return dot(x_rows, hid[:, : 2 * ff], (0, 0)), dot(hid[:, 2 * ff :], s_rows, (0, 0))


def send_kernel(n, side_ref, *refs):
    out = refs[3 * n]
    for e in range(out.shape[0]):
        gate_up, down = halves_of(n, e, side_ref[0], refs)
        depth = gate_up.shape[0]
        out[e, :depth, :] = gate_up.astype(jnp.bfloat16)
        out[e, depth:, :] = down.astype(jnp.bfloat16)


def keep_kernel(n, side_ref, *refs):
    got, outs = refs[3 * n], refs[3 * n + 1 : 3 * n + 4]
    buffers, sem = refs[3 * n + 4 : 3 * n + 7], refs[3 * n + 7]
    copies = []
    for e in range(got.shape[0]):
        gate_up, down = halves_of(n, e, side_ref[0], refs)
        depth = gate_up.shape[0]
        ff = down.shape[0]
        gate_up = gate_up + got[e, :depth, :].astype(jnp.float32)
        buffers[0][e] = gate_up[:, :ff].astype(jnp.bfloat16)
        buffers[1][e] = gate_up[:, ff:].astype(jnp.bfloat16)
        buffers[2][e] = (down + got[e, depth:, :].astype(jnp.float32)).astype(jnp.bfloat16)
        for i in range(3):
            copy = pltpu.make_async_copy(buffers[i].at[e], outs[i].at[e], sem.at[e, i])
            copy.start()
            copies.append(copy)
    for copy in copies:
        copy.wait()


def weight_call(side, x_rows, s_rows, hids, got=None):
    n = len(x_rows)
    experts, rows, width = x_rows[0].shape
    ff = hids[0].shape[2] // 3
    depth = width // 2
    smem, vmem = (pl.BlockSpec(memory_space=m) for m in (pltpu.SMEM, pltpu.VMEM))
    operands = [*x_rows, *s_rows, *hids]
    scratch = []
    if got is None:
        kernel, out_specs = send_kernel, vmem
        out_shape = pltpu.VMEM((experts, depth + ff, depth), jnp.bfloat16)
    else:
        kernel = keep_kernel
        operands = operands + [got]
        shapes = [(experts, depth, ff), (experts, depth, ff), (experts, ff, depth)]
        out_specs = [pl.BlockSpec(memory_space=pl.ANY)] * 3
        out_shape = [jax.ShapeDtypeStruct(s, jnp.bfloat16) for s in shapes]
        scratch = [pltpu.VMEM(s, jnp.bfloat16) for s in shapes] + [pltpu.SemaphoreType.DMA((experts, 3))]
    return pl.pallas_call(
        functools.partial(kernel, n),
        in_specs=[smem] + [vmem] * len(operands),
        out_specs=out_specs,
        out_shape=out_shape,
        scratch_shapes=scratch,
        compiler_params=pltpu.CompilerParams(vmem_limit_bytes=VMEM_LIMIT),
        cost_estimate=pl.CostEstimate(
            flops=2 * experts * n * rows * 3 * ff * depth,
            bytes_accessed=2 * experts * (n * rows * (width + 3 * ff) + 3 * ff * depth),
            transcendentals=0,
        ),
        name="weight_grads",
    )(side, *[in_vmem(v) for v in operands])


def per_device(tokens, upstream, expert_ids, gate_fixed, slots, w_gate, w_up, w_down):
    local_experts = w_gate.shape[0]
    n_group = lax.axis_size("group")
    n_ingroup = lax.axis_size("ingroup")
    experts_all = local_experts * n_group * n_ingroup
    tok_rows, top_count = expert_ids.shape
    width = tokens.shape[1]
    per_group = top_count // GROUPS_TOK
    capacity = max(2, 3 * tok_rows * top_count // (2 * experts_all))
    rows = -(-n_ingroup * capacity // 16) * 16
    z, x, core = (lax.axis_index(a) for a in ("group", "ingroup", "dp"))
    first_expert = ((z * n_ingroup + x) * local_experts).astype(jnp.int32).reshape(1)
    half = core.astype(jnp.int32).reshape(1)
    weights = load_call((w_gate, w_up, w_down))
    wide = lambda v: v.astype(jnp.float32)
    tie = lambda *trees: lax.optimization_barrier(trees)
    order = ring_order(n_group)
    along = lambda k: [(order[i], order[(i + k) % n_group]) for i in range(n_group)]
    shift = lambda s: [(i, (i + s) % n_ingroup) for i in range(n_ingroup)]

    def spread(column):
        return [column] + [lax.ppermute(column, "ingroup", shift(s)) for s in range(1, n_ingroup)]

    def chunk(blocks, joined=False):
        return chunk_call(*blocks, first_expert, weights, tok_rows, capacity, rows, top_count, per_group, joined)

    def across(others):
        return [
            lax.ppermute(others[(s - 1) * tok_rows : s * tok_rows], "ingroup", shift(-s)) for s in range(1, n_ingroup)
        ]

    def group_sum(part, backs):
        group_part = wide(part)
        for back in backs:
            group_part = group_part + wide(back)
        return group_part.astype(jnp.bfloat16)

    def homeward(group_part, k):
        return lax.ppermute(group_part, "group", along(-k))

    tokens, first_expert, half, other_half = tie(tokens, first_expert, half, 1 - half)
    first_tokens, upstream = pack_call(tokens, upstream, expert_ids, slots, gate_fixed)
    blocks, chunks, backs, sent = {}, {}, {}, {}
    last = n_group - 1
    for k in range(n_group):
        pair = [spread(tokens), spread(upstream)]
        if k == 0:
            pair[0][0] = first_tokens
        if k < last:
            tokens, upstream = (lax.ppermute(v, "group", along(1)) for v in (tokens, upstream))
        if k > 0:
            chunks[k - 1] = chunk(blocks[k - 1], k - 1 == 1)
        tokens, pair[0], chunks, weights = tie(tokens, pair[0], chunks, weights)
        upstream, pair[1] = tie(upstream, pair[1])
        blocks[k] = pair

    for k in range(2, last - 1):
        sent[k] = homeward(group_sum(chunks[k][0], across(chunks[k][1])), k)
    near = lax.ppermute(chunks[1][0], "group", along(-1))
    blocks[last], chunks = tie(blocks[last], chunks)
    backs[last - 1] = across(chunks[last - 1][1])
    chunks[last] = chunk(blocks[last])
    last_back = across(chunks[last][1])
    chunks, backs, near = tie(chunks, backs, near)

    backs[last] = last_back
    carried = homeward(group_sum(chunks[last - 1][0], backs[last - 1]), last)
    kept = [[chunks[k][i] for k in range(n_group)] for i in (-3, -2, -1)]
    to_send = weight_call(other_half, *kept)
    to_send, backs[last], carried = tie(to_send, backs[last], carried)

    got = lax.ppermute(to_send, "dp", [(0, 1), (1, 0)])
    sent[last] = homeward(group_sum(chunks[last][0], [*backs[last], carried]), last)
    backs[0] = across((wide(chunks[0][1]) + wide(near[tok_rows:])).astype(jnp.bfloat16))
    grads = weight_call(half, *kept, got)
    grads, sent, backs[0] = tie(grads, sent, backs[0])
    total = wide(chunks[0][0]) + wide(near[:tok_rows])
    for back in backs[0]:
        total = total + wide(back)
    for back in sent.values():
        total = total + wide(back)
    return (total.astype(jnp.bfloat16), *grads)


def solution(mesh):
    rows_spec = P(("parts", "group", "ingroup", "dp"), None)
    weight_spec = P(("group", "ingroup"), None, None)
    out_specs = (
        rows_spec,
        P(("parts", "group", "ingroup"), "dp", None),
        P(("parts", "group", "ingroup"), "dp", None),
        P(("parts", "group", "ingroup"), None, "dp"),
    )
    return jax.shard_map(
        per_device,
        mesh=mesh,
        in_specs=(rows_spec,) * 5 + (weight_spec,) * 3,
        out_specs=out_specs,
        check_vma=False,
    )
```

```python
import functools

import jax
import jax.numpy as jnp
from jax import lax
from jax.experimental import pallas as pl
from jax.experimental.pallas import tpu as pltpu
from jax.sharding import PartitionSpec as P

GROUPS_TOK = 4
ROUTE_ROWS = 8
VMEM_LIMIT = 24 * 1024 * 1024


def dot(a, b, contract):
    return lax.dot_general(a, b, ((contract[:1], contract[1:]), ((), ())), preferred_element_type=jnp.float32)


def in_hbm(v):
    return pltpu.with_memory_space_constraint(v, pltpu.HBM)


def in_vmem(v):
    return pltpu.with_memory_space_constraint(v, pltpu.VMEM)


def gated_parts(pre_gate):
    logistic = jax.nn.sigmoid(pre_gate)
    return (pre_gate * logistic, logistic * (1.0 + pre_gate * (1.0 - logistic)))


def ring_order(size):
    return [0] + list(range(1, size, 2)) + list(range(2, size, 2))[::-1]


def pack_kernel(tokens, upstream, expert_ids, slots, gate_fixed, tokens_out, out, sem):
    top_count, tok_rows = expert_ids.shape
    copies = [
        pltpu.make_async_copy(tokens, tokens_out, sem.at[0]),
        pltpu.make_async_copy(upstream, out.at[pl.ds(0, tok_rows), :], sem.at[1]),
    ]
    for copy in copies:
        copy.start()
    gate = gate_fixed[...]
    out[tok_rows:, :] = jnp.zeros((ROUTE_ROWS, out.shape[1]), jnp.bfloat16)
    for i, field in enumerate((expert_ids[...], slots[...], gate >> 8, gate & 255)):
        out[tok_rows : tok_rows + top_count, i * tok_rows : (i + 1) * tok_rows] = field.astype(jnp.float32).astype(
            jnp.bfloat16
        )
    for copy in copies:
        copy.wait()


def pack_call(tokens, upstream, expert_ids, slots, gate_fixed):
    tok_rows, width = tokens.shape
    vmem, hbm = (pl.BlockSpec(memory_space=m) for m in (pltpu.VMEM, pltpu.HBM))
    operands = [in_hbm(v) for v in (tokens, upstream, expert_ids.T, slots.T, gate_fixed.T)]
    return pl.pallas_call(
        pack_kernel,
        in_specs=[hbm] * 2 + [vmem] * 3,
        out_specs=[vmem] * 2,
        out_shape=[pltpu.VMEM((rows, width), jnp.bfloat16) for rows in (tok_rows, tok_rows + ROUTE_ROWS)],
        scratch_shapes=[pltpu.SemaphoreType.DMA((2,))],
        compiler_params=pltpu.CompilerParams(vmem_limit_bytes=VMEM_LIMIT),
        name="pack",
    )(*operands)


def route_keys(route, first_expert, local_experts, capacity, rows, offset, tok_rows, top_count, per_group):
    field = lambda i: route[:top_count, i * tok_rows : (i + 1) * tok_rows]
    expert = field(0).astype(jnp.int32) - first_expert
    slot = field(1).astype(jnp.int32)
    gate = (field(2) * 256.0 + field(3)) / 65536.0
    valid = (expert >= 0) & (expert < local_experts) & (slot < capacity)
    key = jnp.where(valid, expert * rows + offset + slot, -1)
    gate = jnp.where(valid, gate, 0.0)
    pairs = []
    for i in range(per_group):
        key_out, gate_out = key[i : i + 1, :], gate[i : i + 1, :]
        for j in range(i + per_group, top_count, per_group):
            key_out = jnp.maximum(key_out, key[j : j + 1, :])
            gate_out = jnp.maximum(gate_out, gate[j : j + 1, :])
        pairs.append((key_out, gate_out))
    return pairs


def load_kernel(*refs):
    n = len(refs) // 2
    copies = [pltpu.make_async_copy(refs[i], refs[n + i], refs[-1].at[i]) for i in range(n)]
    for copy in copies:
        copy.start()
    for copy in copies:
        copy.wait()


def load_call(arrays):
    hbm, vmem = (pl.BlockSpec(memory_space=m) for m in (pltpu.HBM, pltpu.VMEM))
    return pl.pallas_call(
        load_kernel,
        in_specs=[hbm] * len(arrays),
        out_specs=[vmem] * len(arrays),
        out_shape=[pltpu.VMEM(v.shape, v.dtype) for v in arrays],
        scratch_shapes=[pltpu.SemaphoreType.DMA((len(arrays),))],
        compiler_params=pltpu.CompilerParams(vmem_limit_bytes=VMEM_LIMIT),
        name="load",
    )(*[in_hbm(v) for v in arrays])


def chunk_kernel(n_blocks, tok_rows, capacity, rows, top_count, per_group, first_ref, *refs):
    tokens, upstream = refs[:n_blocks], refs[n_blocks : 2 * n_blocks]
    w_gate, w_up, w_down = refs[2 * n_blocks : 2 * n_blocks + 3]
    parts = refs[2 * n_blocks + 3 : -4]
    x_rows, s_rows, hids, back_all = refs[-4:]
    experts, width, ff = w_gate.shape

    pairs = []
    for b in range(n_blocks):
        route = upstream[b][tok_rows : tok_rows + ROUTE_ROWS, :].astype(jnp.float32)
        pairs.append(
            route_keys(route, first_ref[0], experts, capacity, rows, b * capacity, tok_rows, top_count, per_group)
        )
    place = lax.broadcasted_iota(jnp.int32, (experts * rows, n_blocks * tok_rows), 0)
    hot = jnp.zeros(place.shape, jnp.float32)
    gate_hot = jnp.zeros(place.shape, jnp.float32)
    for i in range(per_group):
        key = jnp.concatenate([pair[i][0] for pair in pairs], axis=1)
        gate = jnp.concatenate([pair[i][1] for pair in pairs], axis=1)
        match = place == key
        hot = jnp.where(match, 1.0, hot)
        gate_hot = jnp.where(match, gate, gate_hot)
    hot = hot.astype(jnp.bfloat16)
    row_gate = jnp.sum(gate_hot, axis=1, keepdims=True)

    x_all = jnp.concatenate([block[...] for block in tokens], axis=0)
    gathered = dot(hot, x_all, (1, 0)).astype(jnp.bfloat16)
    for e in range(experts):
        x_rows[e] = gathered[e * rows : (e + 1) * rows, :]
    u_all = jnp.concatenate([block[:tok_rows, :] for block in upstream], axis=0)
    scaled = (dot(hot, u_all, (1, 0)) * row_gate).astype(jnp.bfloat16)
    for e in range(experts):
        s_rows[e] = scaled[e * rows : (e + 1) * rows, :]

    for e in range(experts):
        pre_gate = dot(x_rows[e], w_gate[e], (1, 0))
        pre_up = dot(x_rows[e], w_up[e], (1, 0))
        grad_hidden = dot(s_rows[e], w_down[e], (1, 1))
        active, slope = gated_parts(pre_gate)
        grad_gate_pre = (grad_hidden * pre_up * slope).astype(jnp.bfloat16)
        grad_up_pre = (grad_hidden * active).astype(jnp.bfloat16)
        hids[e, :, :ff] = grad_gate_pre
        hids[e, :, ff : 2 * ff] = grad_up_pre
        hids[e, :, 2 * ff :] = (active * pre_up).astype(jnp.bfloat16)
        back = dot(grad_gate_pre, w_gate[e], (1, 1)) + dot(grad_up_pre, w_up[e], (1, 1))
        back_all[e * rows : (e + 1) * rows, :] = back.astype(jnp.bfloat16)

    summed = dot(hot, back_all[...], (0, 0)).astype(jnp.bfloat16)
    start = 0
    for part in parts:
        part[...] = summed[start : start + part.shape[0], :]
        start += part.shape[0]


def chunk_call(tokens, upstream, first_expert, weights, tok_rows, capacity, rows, top_count, per_group, joined):
    n_blocks = len(tokens)
    n_tok = n_blocks * tok_rows
    experts, width, ff = weights[0].shape
    part_shapes = [(n_tok, width)] if joined else [(tok_rows, width), (n_tok - tok_rows, width)]
    kept_shapes = [(experts, rows, width), (experts, rows, width), (experts, rows, 3 * ff)]
    smem, vmem = (pl.BlockSpec(memory_space=m) for m in (pltpu.SMEM, pltpu.VMEM))
    out_shapes = part_shapes + kept_shapes
    return pl.pallas_call(
        functools.partial(chunk_kernel, n_blocks, tok_rows, capacity, rows, top_count, per_group),
        in_specs=[smem] + [vmem] * (2 * n_blocks + 3),
        out_specs=[vmem] * len(out_shapes),
        out_shape=[pltpu.VMEM(shape, jnp.bfloat16) for shape in out_shapes],
        scratch_shapes=[pltpu.VMEM((experts * rows, width), jnp.bfloat16)],
        compiler_params=pltpu.CompilerParams(vmem_limit_bytes=VMEM_LIMIT),
        cost_estimate=pl.CostEstimate(
            flops=2 * experts * rows * width * (5 * ff + 3 * n_tok),
            bytes_accessed=6 * experts * width * ff + 8 * n_tok * width,
            transcendentals=0,
        ),
        name="chunk",
    )(first_expert, *[in_vmem(v) for v in (*tokens, *upstream, *weights)])


def halves_of(n, e, side, refs):
    depth = refs[0].shape[2] // 2
    cols = pl.ds(pl.multiple_of(side * depth, depth), depth)
    cat = lambda parts: jnp.concatenate(parts, axis=0)
    x_rows, s_rows = (cat([ref[e, :, cols] for ref in refs[i * n : (i + 1) * n]]) for i in range(2))
    hid = cat([ref[e] for ref in refs[2 * n : 3 * n]])
    ff = hid.shape[1] // 3
    return dot(x_rows, hid[:, : 2 * ff], (0, 0)), dot(hid[:, 2 * ff :], s_rows, (0, 0))


def send_kernel(n, side_ref, *refs):
    out = refs[3 * n]
    for e in range(out.shape[0]):
        gate_up, down = halves_of(n, e, side_ref[0], refs)
        depth = gate_up.shape[0]
        out[e, :depth, :] = gate_up.astype(jnp.bfloat16)
        out[e, depth:, :] = down.astype(jnp.bfloat16)


def keep_kernel(n, side_ref, *refs):
    got, outs = refs[3 * n], refs[3 * n + 1 : 3 * n + 4]
    buffers, sem = refs[3 * n + 4 : 3 * n + 7], refs[3 * n + 7]
    copies = []
    for e in range(got.shape[0]):
        gate_up, down = halves_of(n, e, side_ref[0], refs)
        depth = gate_up.shape[0]
        ff = down.shape[0]
        gate_up = gate_up + got[e, :depth, :].astype(jnp.float32)
        buffers[0][e] = gate_up[:, :ff].astype(jnp.bfloat16)
        buffers[1][e] = gate_up[:, ff:].astype(jnp.bfloat16)
        buffers[2][e] = (down + got[e, depth:, :].astype(jnp.float32)).astype(jnp.bfloat16)
        for i in range(3):
            copy = pltpu.make_async_copy(buffers[i].at[e], outs[i].at[e], sem.at[e, i])
            copy.start()
            copies.append(copy)
    for copy in copies:
        copy.wait()


def weight_call(side, x_rows, s_rows, hids, got=None):
    n = len(x_rows)
    experts, rows, width = x_rows[0].shape
    ff = hids[0].shape[2] // 3
    depth = width // 2
    smem, vmem = (pl.BlockSpec(memory_space=m) for m in (pltpu.SMEM, pltpu.VMEM))
    operands = [*x_rows, *s_rows, *hids]
    scratch = []
    if got is None:
        kernel, out_specs = send_kernel, vmem
        out_shape = pltpu.VMEM((experts, depth + ff, depth), jnp.bfloat16)
    else:
        kernel = keep_kernel
        operands = operands + [got]
        shapes = [(experts, depth, ff), (experts, depth, ff), (experts, ff, depth)]
        out_specs = [pl.BlockSpec(memory_space=pl.ANY)] * 3
        out_shape = [jax.ShapeDtypeStruct(s, jnp.bfloat16) for s in shapes]
        scratch = [pltpu.VMEM(s, jnp.bfloat16) for s in shapes] + [pltpu.SemaphoreType.DMA((experts, 3))]
    return pl.pallas_call(
        functools.partial(kernel, n),
        in_specs=[smem] + [vmem] * len(operands),
        out_specs=out_specs,
        out_shape=out_shape,
        scratch_shapes=scratch,
        compiler_params=pltpu.CompilerParams(vmem_limit_bytes=VMEM_LIMIT),
        cost_estimate=pl.CostEstimate(
            flops=2 * experts * n * rows * 3 * ff * depth,
            bytes_accessed=2 * experts * (n * rows * (width + 3 * ff) + 3 * ff * depth),
            transcendentals=0,
        ),
        name="weight_grads",
    )(side, *[in_vmem(v) for v in operands])


def per_device(tokens, upstream, expert_ids, gate_fixed, slots, w_gate, w_up, w_down):
    local_experts = w_gate.shape[0]
    n_group = lax.axis_size("group")
    n_ingroup = lax.axis_size("ingroup")
    experts_all = local_experts * n_group * n_ingroup
    tok_rows, top_count = expert_ids.shape
    width = tokens.shape[1]
    per_group = top_count // GROUPS_TOK
    capacity = max(2, 3 * tok_rows * top_count // (2 * experts_all))
    rows = -(-n_ingroup * capacity // 16) * 16
    z, x, core = (lax.axis_index(a) for a in ("group", "ingroup", "dp"))
    first_expert = ((z * n_ingroup + x) * local_experts).astype(jnp.int32).reshape(1)
    half = core.astype(jnp.int32).reshape(1)
    weights = load_call((w_gate, w_up, w_down))
    wide = lambda v: v.astype(jnp.float32)
    tie = lambda *trees: lax.optimization_barrier(trees)
    order = ring_order(n_group)
    along = lambda k: [(order[i], order[(i + k) % n_group]) for i in range(n_group)]
    shift = lambda s: [(i, (i + s) % n_ingroup) for i in range(n_ingroup)]

    def spread(column):
        return [column] + [lax.ppermute(column, "ingroup", shift(s)) for s in range(1, n_ingroup)]

    def chunk(blocks, joined=False):
        return chunk_call(*blocks, first_expert, weights, tok_rows, capacity, rows, top_count, per_group, joined)

    def across(others):
        return [
            lax.ppermute(others[(s - 1) * tok_rows : s * tok_rows], "ingroup", shift(-s)) for s in range(1, n_ingroup)
        ]

    def group_sum(part, backs):
        group_part = wide(part)
        for back in backs:
            group_part = group_part + wide(back)
        return group_part.astype(jnp.bfloat16)

    def homeward(group_part, k):
        return lax.ppermute(group_part, "group", along(-k))

    tokens, first_expert, half, other_half = tie(tokens, first_expert, half, 1 - half)
    first_tokens, upstream = pack_call(tokens, upstream, expert_ids, slots, gate_fixed)
    blocks, chunks, backs, sent = {}, {}, {}, {}
    last = n_group - 1
    for k in range(n_group):
        pair = [spread(tokens), spread(upstream)]
        if k == 0:
            pair[0][0] = first_tokens
        if k < last:
            tokens, upstream = (lax.ppermute(v, "group", along(1)) for v in (tokens, upstream))
        if k > 0:
            chunks[k - 1] = chunk(blocks[k - 1], k - 1 == 1)
        tokens, pair[0], chunks, weights = tie(tokens, pair[0], chunks, weights)
        upstream, pair[1] = tie(upstream, pair[1])
        blocks[k] = pair

    for k in range(2, last - 1):
        sent[k] = homeward(group_sum(chunks[k][0], across(chunks[k][1])), k)
    near = lax.ppermute(chunks[1][0], "group", along(-1))
    blocks[last], chunks = tie(blocks[last], chunks)
    backs[last - 1] = across(chunks[last - 1][1])
    chunks[last] = chunk(blocks[last])
    last_back = across(chunks[last][1])
    chunks, backs, near = tie(chunks, backs, near)

    backs[last] = last_back
    carried = homeward(group_sum(chunks[last - 1][0], backs[last - 1]), last)
    kept = [[chunks[k][i] for k in range(n_group)] for i in (-3, -2, -1)]
    to_send = weight_call(other_half, *kept)
    to_send, backs[last], carried = tie(to_send, backs[last], carried)

    got = lax.ppermute(to_send, "dp", [(0, 1), (1, 0)])
    sent[last] = homeward(group_sum(chunks[last][0], [*backs[last], carried]), last)
    backs[0] = across((wide(chunks[0][1]) + wide(near[tok_rows:])).astype(jnp.bfloat16))
    grads = weight_call(half, *kept, got)
    grads, sent = tie(grads, sent)
    grads, backs[0] = tie(grads, backs[0])
    total = wide(chunks[0][0]) + wide(near[:tok_rows])
    for back in backs[0]:
        total = total + wide(back)
    for back in sent.values():
        total = total + wide(back)
    return (total.astype(jnp.bfloat16), *grads)


def solution(mesh):
    rows_spec = P(("parts", "group", "ingroup", "dp"), None)
    weight_spec = P(("group", "ingroup"), None, None)
    out_specs = (
        rows_spec,
        P(("parts", "group", "ingroup"), "dp", None),
        P(("parts", "group", "ingroup"), "dp", None),
        P(("parts", "group", "ingroup"), None, "dp"),
    )
    return jax.shard_map(
        per_device,
        mesh=mesh,
        in_specs=(rows_spec,) * 5 + (weight_spec,) * 3,
        out_specs=out_specs,
        check_vma=False,
    )
```

```python
import functools

import jax
import jax.numpy as jnp
from jax import lax
from jax.experimental import pallas as pl
from jax.experimental.pallas import tpu as pltpu
from jax.sharding import PartitionSpec as P

GROUPS_TOK = 4
ROUTE_ROWS = 8
VMEM_LIMIT = 24 * 1024 * 1024


def dot(a, b, contract):
    return lax.dot_general(a, b, ((contract[:1], contract[1:]), ((), ())), preferred_element_type=jnp.float32)


def in_hbm(v):
    return pltpu.with_memory_space_constraint(v, pltpu.HBM)


def in_vmem(v):
    return pltpu.with_memory_space_constraint(v, pltpu.VMEM)


def gated_parts(pre_gate):
    logistic = jax.nn.sigmoid(pre_gate)
    return (pre_gate * logistic, logistic * (1.0 + pre_gate * (1.0 - logistic)))


def ring_order(size):
    return [0] + list(range(1, size, 2)) + list(range(2, size, 2))[::-1]


def pack_kernel(tokens, upstream, expert_ids, slots, gate_fixed, tokens_out, out, sem):
    top_count, tok_rows = expert_ids.shape
    copies = [
        pltpu.make_async_copy(tokens, tokens_out, sem.at[0]),
        pltpu.make_async_copy(upstream, out.at[pl.ds(0, tok_rows), :], sem.at[1]),
    ]
    for copy in copies:
        copy.start()
    gate = gate_fixed[...]
    out[tok_rows:, :] = jnp.zeros((ROUTE_ROWS, out.shape[1]), jnp.bfloat16)
    for i, field in enumerate((expert_ids[...], slots[...], gate >> 8, gate & 255)):
        out[tok_rows : tok_rows + top_count, i * tok_rows : (i + 1) * tok_rows] = field.astype(jnp.float32).astype(
            jnp.bfloat16
        )
    for copy in copies:
        copy.wait()


def pack_call(tokens, upstream, expert_ids, slots, gate_fixed):
    tok_rows, width = tokens.shape
    vmem, hbm = (pl.BlockSpec(memory_space=m) for m in (pltpu.VMEM, pltpu.HBM))
    operands = [in_hbm(v) for v in (tokens, upstream, expert_ids.T, slots.T, gate_fixed.T)]
    return pl.pallas_call(
        pack_kernel,
        in_specs=[hbm] * 2 + [vmem] * 3,
        out_specs=[vmem] * 2,
        out_shape=[pltpu.VMEM((rows, width), jnp.bfloat16) for rows in (tok_rows, tok_rows + ROUTE_ROWS)],
        scratch_shapes=[pltpu.SemaphoreType.DMA((2,))],
        compiler_params=pltpu.CompilerParams(vmem_limit_bytes=VMEM_LIMIT),
        name="pack",
    )(*operands)


def route_keys(route, first_expert, local_experts, capacity, rows, offset, tok_rows, top_count, per_group):
    field = lambda i: route[:top_count, i * tok_rows : (i + 1) * tok_rows]
    expert = field(0).astype(jnp.int32) - first_expert
    slot = field(1).astype(jnp.int32)
    gate = (field(2) * 256.0 + field(3)) / 65536.0
    valid = (expert >= 0) & (expert < local_experts) & (slot < capacity)
    key = jnp.where(valid, expert * rows + offset + slot, -1)
    gate = jnp.where(valid, gate, 0.0)
    pairs = []
    for i in range(per_group):
        key_out, gate_out = key[i : i + 1, :], gate[i : i + 1, :]
        for j in range(i + per_group, top_count, per_group):
            key_out = jnp.maximum(key_out, key[j : j + 1, :])
            gate_out = jnp.maximum(gate_out, gate[j : j + 1, :])
        pairs.append((key_out, gate_out))
    return pairs


def load_kernel(*refs):
    n = len(refs) // 2
    copies = [pltpu.make_async_copy(refs[i], refs[n + i], refs[-1].at[i]) for i in range(n)]
    for copy in copies:
        copy.start()
    for copy in copies:
        copy.wait()


def load_call(arrays):
    hbm, vmem = (pl.BlockSpec(memory_space=m) for m in (pltpu.HBM, pltpu.VMEM))
    return pl.pallas_call(
        load_kernel,
        in_specs=[hbm] * len(arrays),
        out_specs=[vmem] * len(arrays),
        out_shape=[pltpu.VMEM(v.shape, v.dtype) for v in arrays],
        scratch_shapes=[pltpu.SemaphoreType.DMA((len(arrays),))],
        compiler_params=pltpu.CompilerParams(vmem_limit_bytes=VMEM_LIMIT),
        name="load",
    )(*[in_hbm(v) for v in arrays])


def chunk_kernel(n_blocks, tok_rows, capacity, rows, top_count, per_group, first_ref, *refs):
    tokens, upstream = refs[:n_blocks], refs[n_blocks : 2 * n_blocks]
    w_gate, w_up, w_down = refs[2 * n_blocks : 2 * n_blocks + 3]
    parts = refs[2 * n_blocks + 3 : -4]
    x_rows, s_rows, hids, back_all = refs[-4:]
    experts, width, ff = w_gate.shape

    pairs = []
    for b in range(n_blocks):
        route = upstream[b][tok_rows : tok_rows + ROUTE_ROWS, :].astype(jnp.float32)
        pairs.append(
            route_keys(route, first_ref[0], experts, capacity, rows, b * capacity, tok_rows, top_count, per_group)
        )
    place = lax.broadcasted_iota(jnp.int32, (experts * rows, n_blocks * tok_rows), 0)
    hot = jnp.zeros(place.shape, jnp.float32)
    gate_hot = jnp.zeros(place.shape, jnp.float32)
    for i in range(per_group):
        key = jnp.concatenate([pair[i][0] for pair in pairs], axis=1)
        gate = jnp.concatenate([pair[i][1] for pair in pairs], axis=1)
        match = place == key
        hot = jnp.where(match, 1.0, hot)
        gate_hot = jnp.where(match, gate, gate_hot)
    hot = hot.astype(jnp.bfloat16)
    row_gate = jnp.sum(gate_hot, axis=1, keepdims=True)

    x_all = jnp.concatenate([block[...] for block in tokens], axis=0)
    gathered = dot(hot, x_all, (1, 0)).astype(jnp.bfloat16)
    for e in range(experts):
        x_rows[e] = gathered[e * rows : (e + 1) * rows, :]
    u_all = jnp.concatenate([block[:tok_rows, :] for block in upstream], axis=0)
    scaled = (dot(hot, u_all, (1, 0)) * row_gate).astype(jnp.bfloat16)
    for e in range(experts):
        s_rows[e] = scaled[e * rows : (e + 1) * rows, :]

    for e in range(experts):
        pre_gate = dot(x_rows[e], w_gate[e], (1, 0))
        pre_up = dot(x_rows[e], w_up[e], (1, 0))
        grad_hidden = dot(s_rows[e], w_down[e], (1, 1))
        active, slope = gated_parts(pre_gate)
        grad_gate_pre = (grad_hidden * pre_up * slope).astype(jnp.bfloat16)
        grad_up_pre = (grad_hidden * active).astype(jnp.bfloat16)
        hids[e, :, :ff] = grad_gate_pre
        hids[e, :, ff : 2 * ff] = grad_up_pre
        hids[e, :, 2 * ff :] = (active * pre_up).astype(jnp.bfloat16)
        back = dot(grad_gate_pre, w_gate[e], (1, 1)) + dot(grad_up_pre, w_up[e], (1, 1))
        back_all[e * rows : (e + 1) * rows, :] = back.astype(jnp.bfloat16)

    summed = dot(hot, back_all[...], (0, 0)).astype(jnp.bfloat16)
    start = 0
    for part in parts:
        part[...] = summed[start : start + part.shape[0], :]
        start += part.shape[0]


def chunk_call(tokens, upstream, first_expert, weights, tok_rows, capacity, rows, top_count, per_group, joined):
    n_blocks = len(tokens)
    n_tok = n_blocks * tok_rows
    experts, width, ff = weights[0].shape
    part_shapes = [(n_tok, width)] if joined else [(tok_rows, width), (n_tok - tok_rows, width)]
    kept_shapes = [(experts, rows, width), (experts, rows, width), (experts, rows, 3 * ff)]
    smem, vmem = (pl.BlockSpec(memory_space=m) for m in (pltpu.SMEM, pltpu.VMEM))
    out_shapes = part_shapes + kept_shapes
    return pl.pallas_call(
        functools.partial(chunk_kernel, n_blocks, tok_rows, capacity, rows, top_count, per_group),
        in_specs=[smem] + [vmem] * (2 * n_blocks + 3),
        out_specs=[vmem] * len(out_shapes),
        out_shape=[pltpu.VMEM(shape, jnp.bfloat16) for shape in out_shapes],
        scratch_shapes=[pltpu.VMEM((experts * rows, width), jnp.bfloat16)],
        compiler_params=pltpu.CompilerParams(vmem_limit_bytes=VMEM_LIMIT),
        cost_estimate=pl.CostEstimate(
            flops=2 * experts * rows * width * (5 * ff + 3 * n_tok),
            bytes_accessed=6 * experts * width * ff + 8 * n_tok * width,
            transcendentals=0,
        ),
        name="chunk",
    )(first_expert, *[in_vmem(v) for v in (*tokens, *upstream, *weights)])


def halves_of(n, e, side, refs):
    depth = refs[0].shape[2] // 2
    cols = pl.ds(pl.multiple_of(side * depth, depth), depth)
    cat = lambda parts: jnp.concatenate(parts, axis=0)
    x_rows, s_rows = (cat([ref[e, :, cols] for ref in refs[i * n : (i + 1) * n]]) for i in range(2))
    hid = cat([ref[e] for ref in refs[2 * n : 3 * n]])
    ff = hid.shape[1] // 3
    return dot(x_rows, hid[:, : 2 * ff], (0, 0)), dot(hid[:, 2 * ff :], s_rows, (0, 0))


def send_kernel(n, side_ref, *refs):
    out = refs[3 * n]
    for e in range(out.shape[0]):
        gate_up, down = halves_of(n, e, side_ref[0], refs)
        depth = gate_up.shape[0]
        out[e, :depth, :] = gate_up.astype(jnp.bfloat16)
        out[e, depth:, :] = down.astype(jnp.bfloat16)


def keep_kernel(n, side_ref, *refs):
    got, outs = refs[3 * n], refs[3 * n + 1 : 3 * n + 4]
    buffers, sem = refs[3 * n + 4 : 3 * n + 7], refs[3 * n + 7]
    copies = []
    for e in range(got.shape[0]):
        gate_up, down = halves_of(n, e, side_ref[0], refs)
        depth = gate_up.shape[0]
        ff = down.shape[0]
        gate_up = gate_up + got[e, :depth, :].astype(jnp.float32)
        buffers[0][e] = gate_up[:, :ff].astype(jnp.bfloat16)
        buffers[1][e] = gate_up[:, ff:].astype(jnp.bfloat16)
        buffers[2][e] = (down + got[e, depth:, :].astype(jnp.float32)).astype(jnp.bfloat16)
        for i in range(3):
            copy = pltpu.make_async_copy(buffers[i].at[e], outs[i].at[e], sem.at[e, i])
            copy.start()
            copies.append(copy)
    for copy in copies:
        copy.wait()


def weight_call(side, x_rows, s_rows, hids, got=None):
    n = len(x_rows)
    experts, rows, width = x_rows[0].shape
    ff = hids[0].shape[2] // 3
    depth = width // 2
    smem, vmem = (pl.BlockSpec(memory_space=m) for m in (pltpu.SMEM, pltpu.VMEM))
    operands = [*x_rows, *s_rows, *hids]
    scratch = []
    if got is None:
        kernel, out_specs = send_kernel, vmem
        out_shape = pltpu.VMEM((experts, depth + ff, depth), jnp.bfloat16)
    else:
        kernel = keep_kernel
        operands = operands + [got]
        shapes = [(experts, depth, ff), (experts, depth, ff), (experts, ff, depth)]
        out_specs = [pl.BlockSpec(memory_space=pl.ANY)] * 3
        out_shape = [jax.ShapeDtypeStruct(s, jnp.bfloat16) for s in shapes]
        scratch = [pltpu.VMEM(s, jnp.bfloat16) for s in shapes] + [pltpu.SemaphoreType.DMA((experts, 3))]
    return pl.pallas_call(
        functools.partial(kernel, n),
        in_specs=[smem] + [vmem] * len(operands),
        out_specs=out_specs,
        out_shape=out_shape,
        scratch_shapes=scratch,
        compiler_params=pltpu.CompilerParams(vmem_limit_bytes=VMEM_LIMIT),
        cost_estimate=pl.CostEstimate(
            flops=2 * experts * n * rows * 3 * ff * depth,
            bytes_accessed=2 * experts * (n * rows * (width + 3 * ff) + 3 * ff * depth),
            transcendentals=0,
        ),
        name="weight_grads",
    )(side, *[in_vmem(v) for v in operands])


def per_device(tokens, upstream, expert_ids, gate_fixed, slots, w_gate, w_up, w_down):
    local_experts = w_gate.shape[0]
    n_group = lax.axis_size("group")
    n_ingroup = lax.axis_size("ingroup")
    experts_all = local_experts * n_group * n_ingroup
    tok_rows, top_count = expert_ids.shape
    width = tokens.shape[1]
    per_group = top_count // GROUPS_TOK
    capacity = max(2, 3 * tok_rows * top_count // (2 * experts_all))
    rows = -(-n_ingroup * capacity // 16) * 16
    z, x, core = (lax.axis_index(a) for a in ("group", "ingroup", "dp"))
    first_expert = ((z * n_ingroup + x) * local_experts).astype(jnp.int32).reshape(1)
    half = core.astype(jnp.int32).reshape(1)
    weights = load_call((w_gate, w_up, w_down))
    wide = lambda v: v.astype(jnp.float32)
    tie = lambda *trees: lax.optimization_barrier(trees)
    order = ring_order(n_group)
    along = lambda k: [(order[i], order[(i + k) % n_group]) for i in range(n_group)]
    shift = lambda s: [(i, (i + s) % n_ingroup) for i in range(n_ingroup)]

    def spread(column):
        return [column] + [lax.ppermute(column, "ingroup", shift(s)) for s in range(1, n_ingroup)]

    def chunk(blocks, joined=False):
        return chunk_call(*blocks, first_expert, weights, tok_rows, capacity, rows, top_count, per_group, joined)

    def across(others):
        return [
            lax.ppermute(others[(s - 1) * tok_rows : s * tok_rows], "ingroup", shift(-s)) for s in range(1, n_ingroup)
        ]

    def group_sum(part, backs):
        group_part = wide(part)
        for back in backs:
            group_part = group_part + wide(back)
        return group_part.astype(jnp.bfloat16)

    def homeward(group_part, k):
        return lax.ppermute(group_part, "group", along(-k))

    tokens, first_expert, half, other_half = tie(tokens, first_expert, half, 1 - half)
    first_tokens, upstream = pack_call(tokens, upstream, expert_ids, slots, gate_fixed)
    blocks, chunks, backs, sent = {}, {}, {}, {}
    last = n_group - 1
    for k in range(n_group):
        pair = [spread(tokens), spread(upstream)]
        if k == 0:
            pair[0][0] = first_tokens
        if k < last:
            tokens, upstream = (lax.ppermute(v, "group", along(1)) for v in (tokens, upstream))
        if k > 0:
            chunks[k - 1] = chunk(blocks[k - 1], k - 1 == 1)
        tokens, pair[0], chunks, weights = tie(tokens, pair[0], chunks, weights)
        upstream, pair[1] = tie(upstream, pair[1])
        blocks[k] = pair

    for k in range(2, last - 1):
        sent[k] = homeward(group_sum(chunks[k][0], across(chunks[k][1])), k)
    near = lax.ppermute(chunks[1][0], "group", along(-1))
    blocks[last], chunks = tie(blocks[last], chunks)
    backs[last - 1] = across(chunks[last - 1][1])
    chunks[last] = chunk(blocks[last])
    last_back = across(chunks[last][1])
    chunks, backs, near = tie(chunks, backs, near)

    backs[last] = last_back
    kept = [[chunks[k][i] for k in range(n_group)] for i in (-3, -2, -1)]
    to_send = weight_call(other_half, *kept)
    passed, to_send = tie(group_sum(chunks[last - 1][0], backs[last - 1]), to_send)
    carried = homeward(passed, last)
    to_send, backs[last] = tie(to_send, backs[last])

    got = lax.ppermute(to_send, "dp", [(0, 1), (1, 0)])
    sent[last] = homeward(group_sum(chunks[last][0], [*backs[last], carried]), last)
    backs[0] = across((wide(chunks[0][1]) + wide(near[tok_rows:])).astype(jnp.bfloat16))
    grads = weight_call(half, *kept, got)
    grads, sent = tie(grads, sent)
    grads, backs[0] = tie(grads, backs[0])
    total = wide(chunks[0][0]) + wide(near[:tok_rows])
    for back in backs[0]:
        total = total + wide(back)
    for back in sent.values():
        total = total + wide(back)
    return (total.astype(jnp.bfloat16), *grads)


def solution(mesh):
    rows_spec = P(("parts", "group", "ingroup", "dp"), None)
    weight_spec = P(("group", "ingroup"), None, None)
    out_specs = (
        rows_spec,
        P(("parts", "group", "ingroup"), "dp", None),
        P(("parts", "group", "ingroup"), "dp", None),
        P(("parts", "group", "ingroup"), None, "dp"),
    )
    return jax.shard_map(
        per_device,
        mesh=mesh,
        in_specs=(rows_spec,) * 5 + (weight_spec,) * 3,
        out_specs=out_specs,
        check_vma=False,
    )
```
